128 devices in a mesh: dev: 128 (over y, x, z, core).
Axes of the slice: x: 4, y: 4, z: 4, core: 2. Of those that a mesh axis runs over, the one named last changes fastest.
Arguments:
- params: float32 [59, 1048576], P(None, 'dev'), as said below
- entry_shard: int32 [2048, 128], P('dev'), may hold values from 0 to 127, as said below
- entry_row: int32 [2048, 128], P('dev'), may hold values from 0 to 8191
- depth_order: int32 [2048, 128], P('dev'), may hold values from 0 to 127, as said below
- live_count: int32 [2048], P('dev'), may hold values from 32 to 128
- tile_of_slot: int32 [2048], P('dev'), may hold values from 0 to 32399, as said below
- prev_slot: int32 [2048], P('dev'), may hold values from 0 to 2047, as said below
- gt_image: bfloat16 [2048, 768], P('dev'), may hold values from 0 to 1
Outputs:
- param_grads: float32 [59, 1048576], P(None, 'dev')
- rendered: float32 [2048, 768], P('dev')
- tile_loss: float32 [2048], P('dev')
The draws below stay inside these ranges and needn't reach their ends.
Inputs may be any that keep to these rules, and one draw needn't show every extreme that they name: `entry_shard`: among the 2048 entries of one device's 16 slots at most 32 name any one device, and in every such block some device is named exactly 32 times. `depth_order`: each row is a permutation of 0 to 127. `tile_of_slot`: 2048 different tiles of the 240 x 135 grid, numbered row by row. `prev_slot`: A permutation of 0 to 2047; the 16 slots of one device take their previous slots from 16 different devices, one each, and each device's previous slots go to 16 different devices, one each. `params`: row 2 lies between 2 and 34 and row 6 between 0.5 and 1.5.
All inputs are finite; a program needn't handle non-finite values.
Results may differ from the reference program's by a relative error of at most 0.0003.
Values may be sent and summed in bfloat16 or wider, within the bound.
No kernel may reach another device: no remote copies, remote signals or barrier semaphores. Data moves between devices by JAX's collectives and lax.ppermute only.
A program may use at most 128 MiB of HBM per device.

```python
import jax
import jax.numpy as jnp
from jax import lax

G_DEV = 8192
TILE_DEV = 16
K = 128
TW = 240
TH = 135
GAUSS = 1048576
TILES = 2048
CAP = 32


def scene_lists(key):
    devices = TILES // TILE_DEV
    entries = TILE_DEV * K

    def one_device(device_key):
        subkeys = jax.random.split(device_key, 3)
        busiest = jax.random.randint(subkeys[0], (), 0, devices, dtype=jnp.int32)
        holder_pool = jnp.repeat(jnp.arange(devices, dtype=jnp.int32), CAP)
        shuffled = jax.random.permutation(subkeys[1], devices * CAP).astype(jnp.int32)
        sort_score = jnp.where(holder_pool == busiest, 0, devices * CAP) + shuffled
        chosen = holder_pool[jnp.argsort(sort_score)][:entries]
        return chosen[jax.random.permutation(subkeys[2], entries)]
    holders = jax.vmap(one_device)(jax.random.split(jax.random.fold_in(key, 101), devices)).reshape(TILES, K)
    rows_drawn = jax.random.randint(jax.random.fold_in(key, 102), (TILES, K), 0, G_DEV, dtype=jnp.int32)
    depth_rank = jax.vmap(lambda row_key: jax.random.permutation(row_key, K))(jax.random.split(jax.random.fold_in(key, 103), TILES)).astype(jnp.int32)
    grid_tiles = TW * TH
    picked = jax.random.permutation(jax.random.fold_in(key, 104), grid_tiles - 1).astype(jnp.int32)[:TILES - 1]
    with_last = jnp.concatenate([picked, jnp.full((1,), grid_tiles - 1, jnp.int32)])
    slot_tiles = with_last[jax.random.permutation(jax.random.fold_in(key, 105), TILES)].astype(jnp.int32)
    return (holders.astype(jnp.int32), rows_drawn, depth_rank, slot_tiles)


def draw_entry_shard(key, part):
    return scene_lists(key)[0]


def draw_entry_row(key, part):
    return scene_lists(key)[1]


def draw_depth_order(key, part):
    return scene_lists(key)[2]


def draw_tile_of_slot(key, part):
    return scene_lists(key)[3]


def draw_live_count(key, part):
    key = jax.random.fold_in(key, 5)
    counts = jax.random.randint(jax.random.fold_in(key, 1), (TILES,), K // 4, K + 1, dtype=jnp.int32)
    fullest = jax.random.randint(jax.random.fold_in(key, 2), (), 0, TILES, dtype=jnp.int32)
    return counts.at[fullest].set(K)


def draw_prev_slot(key, part):
    key = jax.random.fold_in(key, 7)
    devices = TILES // TILE_DEV
    subkeys = jax.random.split(key, 3)
    sigma_perm = jax.random.permutation(subkeys[0], devices).astype(jnp.int32)
    tau_perm = jax.random.permutation(subkeys[1], devices).astype(jnp.int32)
    device_ids = jnp.arange(devices, dtype=jnp.int32)[:, None]
    column_ids = jnp.arange(TILE_DEV, dtype=jnp.int32)[None, :]
    source = sigma_perm[(tau_perm[device_ids] + column_ids) % devices]
    row_perm = jax.vmap(lambda row_key: jax.random.permutation(row_key, TILE_DEV))(jax.random.split(subkeys[2], devices)).astype(jnp.int32)
    previous = source * TILE_DEV + row_perm[source, column_ids]
    return previous.reshape(TILES).astype(jnp.int32)


def draw_params(key, part):
    holders, rows_drawn, depth_rank, slot_tiles = scene_lists(key)
    key = jax.random.fold_in(key, 11)
    gauss_ids = (holders * G_DEV + rows_drawn).reshape(TILES * K)
    home_index = jnp.full((GAUSS,), -1, jnp.int32).at[gauss_ids].max(jnp.arange(TILES * K, dtype=jnp.int32))
    listed = home_index >= 0
    home_entry = jnp.maximum(home_index, 0)
    home_slot = home_entry // K
    column = home_entry % K
    inverse_rank = jnp.argsort(depth_rank, axis=1).astype(jnp.int32)
    depth_place = inverse_rank[home_slot, column].astype(jnp.float32)
    home_tile = slot_tiles[home_slot]
    subkeys = jax.random.split(key, 12)

    def uniform_row(number):
        return jax.random.uniform(subkeys[number], (GAUSS,), jnp.float32)
    depth_value = jnp.where(listed, 2.0 + 0.25 * (depth_place + uniform_row(0)), 2.0 + 0.25 * K * uniform_row(1))
    screen_u = jnp.where(listed, 16.0 * (home_tile % TW).astype(jnp.float32) + 16.0 * uniform_row(2), 16.0 * TW * uniform_row(3))
    screen_v = jnp.where(listed, 16.0 * (home_tile // TW).astype(jnp.float32) + 16.0 * uniform_row(4), 16.0 * TH * uniform_row(5))
    pos_x = (screen_u - 8.0 * TW) * depth_value / 1200.0
    pos_y = (screen_v - 8.0 * TH) * depth_value / 1200.0
    is_base = (jnp.arange(48) % 16 == 0)[:, None]
    sigma_low = 1.5
    sigma_high = 6.0
    base_draw = jax.random.normal(subkeys[10], (48, GAUSS), jnp.float32)
    coefficients = base_draw * jnp.where(is_base, 1.0, 0.3)
    opacity_logit = jax.random.uniform(subkeys[9], (1, GAUSS), jnp.float32, -5.0, -1.5)
    pixel_sigma = jnp.exp(jnp.log(sigma_low) + (jnp.log(sigma_high) - jnp.log(sigma_low)) * jax.random.uniform(subkeys[6], (3, GAUSS), jnp.float32))
    log_scale = jnp.log(pixel_sigma * depth_value[None, :] / 1200.0)
    real_part = 0.5 + jax.random.uniform(subkeys[7], (1, GAUSS), jnp.float32)
    imag_part = jax.random.uniform(subkeys[8], (3, GAUSS), jnp.float32, -0.8, 0.8)
    return jnp.concatenate([pos_x[None], pos_y[None], depth_value[None], log_scale, real_part, imag_part, opacity_logit, coefficients], axis=0)


def draw_gt_image(key, part):
    key = jax.random.fold_in(key, 13)
    subkeys = jax.random.split(key, 2)
    level = jax.random.uniform(subkeys[0], (TILES, 1), jnp.float32, 0.2, 1.0)
    grain = jax.random.uniform(subkeys[1], (TILES, 768), jnp.float32)
    return (level * grain).astype(jnp.bfloat16)


def setup_inputs(seed: int = 0) -> dict:
    splits = jax.random.split(jax.random.key(seed), 9)
    params = draw_params(jax.random.fold_in(splits[8], 71), 0)
    entry_shard = draw_entry_shard(jax.random.fold_in(splits[8], 71), 0)
    entry_row = draw_entry_row(jax.random.fold_in(splits[8], 71), 0)
    depth_order = draw_depth_order(jax.random.fold_in(splits[8], 71), 0)
    live_count = draw_live_count(jax.random.fold_in(splits[8], 71), 0)
    tile_of_slot = draw_tile_of_slot(jax.random.fold_in(splits[8], 71), 0)
    prev_slot = draw_prev_slot(jax.random.fold_in(splits[8], 71), 0)
    gt_image = draw_gt_image(jax.random.fold_in(splits[8], 71), 0)
    return dict(params=params, entry_shard=entry_shard, entry_row=entry_row, depth_order=depth_order, live_count=live_count, tile_of_slot=tile_of_slot, prev_slot=prev_slot, gt_image=gt_image)


focal = 1200.0

def harmonics(unit_x, unit_y, unit_z):
    square_x = unit_x * unit_x
    square_y = unit_y * unit_y
    square_z = unit_z * unit_z
    return [0.28209479177387814 * jnp.ones_like(unit_x), -0.4886025119029199 * unit_y, 0.4886025119029199 * unit_z, -0.4886025119029199 * unit_x, 1.0925484305920792 * unit_x * unit_y, -1.0925484305920792 * unit_y * unit_z, 0.31539156525252005 * (2.0 * square_z - square_x - square_y), -1.0925484305920792 * unit_x * unit_z, 0.5462742152960396 * (square_x - square_y), -0.5900435899266435 * unit_y * (3.0 * square_x - square_y), 2.890611442640554 * unit_x * unit_y * unit_z, -0.4570457994644658 * unit_y * (4.0 * square_z - square_x - square_y), 0.3731763325901154 * unit_z * (2.0 * square_z - 3.0 * square_x - 3.0 * square_y), -0.4570457994644658 * unit_x * (4.0 * square_z - square_x - square_y), 1.445305721320277 * unit_z * (square_x - square_y), -0.5900435899266435 * unit_x * (square_x - 3.0 * square_y)]

def project(params, center_u, center_v):
    pos_x = params[0]
    pos_y = params[1]
    depth_value = params[2]
    scales = jnp.exp(params[3:6])
    quaternion = params[6:10]
    unit_q = quaternion * lax.rsqrt(lax.optimization_barrier(jnp.sum(quaternion * quaternion, axis=0)))
    w_part = unit_q[0]
    x_part = unit_q[1]
    y_part = unit_q[2]
    z_part = unit_q[3]
    rotation = [[1.0 - 2.0 * (y_part * y_part + z_part * z_part), 2.0 * (x_part * y_part - w_part * z_part), 2.0 * (x_part * z_part + w_part * y_part)], [2.0 * (x_part * y_part + w_part * z_part), 1.0 - 2.0 * (x_part * x_part + z_part * z_part), 2.0 * (y_part * z_part - w_part * x_part)], [2.0 * (x_part * z_part - w_part * y_part), 2.0 * (y_part * z_part + w_part * x_part), 1.0 - 2.0 * (x_part * x_part + y_part * y_part)]]
    focal_z = focal / depth_value
    slope_x = -focal * pos_x / (depth_value * depth_value)
    slope_y = -focal * pos_y / (depth_value * depth_value)
    first_row = [(focal_z * rotation[0][column] + slope_x * rotation[2][column]) * scales[column] for column in range(3)]
    second_row = [(focal_z * rotation[1][column] + slope_y * rotation[2][column]) * scales[column] for column in range(3)]
    spread_xx = first_row[0] * first_row[0] + first_row[1] * first_row[1] + first_row[2] * first_row[2] + 0.3
    spread_xy = first_row[0] * second_row[0] + first_row[1] * second_row[1] + first_row[2] * second_row[2]
    spread_yy = second_row[0] * second_row[0] + second_row[1] * second_row[1] + second_row[2] * second_row[2] + 0.3
    determinant = spread_xx * spread_yy - spread_xy * spread_xy
    inverse_norm = lax.rsqrt(pos_x * pos_x + pos_y * pos_y + depth_value * depth_value)
    harmonic_values = harmonics(pos_x * inverse_norm, pos_y * inverse_norm, depth_value * inverse_norm)
    colors = []
    for channel in range(3):
        accum_color = 0.5 + harmonic_values[0] * params[11 + 16 * channel]
        for degree in range(1, 16):
            accum_color = accum_color + harmonic_values[degree] * params[11 + 16 * channel + degree]
        colors.append(accum_color)
    return jnp.stack([focal * pos_x / depth_value + center_u, focal * pos_y / depth_value + center_v, spread_yy / determinant, -spread_xy / determinant, spread_xx / determinant, colors[0], colors[1], colors[2], jax.nn.sigmoid(params[10])])

def render(ordered_rows, live_mask, tile_ids, truth_tiles):
    pixel_index = jnp.arange(256, dtype=jnp.int32)
    base_x = (16 * (tile_ids % TW)).astype(jnp.float32)
    base_y = (16 * (tile_ids // TW)).astype(jnp.float32)
    center_x = base_x[:, None] + (pixel_index % 16).astype(jnp.float32)[None, :] + 0.5
    center_y = base_y[:, None] + (pixel_index // 16).astype(jnp.float32)[None, :] + 0.5
    offset_x = center_x[:, :, None] - ordered_rows[0][:, None, :]
    offset_y = center_y[:, :, None] - ordered_rows[1][:, None, :]
    exponent = -0.5 * (ordered_rows[2][:, None, :] * offset_x * offset_x + 2.0 * ordered_rows[3][:, None, :] * offset_x * offset_y + ordered_rows[4][:, None, :] * offset_y * offset_y)
    opacity_at = (live_mask * ordered_rows[8])[:, None, :] * jnp.exp(exponent)
    through = lax.cumprod(1.0 - opacity_at, axis=2)
    before = jnp.concatenate([jnp.ones_like(through[:, :, :1]), through[:, :, :-1]], axis=2)
    weights = opacity_at * before
    picture = jnp.einsum('tqj,ctj->tcq', weights, ordered_rows[5:8], precision=lax.Precision.HIGHEST)
    flat_picture = picture.reshape(picture.shape[0], 768)
    difference = flat_picture - truth_tiles
    smooth = jnp.sqrt(difference * difference + 0.0001)
    target = truth_tiles.reshape(truth_tiles.shape[0], 3, 256)
    mean_r = lax.optimization_barrier(jnp.mean(picture, axis=2))
    mean_t = lax.optimization_barrier(jnp.mean(target, axis=2))
    centered_r = picture - mean_r[:, :, None]
    centered_t = target - mean_t[:, :, None]
    var_r = lax.optimization_barrier(jnp.mean(centered_r * centered_r, axis=2))
    var_t = lax.optimization_barrier(jnp.mean(centered_t * centered_t, axis=2))
    cov_rt = lax.optimization_barrier(jnp.mean(centered_r * centered_t, axis=2))
    similarity = (2.0 * mean_r * mean_t + 0.0001) * (2.0 * cov_rt + 0.0009) / ((mean_r * mean_r + mean_t * mean_t + 0.0001) * (var_r + var_t + 0.0009))
    losses = 0.8 * lax.optimization_barrier(jnp.sum(smooth, axis=1)) / 3.0 + 0.2 * 256.0 * lax.optimization_barrier(jnp.sum(1.0 - similarity, axis=1)) / 3.0
    return (flat_picture, losses)

def reference(params, entry_shard, entry_row, depth_order, live_count, tile_of_slot, prev_slot, gt_image):
    truth_tiles = gt_image[prev_slot].astype(jnp.float32)
    chosen = jnp.take_along_axis(entry_shard * G_DEV + entry_row, depth_order, axis=1)
    live_mask = (depth_order < live_count[:, None]).astype(jnp.float32)
    blocks = TILES // TILE_DEV

    def one_block(pieces):
        return render(pieces[0], pieces[1], pieces[2], pieces[3])

    def whole_loss(values_in):
        projected = project(values_in, 8.0 * TW, 8.0 * TH)
        gathered = projected[:, chosen]
        grouped = gathered.reshape(9, blocks, TILE_DEV, K).transpose(1, 0, 2, 3)
        pictures, losses = lax.map(jax.checkpoint(one_block), (grouped, live_mask.reshape(blocks, TILE_DEV, K), tile_of_slot.reshape(blocks, TILE_DEV), truth_tiles.reshape(blocks, TILE_DEV, 768)))
        return (jnp.sum(losses), (pictures.reshape(TILES, 768), losses.reshape(TILES)))
    total_loss, pullback, extras = jax.vjp(whole_loss, params, has_aux=True)
    gradients = pullback(jnp.ones_like(total_loss))[0]
    return (gradients, extras[0], extras[1])
```

```python
import jax
import jax.numpy as jnp
from jax import lax
from jax.experimental import pallas as pl
from jax.experimental.pallas import tpu as pltpu
from jax.sharding import PartitionSpec as P

TW = 240
TH = 135
FOCAL = 1200.0
LOG2E = 1.4426950408889634
F32 = jnp.float32
BF16 = jnp.bfloat16
I32 = jnp.int32


def iota(shape, axis):
    return lax.broadcasted_iota(I32, shape, axis)


def take_lane(table, index):
    return jnp.take_along_axis(table, index, axis=1, mode="promise_in_bounds")


def geometry(values):
    (pos_x, pos_y, depth, ls0, ls1, ls2, q0, q1, q2, q3, logit) = values
    scales = [jnp.exp(ls0), jnp.exp(ls1), jnp.exp(ls2)]
    inverse_q = lax.rsqrt(q0 * q0 + q1 * q1 + q2 * q2 + q3 * q3)
    w_part = q0 * inverse_q
    x_part = q1 * inverse_q
    y_part = q2 * inverse_q
    z_part = q3 * inverse_q
    rotation = [
        [
            1.0 - 2.0 * (y_part * y_part + z_part * z_part),
            2.0 * (x_part * y_part - w_part * z_part),
            2.0 * (x_part * z_part + w_part * y_part),
        ],
        [
            2.0 * (x_part * y_part + w_part * z_part),
            1.0 - 2.0 * (x_part * x_part + z_part * z_part),
            2.0 * (y_part * z_part - w_part * x_part),
        ],
        [
            2.0 * (x_part * z_part - w_part * y_part),
            2.0 * (y_part * z_part + w_part * x_part),
            1.0 - 2.0 * (x_part * x_part + y_part * y_part),
        ],
    ]
    inverse_z = 1.0 / depth
    focal_z = FOCAL * inverse_z
    ratio_x = pos_x * inverse_z
    ratio_y = pos_y * inverse_z
    slope_x = -focal_z * ratio_x
    slope_y = -focal_z * ratio_y
    first = [(focal_z * rotation[0][i] + slope_x * rotation[2][i]) * scales[i] for i in range(3)]
    second = [(focal_z * rotation[1][i] + slope_y * rotation[2][i]) * scales[i] for i in range(3)]
    spread_xx = first[0] * first[0] + first[1] * first[1] + first[2] * first[2] + 0.3
    spread_xy = first[0] * second[0] + first[1] * second[1] + first[2] * second[2]
    spread_yy = second[0] * second[0] + second[1] * second[1] + second[2] * second[2] + 0.3
    inverse_det = 1.0 / (spread_xx * spread_yy - spread_xy * spread_xy)
    inverse_norm = lax.rsqrt(pos_x * pos_x + pos_y * pos_y + depth * depth)
    return (
        FOCAL * pos_x / depth + 8.0 * TW,
        FOCAL * pos_y / depth + 8.0 * TH,
        spread_yy * inverse_det,
        -spread_xy * inverse_det,
        spread_xx * inverse_det,
        lax.logistic(logit),
        pos_x * inverse_norm,
        pos_y * inverse_norm,
        depth * inverse_norm,
    )


def harmonics(unit_x, unit_y, unit_z):
    square_x = unit_x * unit_x
    square_y = unit_y * unit_y
    square_z = unit_z * unit_z
    return [
        0.28209479177387814 * jnp.ones_like(unit_x),
        -0.4886025119029199 * unit_y,
        0.4886025119029199 * unit_z,
        -0.4886025119029199 * unit_x,
        1.0925484305920792 * unit_x * unit_y,
        -1.0925484305920792 * unit_y * unit_z,
        0.31539156525252005 * (2.0 * square_z - square_x - square_y),
        -1.0925484305920792 * unit_x * unit_z,
        0.5462742152960396 * (square_x - square_y),
        -0.5900435899266435 * unit_y * (3.0 * square_x - square_y),
        2.890611442640554 * unit_x * unit_y * unit_z,
        -0.4570457994644658 * unit_y * (4.0 * square_z - square_x - square_y),
        0.3731763325901154 * unit_z * (2.0 * square_z - 3.0 * square_x - 3.0 * square_y),
        -0.4570457994644658 * unit_x * (4.0 * square_z - square_x - square_y),
        1.445305721320277 * unit_z * (square_x - square_y),
        -0.5900435899266435 * unit_x * (square_x - 3.0 * square_y),
    ]


def route_kernel(
    shard_ref, row_ref, order_ref, live_ref, prev_ref,
    request_ref, holder_ref, place_ref, back_j_ref, back_t_ref,
):
    tiles, length = shard_ref.shape
    order = order_ref[...]
    shards = take_lane(shard_ref[...], order)
    rows = take_lane(row_ref[...], order)
    sub = iota((128, 128), 0)
    lane = iota((128, 128), 1)
    wide_row = iota((128, 256), 0)
    wide_lane = iota((128, 256), 1)
    counter = jnp.where((wide_lane >= 128) | (wide_row < wide_lane), 1.0, 0.0).astype(BF16)
    sub_k = iota((32, 128), 0)
    j_code = iota((1, 128), 1).astype(F32)
    carry = jnp.zeros((128, 128), F32)
    request = jnp.zeros((128, 128), F32)
    back = jnp.zeros((64, 128), F32)
    truth = jnp.zeros((128, 128), I32)
    nothing = jnp.zeros((96, 256), F32)
    for t in range(tiles):
        live = order[t : t + 1, :] < live_ref[t]
        holder = jnp.where(live, shards[t : t + 1, :], -1)
        match = jnp.broadcast_to(holder, (128, 128)) == sub
        hot = jnp.where(match, 1.0, 0.0).astype(BF16)
        counted = jnp.dot(hot, counter, preferred_element_type=F32)
        place = jnp.sum(
            jnp.where(match, counted[:, :128] + carry, 0.0), axis=0, keepdims=True
        ).astype(I32)
        carry = carry + counted[:, 128:]
        holder_ref[t : t + 1, :] = holder
        place_ref[t : t + 1, :] = jnp.where(live, place, -1)
        match_k = jnp.broadcast_to(place, (32, 128)) == sub_k
        row = rows[t : t + 1, :]
        high = jnp.where(match_k, ((row >> 7) * 128).astype(F32), 0.0)
        low = jnp.where(match_k, (row & 127).astype(F32), 0.0)
        asked = jnp.concatenate(
            [jnp.concatenate([high, low], axis=1), nothing], axis=0
        ).astype(BF16)
        request = request + lax.dot_general(
            jnp.concatenate([hot, hot], axis=1), asked,
            (((1,), (1,)), ((), ())), preferred_element_type=F32,
        )
        codes = jnp.concatenate(
            [jnp.where(match_k, j_code, 0.0), jnp.where(match_k, t + 1.0, 0.0)], axis=0
        ).astype(BF16)
        back = back + lax.dot_general(
            codes, hot, (((1,), (1,)), ((), ())), preferred_element_type=F32
        )
        previous = prev_ref[t]
        truth = jnp.where(sub == lax.shift_right_logical(previous, 4), previous & 15, truth)
    request_ref[...] = jnp.where(lane == 32, truth, request.astype(I32))
    back_j_ref[...] = back[:32, :].astype(I32)
    back_t_ref[...] = back[32:, :].astype(I32) - 1


def project_kernel(params_ref, out_ref):
    def step(block, unused):
        start = pl.multiple_of(block * 1024, 1024)
        values = params_ref[:, pl.ds(start, 1024)].reshape(59, 8, 128)
        p = [values[i] for i in range(59)]
        (u, v, ca, cb, cc, opacity, ux, uy, uz) = geometry(p[:11])
        basis = harmonics(ux, uy, uz)
        colors = []
        for channel in range(3):
            color = 0.5 + basis[0] * p[11 + 16 * channel]
            for degree in range(1, 16):
                color = color + basis[degree] * p[11 + 16 * channel + degree]
            colors.append(color)
        for c, value in enumerate([u, v, ca, cb, cc] + colors + [opacity]):
            out_ref[c, pl.ds(pl.multiple_of(block * 8, 8), 8), :] = value
        return unused

    lax.fori_loop(0, 8, step, 0)


def pick_kernel(asked_ref, table_ref, out_ref):
    index = asked_ref[...].astype(F32).T[:32, :].astype(I32)
    high = index >> 7
    low = index & 127
    zeros = tuple(jnp.zeros((32, 128), F32) for _ in range(9))

    def step(h, sums):
        match = high == h
        return tuple(
            jnp.where(
                match,
                take_lane(jnp.broadcast_to(table_ref[c, pl.ds(h, 1), :], (32, 128)), low),
                sums[c],
            )
            for c in range(9)
        )

    found = lax.fori_loop(0, 64, step, zeros, unroll=4)
    put_rows(out_ref, found)


def put_rows(out_ref, found):
    blank = jnp.zeros((96, 128), F32)
    for i in range(3):
        group = list(found[4 * i : 4 * i + 4])
        if i == 2:
            group.append(blank)
        out_ref[pl.ds(i, 128, stride=3), :] = jnp.concatenate(group, axis=0).T


def truth_kernel(asked_ref, image_ref, out_ref):
    hot = jnp.where(asked_ref[:, 32:33] == iota((128, 16), 1), 1.0, 0.0).astype(BF16)
    out_ref[...] = jnp.dot(hot, image_ref[...], preferred_element_type=F32).astype(BF16)


def render_kernel(
    arrived_ref, holder_ref, place_ref, back_j_ref, back_t_ref, delivered_ref, tile_ref, prev_ref,
    picture_ref, loss_ref, out_ref,
    table_ref, ordered_ref, alpha_ref, weight_ref, reach_ref, grad_ref,
):
    for i in range(3):
        table_ref[128 * i : 128 * (i + 1), :] = arrived_ref[pl.ds(i, 128, stride=3), :].T
    holder = jnp.maximum(holder_ref[...], 0)
    place = place_ref[...]
    values = [jnp.zeros((16, 128), F32) for _ in range(9)]
    for k in range(32):
        match = place == k
        for c in range(9):
            row = jnp.broadcast_to(table_ref[32 * c + k : 32 * c + k + 1, :], (16, 128))
            values[c] = jnp.where(match, take_lane(row, holder), values[c])
    sub = iota((16, 128), 0)
    base_x = jnp.zeros((16, 128), F32)
    base_y = jnp.zeros((16, 128), F32)
    source = jnp.zeros((16, 128), I32)
    for t in range(16):
        number = tile_ref[t]
        tile_row = number // TW
        tile_column = number - tile_row * TW
        base_x = jnp.where(sub == t, (16 * tile_column + 8).astype(F32), base_x)
        base_y = jnp.where(sub == t, (16 * tile_row + 8).astype(F32), base_y)
        source = jnp.where(sub == t, lax.shift_right_logical(prev_ref[t], 4), source)
    (u, v, ca, cb, cc, red, green, blue, opacity) = values
    u = u - base_x
    v = v - base_y
    for c, value in enumerate(
        [u, v, (-0.5 * LOG2E) * ca, (-LOG2E) * cb, (-0.5 * LOG2E) * cc, red, green, blue, opacity]
    ):
        ordered_ref[c] = value
    pixel = iota((8, 128), 1)
    grid_x = (pixel & 15).astype(F32) - 7.5
    grid_y = [(pixel >> 4).astype(F32) - 7.5, (pixel >> 4).astype(F32) + 0.5]

    def column(c, g, j):
        return take_lane(
            ordered_ref[c, 8 * g : 8 * g + 8, :], jnp.full((8, 128), j, I32)
        )

    ones = jnp.ones((8, 128), F32)
    zero = jnp.zeros((8, 128), F32)

    def forward(j, state):
        reach, sums = state
        reach = list(reach)
        sums = list(sums)
        for g in range(2):
            (gu, gv, ga, gb, gc, g0, g1, g2, go) = [column(c, g, j) for c in range(9)]
            dx = grid_x - gu
            part_a = ga * dx * dx
            part_b = gb * dx
            for h in range(2):
                n = 2 * g + h
                dy = grid_y[h] - gv
                fall = jnp.exp2(part_a + dy * (part_b + gc * dy))
                alpha = go * fall
                weight = alpha * reach[n]
                alpha_ref[j, n] = alpha
                weight_ref[j, n] = weight
                reach_ref[j, n] = fall * reach[n]
                reach[n] = reach[n] - weight
                sums[3 * n] = sums[3 * n] + weight * g0
                sums[3 * n + 1] = sums[3 * n + 1] + weight * g1
                sums[3 * n + 2] = sums[3 * n + 2] + weight * g2
        return (tuple(reach), tuple(sums))

    unused, sums = lax.fori_loop(
        0, 128, forward, (tuple([ones] * 4), tuple([zero] * 12)), unroll=4
    )
    hot = jnp.where(source == iota((16, 128), 1), 1.0, 0.0).astype(BF16)
    target = jnp.dot(hot, delivered_ref[...], preferred_element_type=F32)
    loss = jnp.zeros((16, 1), F32)
    slopes = []
    for k in range(3):
        image = jnp.concatenate(
            [
                jnp.concatenate([sums[3 * (2 * g) + k], sums[3 * (2 * g + 1) + k]], axis=1)
                for g in range(2)
            ],
            axis=0,
        )
        picture_ref[:, 256 * k : 256 * (k + 1)] = image
        wanted = target[:, 256 * k : 256 * (k + 1)]
        difference = image - wanted
        smooth = jnp.sqrt(difference * difference + 0.0001)
        mean_r = jnp.sum(image, axis=1, keepdims=True) / 256.0
        mean_t = jnp.sum(wanted, axis=1, keepdims=True) / 256.0
        centered_r = image - mean_r
        centered_t = wanted - mean_t
        var_r = jnp.sum(centered_r * centered_r, axis=1, keepdims=True) / 256.0
        var_t = jnp.sum(centered_t * centered_t, axis=1, keepdims=True) / 256.0
        cov = jnp.sum(centered_r * centered_t, axis=1, keepdims=True) / 256.0
        top_m = 2.0 * mean_r * mean_t + 0.0001
        top_c = 2.0 * cov + 0.0009
        low_m = mean_r * mean_r + mean_t * mean_t + 0.0001
        low_v = var_r + var_t + 0.0009
        below = 1.0 / (low_m * low_v)
        similarity = top_m * top_c * below
        loss = loss + (0.8 / 3.0) * jnp.sum(smooth, axis=1, keepdims=True)
        loss = loss + (0.2 * 256.0 / 3.0) * (1.0 - similarity)
        by_mean = 2.0 * mean_t * top_c * below - similarity * 2.0 * mean_r / low_m
        by_cov = 2.0 * top_m * below
        by_var = -similarity / low_v
        slopes.append(
            (0.8 / 3.0) * difference / smooth
            - (0.2 / 3.0) * (by_mean + 2.0 * by_var * centered_r + by_cov * centered_t)
        )
    loss_ref[...] = jnp.broadcast_to(loss, (16, 128))
    slope = [
        [slopes[k][8 * g : 8 * g + 8, 128 * h : 128 * h + 128] for k in range(3)]
        for g in range(2)
        for h in range(2)
    ]
    grid_yy = [grid_y[h] * grid_y[h] for h in range(2)]
    for c in range(9):
        grad_ref[c] = jnp.zeros((16, 128), F32)

    def backward(step, state):
        j = 127 - step
        behind = list(state)
        here = iota((8, 128), 1) == j
        for g in range(2):
            (g0, g1, g2) = [column(c, g, j) for c in (5, 6, 7)]
            pulls = []
            shares = []
            for h in range(2):
                n = 2 * g + h
                value = slope[n][0] * g0 + slope[n][1] * g1 + slope[n][2] * g2
                gap = value - behind[n]
                pulls.append(reach_ref[j, n] * gap)
                behind[n] = behind[n] + alpha_ref[j, n] * gap
                weight = weight_ref[j, n]
                shares.append([weight * slope[n][k] for k in range(3)])
            both = pulls[0] + pulls[1]
            tall = pulls[0] * grid_y[0] + pulls[1] * grid_y[1]
            taller = pulls[0] * grid_yy[0] + pulls[1] * grid_yy[1]
            both_x = both * grid_x
            moments = [
                both,
                both_x,
                tall,
                both_x * grid_x,
                tall * grid_x,
                taller,
                shares[0][0] + shares[1][0],
                shares[0][1] + shares[1][1],
                shares[0][2] + shares[1][2],
            ]
            for c, moment in enumerate(moments):
                total = jnp.sum(moment, axis=1, keepdims=True)
                spot = grad_ref[c, 8 * g : 8 * g + 8, :]
                grad_ref[c, 8 * g : 8 * g + 8, :] = jnp.where(here, total, spot)
        return tuple(behind)

    lax.fori_loop(0, 128, backward, tuple([zero] * 4), unroll=4)
    (m0, mx, my, mxx, mxy, myy, d_red, d_green, d_blue) = [grad_ref[c] for c in range(9)]
    sx = mx - u * m0
    sy = my - v * m0
    sxx = mxx - u * (mx + sx)
    syy = myy - v * (my + sy)
    sxy = mxy - u * my - v * sx
    results = [
        opacity * (ca * sx + cb * sy),
        opacity * (cb * sx + cc * sy),
        -0.5 * opacity * sxx,
        -opacity * sxy,
        -0.5 * opacity * syy,
        d_red,
        d_green,
        d_blue,
        m0,
    ]
    back_j = back_j_ref[...]
    back_t = back_t_ref[...]
    for c in range(9):
        grad_ref[c] = results[c]
    found = [jnp.zeros((32, 128), F32) for _ in range(9)]
    for t in range(16):
        match = back_t == t
        for c in range(9):
            row = jnp.broadcast_to(grad_ref[c, t : t + 1, :], (32, 128))
            found[c] = jnp.where(match, take_lane(row, back_j), found[c])
    put_rows(out_ref, found)


def update_kernel(returned_ref, asked_ref, params_ref, out_ref, high_ref, low_ref, piece_ref, sum_ref):
    index = asked_ref[...].astype(F32).T[:32, :].astype(I32)
    high_ref[...] = (index >> 7) & 31
    low_ref[...] = (index & 127) + 128 * (index >> 12)
    for i in range(3):
        block = returned_ref[pl.ds(i, 128, stride=3), :].T
        rows = 128 if i < 2 else 32
        block = block[:rows, :]
        upper = block.astype(BF16).astype(F32)
        piece_ref[0, 128 * i : 128 * i + rows, :] = upper
        piece_ref[1, 128 * i : 128 * i + rows, :] = block - upper
    sum_ref[...] = jnp.zeros((288, 256), F32)
    sub_high = iota((32, 128), 0)
    sub_low = iota((256, 128), 0)

    def scatter(pair, unused):
        right = []
        left = [[], []]
        for half in range(2):
            k = 2 * pair + half
            low = jnp.broadcast_to(low_ref[pl.ds(k, 1), :], (256, 128))
            right.append(jnp.where(low == sub_low, 1.0, 0.0).astype(BF16))
            high = jnp.broadcast_to(high_ref[pl.ds(k, 1), :], (32, 128)) == sub_high
            for p in range(2):
                left[p].append(
                    jnp.concatenate(
                        [
                            jnp.where(high, piece_ref[p, pl.ds(32 * c + k, 1), :], 0.0)
                            for c in range(9)
                        ],
                        axis=0,
                    ).astype(BF16)
                )
        right = jnp.concatenate(right, axis=1)
        total = sum_ref[...]
        for p in range(2):
            total = total + lax.dot_general(
                jnp.concatenate(left[p], axis=1), right,
                (((1,), (1,)), ((), ())), preferred_element_type=F32,
            )
        sum_ref[...] = total
        return unused

    lax.fori_loop(0, 16, scatter, 0)

    def pull(block, half):
        start = pl.multiple_of(half * 4096 + block * 1024, 1024)
        values = params_ref[:, pl.ds(start, 1024)].reshape(59, 8, 128)
        p = [values[i] for i in range(59)]
        g = [
            sum_ref[pl.ds(pl.multiple_of(32 * c + 8 * block, 8), 8), 128 * half : 128 * half + 128]
            for c in range(9)
        ]
        primal, pull_geometry = jax.vjp(lambda *a: geometry(a), *p[:11])
        basis, pull_basis = jax.vjp(lambda *a: tuple(harmonics(*a)), *primal[6:9])
        d_basis = tuple(
            g[5] * p[11 + i] + g[6] * p[27 + i] + g[7] * p[43 + i] for i in range(16)
        )
        d_unit = pull_basis(d_basis)
        d_first = pull_geometry((g[0], g[1], g[2], g[3], g[4], g[8]) + tuple(d_unit))
        rows = list(d_first) + [g[5 + k] * basis[i] for k in range(3) for i in range(16)]
        out_ref[:, pl.ds(start, 1024)] = jnp.stack(rows, axis=0).reshape(59, 1024)

    for half in range(2):
        lax.fori_loop(0, 4, lambda b, unused, half=half: (pull(b, half), unused)[1], 0)


def vmem():
    return pl.BlockSpec(memory_space=pltpu.VMEM)


def smem():
    return pl.BlockSpec(memory_space=pltpu.SMEM)


def shape(dims, dtype=F32):
    return jax.ShapeDtypeStruct(dims, dtype)


ROOM = pltpu.CompilerParams(vmem_limit_bytes=40 * 1024 * 1024)


def swap(values):
    return lax.all_to_all(values, "dev", split_axis=0, concat_axis=0, tiled=True)


def body(
    params, entry_shard, entry_row, depth_order, live_count, tile_of_slot, prev_slot, gt_image
):
    request, holder, place, back_j, back_t = pl.pallas_call(
        route_kernel,
        out_shape=(
            shape((128, 128), I32),
            shape((16, 128), I32),
            shape((16, 128), I32),
            shape((32, 128), I32),
            shape((32, 128), I32),
        ),
        in_specs=[vmem(), vmem(), vmem(), smem(), smem()],
        out_specs=(vmem(),) * 5,
        compiler_params=ROOM,
        name="route",
    )(entry_shard, entry_row, depth_order, live_count, prev_slot)
    asked = swap(request)
    table = pl.pallas_call(
        project_kernel,
        out_shape=shape((9, 64, 128)),
        in_specs=[vmem()],
        out_specs=vmem(),
        compiler_params=ROOM,
        name="project",
    )(params)
    picked = pl.pallas_call(
        pick_kernel,
        out_shape=shape((384, 128)),
        in_specs=[vmem(), vmem()],
        out_specs=vmem(),
        compiler_params=ROOM,
        name="pick",
    )(asked, table)
    arrived = swap(picked)
    sent_truth = pl.pallas_call(
        truth_kernel,
        out_shape=shape((128, 768), BF16),
        in_specs=[vmem(), vmem()],
        out_specs=vmem(),
        compiler_params=ROOM,
        name="truth",
    )(asked, gt_image)
    delivered = swap(sent_truth)
    picture, loss, outgoing = pl.pallas_call(
        render_kernel,
        out_shape=(shape((16, 768)), shape((16, 128)), shape((384, 128))),
        in_specs=[vmem()] * 6 + [smem(), smem()],
        out_specs=(vmem(),) * 3,
        scratch_shapes=[
            pltpu.VMEM((384, 128), F32),
            pltpu.VMEM((9, 16, 128), F32),
            pltpu.VMEM((128, 4, 8, 128), F32),
            pltpu.VMEM((128, 4, 8, 128), F32),
            pltpu.VMEM((128, 4, 8, 128), F32),
            pltpu.VMEM((9, 16, 128), F32),
        ],
        compiler_params=ROOM,
        name="render",
    )(arrived, holder, place, back_j, back_t, delivered, tile_of_slot, prev_slot)
    returned = swap(outgoing)
    gradients = pl.pallas_call(
        update_kernel,
        out_shape=shape((59, 8192)),
        in_specs=[vmem()] * 3,
        out_specs=vmem(),
        scratch_shapes=[
            pltpu.VMEM((32, 128), I32),
            pltpu.VMEM((32, 128), I32),
            pltpu.VMEM((2, 288, 128), F32),
            pltpu.VMEM((288, 256), F32),
        ],
        compiler_params=ROOM,
        name="update",
    )(returned, asked, params)
    return (gradients, picture, loss[:, 0])


def solution(mesh):
    return jax.shard_map(
        body,
        mesh=mesh,
        in_specs=(
            P(None, "dev"),
            P("dev", None),
            P("dev", None),
            P("dev", None),
            P("dev"),
            P("dev"),
            P("dev"),
            P("dev", None),
        ),
        out_specs=(P(None, "dev"), P("dev", None), P("dev")),
        check_vma=False,
    )
```

```python
import jax
import jax.numpy as jnp
from jax import lax
from jax.experimental import pallas as pl
from jax.experimental.pallas import tpu as pltpu
from jax.sharding import PartitionSpec as P

TW = 240
TH = 135
FOCAL = 1200.0
LOG2E = 1.4426950408889634
F32 = jnp.float32
BF16 = jnp.bfloat16
I32 = jnp.int32


def iota(shape, axis):
    return lax.broadcasted_iota(I32, shape, axis)


def take_lane(table, index):
    return jnp.take_along_axis(table, index, axis=1, mode="promise_in_bounds")


def geometry(values):
    (pos_x, pos_y, depth, ls0, ls1, ls2, q0, q1, q2, q3, logit) = values
    scales = [jnp.exp(ls0), jnp.exp(ls1), jnp.exp(ls2)]
    inverse_q = lax.rsqrt(q0 * q0 + q1 * q1 + q2 * q2 + q3 * q3)
    w_part = q0 * inverse_q
    x_part = q1 * inverse_q
    y_part = q2 * inverse_q
    z_part = q3 * inverse_q
    rotation = [
        [
            1.0 - 2.0 * (y_part * y_part + z_part * z_part),
            2.0 * (x_part * y_part - w_part * z_part),
            2.0 * (x_part * z_part + w_part * y_part),
        ],
        [
            2.0 * (x_part * y_part + w_part * z_part),
            1.0 - 2.0 * (x_part * x_part + z_part * z_part),
            2.0 * (y_part * z_part - w_part * x_part),
        ],
        [
            2.0 * (x_part * z_part - w_part * y_part),
            2.0 * (y_part * z_part + w_part * x_part),
            1.0 - 2.0 * (x_part * x_part + y_part * y_part),
        ],
    ]
    inverse_z = 1.0 / depth
    focal_z = FOCAL * inverse_z
    ratio_x = pos_x * inverse_z
    ratio_y = pos_y * inverse_z
    slope_x = -focal_z * ratio_x
    slope_y = -focal_z * ratio_y
    first = [(focal_z * rotation[0][i] + slope_x * rotation[2][i]) * scales[i] for i in range(3)]
    second = [(focal_z * rotation[1][i] + slope_y * rotation[2][i]) * scales[i] for i in range(3)]
    spread_xx = first[0] * first[0] + first[1] * first[1] + first[2] * first[2] + 0.3
    spread_xy = first[0] * second[0] + first[1] * second[1] + first[2] * second[2]
    spread_yy = second[0] * second[0] + second[1] * second[1] + second[2] * second[2] + 0.3
    inverse_det = 1.0 / (spread_xx * spread_yy - spread_xy * spread_xy)
    inverse_norm = lax.rsqrt(pos_x * pos_x + pos_y * pos_y + depth * depth)
    return (
        FOCAL * pos_x / depth + 8.0 * TW,
        FOCAL * pos_y / depth + 8.0 * TH,
        spread_yy * inverse_det,
        -spread_xy * inverse_det,
        spread_xx * inverse_det,
        lax.logistic(logit),
        pos_x * inverse_norm,
        pos_y * inverse_norm,
        depth * inverse_norm,
    )


def harmonics(unit_x, unit_y, unit_z):
    square_x = unit_x * unit_x
    square_y = unit_y * unit_y
    square_z = unit_z * unit_z
    return [
        0.28209479177387814 * jnp.ones_like(unit_x),
        -0.4886025119029199 * unit_y,
        0.4886025119029199 * unit_z,
        -0.4886025119029199 * unit_x,
        1.0925484305920792 * unit_x * unit_y,
        -1.0925484305920792 * unit_y * unit_z,
        0.31539156525252005 * (2.0 * square_z - square_x - square_y),
        -1.0925484305920792 * unit_x * unit_z,
        0.5462742152960396 * (square_x - square_y),
        -0.5900435899266435 * unit_y * (3.0 * square_x - square_y),
        2.890611442640554 * unit_x * unit_y * unit_z,
        -0.4570457994644658 * unit_y * (4.0 * square_z - square_x - square_y),
        0.3731763325901154 * unit_z * (2.0 * square_z - 3.0 * square_x - 3.0 * square_y),
        -0.4570457994644658 * unit_x * (4.0 * square_z - square_x - square_y),
        1.445305721320277 * unit_z * (square_x - square_y),
        -0.5900435899266435 * unit_x * (square_x - 3.0 * square_y),
    ]


def split(value, pieces):
    parts = []
    for _ in range(pieces - 1):
        part = value.astype(BF16)
        parts.append(part)
        value = value - part.astype(F32)
    parts.append(value.astype(BF16))
    return parts


def contract_lanes(left, right):
    return lax.dot_general(left, right, (((1,), (1,)), ((), ())), preferred_element_type=F32)


def indicator(condition):
    return jnp.where(condition, 1.0, 0.0).astype(BF16)


def spread(row, count):
    return jnp.broadcast_to(row, (count, row.shape[1]))


def route_kernel(
    shard_hbm, row_hbm, order_hbm, live_hbm, prev_hbm, request_ref, holder_ref, place_ref,
    shard_ref, row_ref, order_ref, live_ref, prev_ref, sems,
):
    tiles, length = shard_ref.shape
    copies = [
        pltpu.make_async_copy(source, target, sems.at[n])
        for n, (source, target) in enumerate(
            [
                (order_hbm, order_ref),
                (shard_hbm, shard_ref),
                (row_hbm, row_ref),
                (live_hbm, live_ref),
                (prev_hbm, prev_ref),
            ]
        )
    ]
    for copy in copies:
        copy.start()
    for copy in copies:
        copy.wait()
    order = order_ref[...]
    shards = take_lane(shard_ref[...], order)
    rows = take_lane(row_ref[...], order)
    sub = iota((128, 128), 0)
    lane = iota((128, 128), 1)
    wide_row = iota((128, 256), 0)
    wide_lane = iota((128, 256), 1)
    counter = indicator((wide_lane >= 128) | (wide_row < wide_lane))
    sub_k = iota((32, 128), 0)
    carry = jnp.zeros((128, 128), F32)
    request = jnp.zeros((128, 128), F32)
    truth = jnp.zeros((128, 128), I32)
    nothing = jnp.zeros((96, 256), F32)
    for t in range(tiles):
        live = order[t : t + 1, :] < live_ref[t]
        holder = jnp.where(live, shards[t : t + 1, :], -1)
        match = spread(holder, 128) == sub
        hot = indicator(match)
        counted = jnp.dot(hot, counter, preferred_element_type=F32)
        place = jnp.sum(
            jnp.where(match, counted[:, :128] + carry, 0.0), axis=0, keepdims=True
        ).astype(I32)
        carry = carry + counted[:, 128:]
        holder_ref[t : t + 1, :] = holder
        place_ref[t : t + 1, :] = jnp.where(live, place, -1)
        match_k = spread(place, 32) == sub_k
        row = rows[t : t + 1, :]
        high = jnp.where(match_k, ((row >> 7) * 128).astype(F32), 0.0)
        low = jnp.where(match_k, (row & 127).astype(F32), 0.0)
        asked = jnp.concatenate(
            [jnp.concatenate([high, low], axis=1), nothing], axis=0
        ).astype(BF16)
        request = request + contract_lanes(jnp.concatenate([hot, hot], axis=1), asked)
        previous = prev_ref[t]
        truth = jnp.where(sub == lax.shift_right_logical(previous, 4), previous & 15, truth)
    request_ref[...] = jnp.where(lane == 32, truth, request.astype(I32))


def project_kernel(params_ref, out_ref, table_ref):
    def step(block, half):
        start = pl.multiple_of(half * 4096 + block * 1024, 1024)
        values = params_ref[:, pl.ds(start, 1024)].reshape(59, 8, 128)
        p = [values[i] for i in range(59)]
        (u, v, ca, cb, cc, opacity, ux, uy, uz) = geometry(p[:11])
        basis = harmonics(ux, uy, uz)
        colors = []
        for channel in range(3):
            color = 0.5 + basis[0] * p[11 + 16 * channel]
            for degree in range(1, 16):
                color = color + basis[degree] * p[11 + 16 * channel + degree]
            colors.append(color)
        for c, value in enumerate([u, v, ca, cb, cc] + colors + [opacity]):
            spot = pl.ds(pl.multiple_of(32 * c + 8 * block, 8), 8)
            table_ref[spot, 128 * half : 128 * half + 128] = value

    for half in range(2):
        lax.fori_loop(0, 4, lambda b, unused, half=half: (step(b, half), unused)[1], 0)
    for n, part in enumerate(split(table_ref[...], 3)):
        out_ref[288 * n : 288 * (n + 1), :] = part


def pick_kernel(
    asked_ref, table_ref, image_ref, out_ref, high_ref, low_ref, found_ref, stage_ref
):
    asked = asked_ref[...]
    index = asked.astype(F32).T[:32, :].astype(I32)
    high_ref[...] = (index >> 7) & 31
    low_ref[...] = (index & 127) + 128 * (index >> 12)
    sub_high = iota((32, 256), 0)
    sub_low = iota((256, 256), 0)
    for k in range(0, 32, 2):
        low = jnp.concatenate([low_ref[k : k + 1, :], low_ref[k + 1 : k + 2, :]], axis=1)
        high = jnp.concatenate([high_ref[k : k + 1, :], high_ref[k + 1 : k + 2, :]], axis=1)
        hot = indicator(spread(low, 256) == sub_low)
        parts = jnp.dot(table_ref[...], hot, preferred_element_type=F32)
        whole = parts[:288] + parts[288:576] + parts[576:]
        match = spread(high, 32) == sub_high
        for c in range(9):
            row = jnp.sum(
                jnp.where(match, whole[32 * c : 32 * c + 32], 0.0), axis=0, keepdims=True
            )
            found_ref[32 * c + k : 32 * c + k + 1, :] = row[:, :128]
            found_ref[32 * c + k + 1 : 32 * c + k + 2, :] = row[:, 128:]
    found_ref[288:, :] = jnp.zeros((96, 128), F32)
    truth = jnp.dot(
        indicator(asked[:, 32:33] == iota((128, 16), 1)), image_ref[...],
        preferred_element_type=F32,
    )
    for i in range(3):
        block = found_ref[128 * i : 128 * (i + 1), :].T
        for n, part in enumerate(split(block, 3)):
            stage_ref[pl.ds(3 * i + n, 128, stride=16), :] = part.astype(F32)
    for i in range(6):
        stage_ref[pl.ds(9 + i, 128, stride=16), :] = truth[:, 128 * i : 128 * (i + 1)]
    stage_ref[pl.ds(15, 128, stride=16), :] = jnp.zeros((128, 128), F32)
    out_ref[...] = stage_ref[...].astype(BF16)


def put_rows(out_ref, found_ref):
    for i in range(3):
        out_ref[pl.ds(i, 128, stride=4), :] = found_ref[128 * i : 128 * (i + 1), :].T
    out_ref[pl.ds(3, 128, stride=4), :] = jnp.zeros((128, 128), F32)


def swap_blocks(value):
    sub = iota((8, 128), 0)
    block = iota((8, 128), 1) >> 4
    for s in (4, 2, 1):
        up = pltpu.roll(pltpu.roll(value, 8 - s, 0), 16 * s, 1)
        down = up if s == 4 else pltpu.roll(pltpu.roll(value, s, 0), 128 - 16 * s, 1)
        sub_bit = sub & s
        block_bit = block & s
        value = jnp.where(
            sub_bit == block_bit, value, jnp.where(sub_bit < block_bit, up, down)
        )
    return value


def loss_and_slopes(images, target):
    loss = jnp.zeros((16, 1), F32)
    slopes = []
    for k in range(3):
        image = images[k]
        wanted = target[:, 256 * k : 256 * (k + 1)]
        difference = image - wanted
        smooth = jnp.sqrt(difference * difference + 0.0001)
        mean_r = jnp.sum(image, axis=1, keepdims=True) / 256.0
        mean_t = jnp.sum(wanted, axis=1, keepdims=True) / 256.0
        centered_r = image - mean_r
        centered_t = wanted - mean_t
        var_r = jnp.sum(centered_r * centered_r, axis=1, keepdims=True) / 256.0
        var_t = jnp.sum(centered_t * centered_t, axis=1, keepdims=True) / 256.0
        cov = jnp.sum(centered_r * centered_t, axis=1, keepdims=True) / 256.0
        top_m = 2.0 * mean_r * mean_t + 0.0001
        top_c = 2.0 * cov + 0.0009
        low_m = mean_r * mean_r + mean_t * mean_t + 0.0001
        low_v = var_r + var_t + 0.0009
        below = 1.0 / (low_m * low_v)
        similarity = top_m * top_c * below
        loss = loss + (0.8 / 3.0) * jnp.sum(smooth, axis=1, keepdims=True)
        loss = loss + (0.2 * 256.0 / 3.0) * (1.0 - similarity)
        by_mean = 2.0 * mean_t * top_c * below - similarity * 2.0 * mean_r / low_m
        by_cov = 2.0 * top_m * below
        by_var = -similarity / low_v
        slopes.append(
            (0.8 / 3.0) * difference / smooth
            - (0.2 / 3.0) * (by_mean + 2.0 * by_var * centered_r + by_cov * centered_t)
        )
    return loss, slopes


def render_kernel(
    arrived_ref, holder_ref, place_ref, tile_ref, prev_ref,
    picture_ref, loss_ref, out_ref, stage_ref,
    ordered_ref, row_ref, dx_ref, alpha_ref, weight_ref, reach_ref, moment_ref, found_ref,
):
    stage_ref[...] = arrived_ref[...].astype(F32)
    came = [stage_ref[pl.ds(i, 128, stride=16), :] for i in range(15)]
    table = [(came[3 * i] + came[3 * i + 1] + came[3 * i + 2]).T for i in range(3)]
    folded = []
    for c in range(9):
        part = table[c // 4][32 * (c % 4) : 32 * (c % 4) + 32, :]
        folded.append(jnp.concatenate([part[:16], part[16:]], axis=1))
    pieces = jnp.concatenate(split(jnp.concatenate(folded, axis=0), 3), axis=0)
    sub_slot = iota((256, 256), 0)
    sub_place = iota((16, 256), 0)
    for t in range(0, 16, 2):
        holder = jnp.concatenate([holder_ref[t : t + 1, :], holder_ref[t + 1 : t + 2, :]], axis=1)
        place = jnp.concatenate([place_ref[t : t + 1, :], place_ref[t + 1 : t + 2, :]], axis=1)
        hot = indicator(spread((place >> 4) * 128 + holder, 256) == sub_slot)
        parts = jnp.dot(pieces, hot, preferred_element_type=F32)
        whole = parts[:144] + parts[144:288] + parts[288:]
        match = spread(place & 15, 16) == sub_place
        for c in range(9):
            row = jnp.sum(
                jnp.where(match, whole[16 * c : 16 * c + 16], 0.0), axis=0, keepdims=True
            )
            ordered_ref[16 * c + t : 16 * c + t + 1, :] = row[:, :128]
            ordered_ref[16 * c + t + 1 : 16 * c + t + 2, :] = row[:, 128:]
    sub = iota((16, 128), 0)
    base_x = jnp.zeros((16, 128), F32)
    base_y = jnp.zeros((16, 128), F32)
    source = jnp.zeros((16, 128), I32)
    for t in range(16):
        number = tile_ref[t]
        tile_row = number // TW
        tile_column = number - tile_row * TW
        base_x = jnp.where(sub == t, (16 * tile_column + 8).astype(F32), base_x)
        base_y = jnp.where(sub == t, (16 * tile_row + 8).astype(F32), base_y)
        source = jnp.where(sub == t, lax.shift_right_logical(prev_ref[t], 4), source)
    ordered_ref[0:16, :] = ordered_ref[0:16, :] - base_x
    ordered_ref[16:32, :] = ordered_ref[16:32, :] - base_y
    ordered_ref[144:, :] = jnp.zeros((112, 128), F32)
    turned = [ordered_ref[0:128, :].T, ordered_ref[128:256, :].T]
    lane = iota((128, 128), 1)
    grid_x = (lane & 15).astype(F32) - 7.5
    for g in range(2):
        owner = (lane >> 4) + 8 * g

        def wide(c):
            return take_lane(turned[c // 8], owner + 16 * (c % 8))

        dx = grid_x - wide(0)
        dx_ref[g] = dx
        row_ref[g, 0] = (-0.5 * LOG2E) * wide(2) * dx * dx
        row_ref[g, 1] = (-LOG2E) * wide(3) * dx
        row_ref[g, 2] = (-0.5 * LOG2E) * wide(4)
        row_ref[g, 3] = wide(1)
        row_ref[g, 4] = wide(8)
        row_ref[g, 5] = wide(5)
        row_ref[g, 6] = wide(6)
        row_ref[g, 7] = wide(7)
    sub8 = iota((8, 128), 0)
    grid_y = [sub8.astype(F32) - 7.5, sub8.astype(F32) + 0.5]
    ones = jnp.ones((8, 128), F32)
    zero = jnp.zeros((8, 128), F32)

    def row_of(g, r, j):
        return spread(row_ref[g, r, pl.ds(j, 1), :], 8)

    def forward(j, state):
        reach = list(state[0])
        sums = list(state[1])
        for g in range(2):
            (part_a, part_b, part_c, gv, go, g0, g1, g2) = [row_of(g, r, j) for r in range(8)]
            for h in range(2):
                n = 2 * g + h
                dy = grid_y[h] - gv
                fall = jnp.exp2(part_a + dy * (part_b + part_c * dy))
                alpha = go * fall
                weight = alpha * reach[n]
                alpha_ref[j, n] = alpha
                weight_ref[j, n] = weight
                reach_ref[j, n] = fall * reach[n]
                reach[n] = reach[n] - weight
                sums[3 * n] = sums[3 * n] + weight * g0
                sums[3 * n + 1] = sums[3 * n + 1] + weight * g1
                sums[3 * n + 2] = sums[3 * n + 2] + weight * g2
        return (tuple(reach), tuple(sums))

    unused, sums = lax.fori_loop(
        0, 128, forward, (tuple([ones] * 4), tuple([zero] * 12)), unroll=4
    )
    chosen = indicator(source == iota((16, 128), 1))
    target = jnp.concatenate(
        [
            jnp.dot(chosen, came[9 + i].astype(BF16), preferred_element_type=F32)
            for i in range(6)
        ],
        axis=1,
    )
    images = []
    for k in range(3):
        image = jnp.concatenate(
            [
                jnp.concatenate(
                    [swap_blocks(sums[6 * g + k]), swap_blocks(sums[6 * g + 3 + k])], axis=1
                )
                for g in range(2)
            ],
            axis=0,
        )
        picture_ref[:, 256 * k : 256 * (k + 1)] = image
        images.append(image)
    loss, slopes = loss_and_slopes(images, target)
    loss_ref[...] = jnp.broadcast_to(loss, (16, 128))
    slope = [
        [
            swap_blocks(slopes[k][8 * g : 8 * g + 8, 128 * h : 128 * h + 128])
            for k in range(3)
        ]
        for g in range(2)
        for h in range(2)
    ]
    grid_yy = [grid_y[h] * grid_y[h] for h in range(2)]

    def fold(first, second, distance):
        bit = (sub8 & distance) != 0
        if distance == 4:
            return jnp.where(bit, second, first) + pltpu.roll(
                jnp.where(bit, first, second), 4, 0
            )
        return jnp.where(
            bit,
            second + pltpu.roll(second, distance, 0),
            first + pltpu.roll(first, 8 - distance, 0),
        )

    def backward(block, state):
        behind = list(state)
        base = pl.multiple_of(120 - 8 * block, 8)
        for g in range(2):
            waiting = {}
            for s in range(7, -1, -1):
                j = base + s
                (g0, g1, g2) = [row_of(g, r, j) for r in (5, 6, 7)]
                pulls = []
                shares = []
                for h in range(2):
                    n = 2 * g + h
                    value = slope[n][0] * g0 + slope[n][1] * g1 + slope[n][2] * g2
                    gap = value - behind[n]
                    pulls.append(reach_ref[j, n] * gap)
                    behind[n] = behind[n] + alpha_ref[j, n] * gap
                    weight = weight_ref[j, n]
                    shares.append([weight * slope[n][k] for k in range(3)])
                found = [
                    pulls[0] + pulls[1],
                    pulls[0] * grid_y[0] + pulls[1] * grid_y[1],
                    pulls[0] * grid_yy[0] + pulls[1] * grid_yy[1],
                    shares[0][0] + shares[1][0],
                    shares[0][1] + shares[1][1],
                    shares[0][2] + shares[1][2],
                ]
                spot = s
                for distance in (1, 2, 4):
                    if spot & distance:
                        break
                    above = waiting.pop((distance, spot + distance))
                    found = [fold(a, b, distance) for a, b in zip(found, above)]
                    if distance == 4:
                        for q in range(6):
                            moment_ref[g, q, pl.ds(base, 8), :] = found[q]
                else:
                    continue
                waiting[(distance, spot)] = found
        return tuple(behind)

    lax.fori_loop(0, 16, backward, tuple([zero] * 4))
    totals = jnp.zeros((16, 1152), F32)
    for g in range(2):
        dx = dx_ref[g]
        gv = row_ref[g, 3]
        m0 = moment_ref[g, 0]
        m1 = moment_ref[g, 1]
        sx = dx * m0
        sy = m1 - gv * m0
        syy = moment_ref[g, 2] - gv * (m1 + sy)
        stack = jnp.concatenate(
            [m0, sx, sy, dx * sx, dx * sy, syy]
            + [moment_ref[g, q] for q in range(3, 6)],
            axis=0,
        )
        tile = iota((16, 256), 0)
        pick = indicator(tile == ((iota((16, 256), 1) >> 4) & 7) + 8 * g)
        totals = totals + contract_lanes(pick, jnp.concatenate(split(stack, 2), axis=1))
    (m0, sx, sy, sxx, sxy, syy, d_red, d_green, d_blue) = [
        totals[:, 128 * c : 128 * c + 128] for c in range(9)
    ]
    (ca, cb, cc) = [ordered_ref[16 * c : 16 * c + 16, :] for c in (2, 3, 4)]
    opacity = ordered_ref[128:144, :]
    results = [
        opacity * (ca * sx + cb * sy),
        opacity * (cb * sx + cc * sy),
        -0.5 * opacity * sxx,
        -opacity * sxy,
        -0.5 * opacity * syy,
        d_red,
        d_green,
        d_blue,
        m0,
    ]
    parts = [[part.astype(F32) for part in split(result, 2)] for result in results]
    sub_k = iota((32, 128), 0)
    sub_h = iota((128, 128), 0)
    total = jnp.zeros((288, 128), F32)
    for t in range(0, 16, 2):
        hot = []
        left = [[], []]
        for tile in (t, t + 1):
            hot.append(indicator(spread(holder_ref[tile : tile + 1, :], 128) == sub_h))
            match = spread(place_ref[tile : tile + 1, :], 32) == sub_k
            for p in range(2):
                left[p].append(
                    jnp.concatenate(
                        [
                            jnp.where(match, parts[c][p][tile : tile + 1, :], 0.0)
                            for c in range(9)
                        ],
                        axis=0,
                    ).astype(BF16)
                )
        hot = jnp.concatenate(hot, axis=1)
        for p in range(2):
            total = total + contract_lanes(jnp.concatenate(left[p], axis=1), hot)
    found_ref[0:288, :] = total
    found_ref[288:, :] = jnp.zeros((96, 128), F32)
    put_rows(out_ref, found_ref)


def update_kernel(returned_ref, asked_ref, params_ref, out_ref, high_ref, low_ref, piece_ref, sum_ref):
    index = asked_ref[...].astype(F32).T[:32, :].astype(I32)
    high_ref[...] = (index >> 7) & 31
    low_ref[...] = (index & 127) + 128 * (index >> 12)
    for i in range(3):
        block = returned_ref[pl.ds(i, 128, stride=4), :].T
        rows = 128 if i < 2 else 32
        block = block[:rows, :]
        upper = block.astype(BF16).astype(F32)
        piece_ref[0, 128 * i : 128 * i + rows, :] = upper
        piece_ref[1, 128 * i : 128 * i + rows, :] = block - upper
    sum_ref[...] = jnp.zeros((288, 256), F32)
    sub_high = iota((32, 128), 0)
    sub_low = iota((256, 128), 0)

    def scatter(pair, unused):
        right = []
        left = [[], []]
        for half in range(2):
            k = 2 * pair + half
            low = jnp.broadcast_to(low_ref[pl.ds(k, 1), :], (256, 128))
            right.append(jnp.where(low == sub_low, 1.0, 0.0).astype(BF16))
            high = jnp.broadcast_to(high_ref[pl.ds(k, 1), :], (32, 128)) == sub_high
            for p in range(2):
                left[p].append(
                    jnp.concatenate(
                        [
                            jnp.where(high, piece_ref[p, pl.ds(32 * c + k, 1), :], 0.0)
                            for c in range(9)
                        ],
                        axis=0,
                    ).astype(BF16)
                )
        right = jnp.concatenate(right, axis=1)
        total = sum_ref[...]
        for p in range(2):
            total = total + lax.dot_general(
                jnp.concatenate(left[p], axis=1), right,
                (((1,), (1,)), ((), ())), preferred_element_type=F32,
            )
        sum_ref[...] = total
        return unused

    lax.fori_loop(0, 16, scatter, 0, unroll=16)

    def pull(block, half):
        start = pl.multiple_of(half * 4096 + block * 1024, 1024)
        values = params_ref[:, pl.ds(start, 1024)].reshape(59, 8, 128)
        p = [values[i] for i in range(59)]
        g = [
            sum_ref[pl.ds(pl.multiple_of(32 * c + 8 * block, 8), 8), 128 * half : 128 * half + 128]
            for c in range(9)
        ]
        primal, pull_geometry = jax.vjp(lambda *a: geometry(a), *p[:11])
        basis, pull_basis = jax.vjp(lambda *a: tuple(harmonics(*a)), *primal[6:9])
        d_basis = tuple(
            g[5] * p[11 + i] + g[6] * p[27 + i] + g[7] * p[43 + i] for i in range(16)
        )
        d_unit = pull_basis(d_basis)
        d_first = pull_geometry((g[0], g[1], g[2], g[3], g[4], g[8]) + tuple(d_unit))
        rows = list(d_first) + [g[5 + k] * basis[i] for k in range(3) for i in range(16)]
        out_ref[:, pl.ds(start, 1024)] = jnp.stack(rows, axis=0).reshape(59, 1024)

    for half in range(2):
        lax.fori_loop(0, 4, lambda b, unused, half=half: (pull(b, half), unused)[1], 0)


def vmem():
    return pl.BlockSpec(memory_space=pltpu.VMEM)


def smem():
    return pl.BlockSpec(memory_space=pltpu.SMEM)


def shape(dims, dtype=F32):
    return jax.ShapeDtypeStruct(dims, dtype)


ROOM = pltpu.CompilerParams(vmem_limit_bytes=40 * 1024 * 1024)


def swap(values):
    return lax.all_to_all(values, "dev", split_axis=0, concat_axis=0, tiled=True)


def swap_rows(values, rows):
    return swap(values.reshape(128, rows, 128)).reshape(128 * rows, 128)


def body(
    params, entry_shard, entry_row, depth_order, live_count, tile_of_slot, prev_slot, gt_image
):
    request, holder, place = pl.pallas_call(
        route_kernel,
        out_shape=(shape((128, 128), I32), shape((16, 128), I32), shape((16, 128), I32)),
        in_specs=[pl.BlockSpec(memory_space=pl.ANY)] * 5,
        out_specs=(vmem(),) * 3,
        scratch_shapes=[pltpu.VMEM((16, 128), I32)] * 3
        + [pltpu.SMEM((16,), I32)] * 2
        + [pltpu.SemaphoreType.DMA((5,))],
        compiler_params=pltpu.CompilerParams(vmem_limit_bytes=58 * 1024 * 1024),
        name="route",
    )(entry_shard, entry_row, depth_order, live_count, prev_slot)
    asked = swap(request)
    table = pl.pallas_call(
        project_kernel,
        out_shape=shape((864, 256), BF16),
        in_specs=[vmem()],
        out_specs=vmem(),
        scratch_shapes=[pltpu.VMEM((288, 256), F32)],
        compiler_params=ROOM,
        cost_estimate=pl.CostEstimate(
            flops=20_000_000, bytes_accessed=20_000_000, transcendentals=100_000
        ),
        name="project",
    )(params)
    picked = pl.pallas_call(
        pick_kernel,
        out_shape=shape((2048, 128), BF16),
        in_specs=[vmem(), vmem(), vmem()],
        out_specs=vmem(),
        scratch_shapes=[
            pltpu.VMEM((32, 128), I32),
            pltpu.VMEM((32, 128), I32),
            pltpu.VMEM((384, 128), F32),
            pltpu.VMEM((2048, 128), F32),
        ],
        compiler_params=ROOM,
        name="pick",
    )(asked, table, gt_image)
    arrived = swap_rows(picked, 16)
    picture, loss, outgoing = pl.pallas_call(
        render_kernel,
        out_shape=(shape((16, 768)), shape((16, 128)), shape((512, 128))),
        in_specs=[vmem()] * 3 + [smem(), smem()],
        out_specs=(vmem(),) * 3,
        scratch_shapes=[
            pltpu.VMEM((2048, 128), F32),
            pltpu.VMEM((256, 128), F32),
            pltpu.VMEM((2, 8, 128, 128), F32),
            pltpu.VMEM((2, 128, 128), F32),
            pltpu.VMEM((128, 4, 8, 128), F32),
            pltpu.VMEM((128, 4, 8, 128), F32),
            pltpu.VMEM((128, 4, 8, 128), F32),
            pltpu.VMEM((2, 6, 128, 128), F32),
            pltpu.VMEM((384, 128), F32),
        ],
        compiler_params=ROOM,
        name="render",
    )(arrived, holder, place, tile_of_slot, prev_slot)
    returned = swap_rows(outgoing, 4)
    gradients = pl.pallas_call(
        update_kernel,
        out_shape=shape((59, 8192)),
        in_specs=[vmem()] * 3,
        out_specs=vmem(),
        scratch_shapes=[
            pltpu.VMEM((32, 128), I32),
            pltpu.VMEM((32, 128), I32),
            pltpu.VMEM((2, 288, 128), F32),
            pltpu.VMEM((288, 256), F32),
        ],
        compiler_params=ROOM,
        name="update",
    )(returned, asked, params)
    return (gradients, picture, loss[:, 0])


def solution(mesh):
    return jax.shard_map(
        body,
        mesh=mesh,
        in_specs=(
            P(None, "dev"),
            P("dev", None),
            P("dev", None),
            P("dev", None),
            P("dev"),
            P("dev"),
            P("dev"),
            P("dev", None),
        ),
        out_specs=(P(None, "dev"), P("dev", None), P("dev")),
        check_vma=False,
    )
```

```python
import jax
import jax.numpy as jnp
from jax import lax
from jax.experimental import pallas as pl
from jax.experimental.pallas import tpu as pltpu
from jax.sharding import PartitionSpec as P

TW = 240
TH = 135
FOCAL = 1200.0
LOG2E = 1.4426950408889634
F32 = jnp.float32
BF16 = jnp.bfloat16
I32 = jnp.int32


def iota(shape, axis):
    return lax.broadcasted_iota(I32, shape, axis)


def take_lane(table, index):
    return jnp.take_along_axis(table, index, axis=1, mode="promise_in_bounds")


def conic(pos_x, pos_y, depth, ls0, ls1, ls2, q0, q1, q2, q3):
    scales = [jnp.exp(ls0), jnp.exp(ls1), jnp.exp(ls2)]
    inverse_q = lax.rsqrt(q0 * q0 + q1 * q1 + q2 * q2 + q3 * q3)
    w_part = q0 * inverse_q
    x_part = q1 * inverse_q
    y_part = q2 * inverse_q
    z_part = q3 * inverse_q
    rotation = [
        [
            1.0 - 2.0 * (y_part * y_part + z_part * z_part),
            2.0 * (x_part * y_part - w_part * z_part),
            2.0 * (x_part * z_part + w_part * y_part),
        ],
        [
            2.0 * (x_part * y_part + w_part * z_part),
            1.0 - 2.0 * (x_part * x_part + z_part * z_part),
            2.0 * (y_part * z_part - w_part * x_part),
        ],
        [
            2.0 * (x_part * z_part - w_part * y_part),
            2.0 * (y_part * z_part + w_part * x_part),
            1.0 - 2.0 * (x_part * x_part + y_part * y_part),
        ],
    ]
    inverse_z = 1.0 / depth
    focal_z = FOCAL * inverse_z
    ratio_x = pos_x * inverse_z
    ratio_y = pos_y * inverse_z
    slope_x = -focal_z * ratio_x
    slope_y = -focal_z * ratio_y
    first = [(focal_z * rotation[0][i] + slope_x * rotation[2][i]) * scales[i] for i in range(3)]
    second = [(focal_z * rotation[1][i] + slope_y * rotation[2][i]) * scales[i] for i in range(3)]
    spread_xx = first[0] * first[0] + first[1] * first[1] + first[2] * first[2] + 0.3
    spread_xy = first[0] * second[0] + first[1] * second[1] + first[2] * second[2]
    spread_yy = second[0] * second[0] + second[1] * second[1] + second[2] * second[2] + 0.3
    inverse_det = 1.0 / (spread_xx * spread_yy - spread_xy * spread_xy)
    return (spread_yy * inverse_det, -spread_xy * inverse_det, spread_xx * inverse_det)


def direction(pos_x, pos_y, depth):
    inverse_norm = lax.rsqrt(pos_x * pos_x + pos_y * pos_y + depth * depth)
    return (pos_x * inverse_norm, pos_y * inverse_norm, depth * inverse_norm)


def harmonics(unit_x, unit_y, unit_z):
    square_x = unit_x * unit_x
    square_y = unit_y * unit_y
    square_z = unit_z * unit_z
    return [
        0.28209479177387814 * jnp.ones_like(unit_x),
        -0.4886025119029199 * unit_y,
        0.4886025119029199 * unit_z,
        -0.4886025119029199 * unit_x,
        1.0925484305920792 * unit_x * unit_y,
        -1.0925484305920792 * unit_y * unit_z,
        0.31539156525252005 * (2.0 * square_z - square_x - square_y),
        -1.0925484305920792 * unit_x * unit_z,
        0.5462742152960396 * (square_x - square_y),
        -0.5900435899266435 * unit_y * (3.0 * square_x - square_y),
        2.890611442640554 * unit_x * unit_y * unit_z,
        -0.4570457994644658 * unit_y * (4.0 * square_z - square_x - square_y),
        0.3731763325901154 * unit_z * (2.0 * square_z - 3.0 * square_x - 3.0 * square_y),
        -0.4570457994644658 * unit_x * (4.0 * square_z - square_x - square_y),
        1.445305721320277 * unit_z * (square_x - square_y),
        -0.5900435899266435 * unit_x * (square_x - 3.0 * square_y),
    ]


def split(value, pieces):
    parts = []
    for _ in range(pieces - 1):
        part = value.astype(BF16)
        parts.append(part)
        value = value - part.astype(F32)
    parts.append(value.astype(BF16))
    return parts


def contract_lanes(left, right):
    return lax.dot_general(left, right, (((1,), (1,)), ((), ())), preferred_element_type=F32)


def indicator(condition):
    return jnp.where(condition, 1.0, 0.0).astype(BF16)


def spread(row, count):
    return jnp.broadcast_to(row, (count, row.shape[1]))


def pair_rows(ref, row, count):
    return jnp.concatenate(
        [spread(ref[pl.ds(row + n, 1), :], count) for n in range(2)], axis=1
    )


def route_kernel(
    shard_hbm, row_hbm, order_hbm, live_hbm, prev_hbm, request_ref, holder_ref, place_ref,
    shard_ref, row_ref, order_ref, live_ref, prev_ref, sems,
):
    tiles, length = shard_ref.shape
    copies = [
        pltpu.make_async_copy(source, target, sems.at[n])
        for n, (source, target) in enumerate(
            [
                (order_hbm, order_ref),
                (shard_hbm, shard_ref),
                (row_hbm, row_ref),
                (live_hbm, live_ref),
                (prev_hbm, prev_ref),
            ]
        )
    ]
    for copy in copies:
        copy.start()
    for copy in copies:
        copy.wait()
    order = order_ref[...]
    shards = take_lane(shard_ref[...], order)
    rows = take_lane(row_ref[...], order)
    sub = iota((128, 128), 0)
    lane = iota((128, 128), 1)
    wide_row = iota((128, 256), 0)
    wide_lane = iota((128, 256), 1)
    counter = indicator((wide_lane >= 128) | (wide_row < wide_lane))
    sub_k = iota((32, 128), 0)
    carry = jnp.zeros((128, 128), F32)
    request = jnp.zeros((128, 128), F32)
    truth = jnp.zeros((128, 128), I32)
    nothing = jnp.zeros((96, 256), F32)
    for t in range(tiles):
        live = order[t : t + 1, :] < live_ref[t]
        holder = jnp.where(live, shards[t : t + 1, :], -1)
        match = spread(holder, 128) == sub
        hot = indicator(match)
        counted = jnp.dot(hot, counter, preferred_element_type=F32)
        place = jnp.sum(
            jnp.where(match, counted[:, :128] + carry, 0.0), axis=0, keepdims=True
        ).astype(I32)
        carry = carry + counted[:, 128:]
        holder_ref[t : t + 1, :] = holder
        place_ref[t : t + 1, :] = jnp.where(live, place, -1)
        match_k = spread(place, 32) == sub_k
        row = rows[t : t + 1, :]
        high = jnp.where(match_k, ((row >> 7) * 128).astype(F32), 0.0)
        low = jnp.where(match_k, (row & 127).astype(F32), 0.0)
        asked = jnp.concatenate(
            [jnp.concatenate([high, low], axis=1), nothing], axis=0
        ).astype(BF16)
        request = request + contract_lanes(jnp.concatenate([hot, hot], axis=1), asked)
        previous = prev_ref[t]
        truth = jnp.where(sub == lax.shift_right_logical(previous, 4), previous & 15, truth)
    request_ref[...] = jnp.where(lane == 32, truth, request.astype(I32))


def project_kernel(params_ref, out_ref, table_ref):
    def step(block, half):
        start = pl.multiple_of(half * 4096 + block * 1024, 1024)
        values = params_ref[:, pl.ds(start, 1024)].reshape(59, 8, 128)
        p = [values[i] for i in range(59)]
        (ca, cb, cc) = conic(*p[:10])
        u = FOCAL * p[0] / p[2] + 8.0 * TW
        v = FOCAL * p[1] / p[2] + 8.0 * TH
        opacity = lax.logistic(p[10])
        basis = harmonics(*direction(*p[:3]))
        colors = []
        for channel in range(3):
            color = 0.5 + basis[0] * p[11 + 16 * channel]
            for degree in range(1, 16):
                color = color + basis[degree] * p[11 + 16 * channel + degree]
            colors.append(color)
        for c, value in enumerate([u, v, ca, cb, cc] + colors + [opacity]):
            spot = pl.ds(pl.multiple_of(32 * c + 8 * block, 8), 8)
            table_ref[spot, 128 * half : 128 * half + 128] = value

    for half in range(2):
        lax.fori_loop(0, 4, lambda b, unused, half=half: (step(b, half), unused)[1], 0)
    for n, part in enumerate(split(table_ref[...], 3)):
        out_ref[288 * n : 288 * (n + 1), :] = part


def pick_kernel(
    asked_ref, table_ref, image_ref, out_ref, high_ref, low_ref, found_ref, stage_ref
):
    asked = asked_ref[...]
    index = asked.astype(F32).T[:32, :].astype(I32)
    high_ref[...] = (index >> 7) & 31
    low_ref[...] = (index & 127) + 128 * (index >> 12)
    sub_high = iota((32, 256), 0)
    sub_low = iota((256, 256), 0)
    for k in range(0, 32, 2):
        hot = indicator(pair_rows(low_ref, k, 256) == sub_low)
        parts = jnp.dot(table_ref[...], hot, preferred_element_type=F32)
        whole = parts[:288] + parts[288:576] + parts[576:]
        match = pair_rows(high_ref, k, 32) == sub_high
        for c in range(9):
            row = jnp.sum(
                jnp.where(match, whole[32 * c : 32 * c + 32], 0.0), axis=0, keepdims=True
            )
            found_ref[32 * c + k : 32 * c + k + 1, :] = row[:, :128]
            found_ref[32 * c + k + 1 : 32 * c + k + 2, :] = row[:, 128:]
    found_ref[288:, :] = jnp.zeros((96, 128), F32)
    truth = jnp.dot(
        indicator(asked[:, 32:33] == iota((128, 16), 1)), image_ref[...],
        preferred_element_type=F32,
    )
    for i in range(3):
        block = found_ref[128 * i : 128 * (i + 1), :].T
        for n, part in enumerate(split(block, 3)):
            stage_ref[pl.ds(3 * i + n, 128, stride=16), :] = part.astype(F32)
    for i in range(6):
        stage_ref[pl.ds(9 + i, 128, stride=16), :] = truth[:, 128 * i : 128 * (i + 1)]
    stage_ref[pl.ds(15, 128, stride=16), :] = jnp.zeros((128, 128), F32)
    out_ref[...] = stage_ref[...].astype(BF16)


def put_rows(out_ref, found_ref):
    for i in range(3):
        out_ref[pl.ds(i, 128, stride=3), :] = found_ref[128 * i : 128 * (i + 1), :].T


def swap_blocks(value):
    sub = iota((8, 128), 0)
    block = iota((8, 128), 1) >> 4
    for s in (4, 2, 1):
        up = pltpu.roll(pltpu.roll(value, 8 - s, 0), 16 * s, 1)
        down = up if s == 4 else pltpu.roll(pltpu.roll(value, s, 0), 128 - 16 * s, 1)
        sub_bit = sub & s
        block_bit = block & s
        value = jnp.where(
            sub_bit == block_bit, value, jnp.where(sub_bit < block_bit, up, down)
        )
    return value


def loss_and_slopes(images, target):
    loss = jnp.zeros((16, 1), F32)
    slopes = []
    for k in range(3):
        image = images[k]
        wanted = target[:, 256 * k : 256 * (k + 1)]
        difference = image - wanted
        smooth = jnp.sqrt(difference * difference + 0.0001)
        mean_r = jnp.sum(image, axis=1, keepdims=True) / 256.0
        mean_t = jnp.sum(wanted, axis=1, keepdims=True) / 256.0
        centered_r = image - mean_r
        centered_t = wanted - mean_t
        var_r = jnp.sum(centered_r * centered_r, axis=1, keepdims=True) / 256.0
        var_t = jnp.sum(centered_t * centered_t, axis=1, keepdims=True) / 256.0
        cov = jnp.sum(centered_r * centered_t, axis=1, keepdims=True) / 256.0
        top_m = 2.0 * mean_r * mean_t + 0.0001
        top_c = 2.0 * cov + 0.0009
        low_m = mean_r * mean_r + mean_t * mean_t + 0.0001
        low_v = var_r + var_t + 0.0009
        below = 1.0 / (low_m * low_v)
        similarity = top_m * top_c * below
        loss = loss + (0.8 / 3.0) * jnp.sum(smooth, axis=1, keepdims=True)
        loss = loss + (0.2 * 256.0 / 3.0) * (1.0 - similarity)
        by_mean = 2.0 * mean_t * top_c * below - similarity * 2.0 * mean_r / low_m
        by_cov = 2.0 * top_m * below
        by_var = -similarity / low_v
        slopes.append(
            (0.8 / 3.0) * difference / smooth
            - (0.2 / 3.0) * (by_mean + 2.0 * by_var * centered_r + by_cov * centered_t)
        )
    return loss, slopes


def render_kernel(
    arrived_ref, holder_ref, place_ref, tile_ref, prev_ref,
    picture_ref, loss_ref, out_ref, stage_ref,
    ordered_ref, row_ref, dx_ref, alpha_ref, weight_ref, reach_ref, moment_ref, found_ref,
    code_ref, low_ref, part_ref,
):
    code_ref[...] = (place_ref[...] >> 4) * 128 + holder_ref[...]
    low_ref[...] = place_ref[...] & 15
    stage_ref[...] = arrived_ref[...].astype(F32)
    came = [stage_ref[pl.ds(i, 128, stride=16), :] for i in range(15)]
    table = [(came[3 * i] + came[3 * i + 1] + came[3 * i + 2]).T for i in range(3)]
    folded = []
    for c in range(9):
        part = table[c // 4][32 * (c % 4) : 32 * (c % 4) + 32, :]
        folded.append(jnp.concatenate([part[:16], part[16:]], axis=1))
    pieces = jnp.concatenate(split(jnp.concatenate(folded, axis=0), 3), axis=0)
    sub_slot = iota((256, 256), 0)
    sub_place = iota((16, 256), 0)

    def pick(pair, unused):
        t = 2 * pair
        hot = indicator(pair_rows(code_ref, t, 256) == sub_slot)
        parts = jnp.dot(pieces, hot, preferred_element_type=F32)
        whole = parts[:144] + parts[144:288] + parts[288:]
        match = pair_rows(low_ref, t, 16) == sub_place
        for c in range(9):
            row = jnp.sum(
                jnp.where(match, whole[16 * c : 16 * c + 16], 0.0), axis=0, keepdims=True
            )
            ordered_ref[pl.ds(16 * c + t, 1), :] = row[:, :128]
            ordered_ref[pl.ds(16 * c + t + 1, 1), :] = row[:, 128:]
        return unused

    lax.fori_loop(0, 8, pick, 0, unroll=PICK_UNROLL)
    sub = iota((16, 128), 0)
    base_x = jnp.zeros((16, 128), F32)
    base_y = jnp.zeros((16, 128), F32)
    source = jnp.zeros((16, 128), I32)
    for t in range(16):
        number = tile_ref[t]
        tile_row = number // TW
        tile_column = number - tile_row * TW
        base_x = jnp.where(sub == t, (16 * tile_column + 8).astype(F32), base_x)
        base_y = jnp.where(sub == t, (16 * tile_row + 8).astype(F32), base_y)
        source = jnp.where(sub == t, lax.shift_right_logical(prev_ref[t], 4), source)
    ordered_ref[0:16, :] = ordered_ref[0:16, :] - base_x
    ordered_ref[16:32, :] = ordered_ref[16:32, :] - base_y
    ordered_ref[144:, :] = jnp.zeros((112, 128), F32)
    turned = [ordered_ref[0:128, :].T, ordered_ref[128:256, :].T]
    lane = iota((128, 128), 1)
    grid_x = (lane & 15).astype(F32) - 7.5
    for g in range(2):
        owner = (lane >> 4) + 8 * g

        def wide(c):
            return take_lane(turned[c // 8], owner + 16 * (c % 8))

        dx = grid_x - wide(0)
        dx_ref[g] = dx
        row_ref[g, 0] = (-0.5 * LOG2E) * wide(2) * dx * dx
        row_ref[g, 1] = (-LOG2E) * wide(3) * dx
        row_ref[g, 2] = (-0.5 * LOG2E) * wide(4)
        row_ref[g, 3] = wide(1)
        row_ref[g, 4] = wide(8)
        row_ref[g, 5] = wide(5)
        row_ref[g, 6] = wide(6)
        row_ref[g, 7] = wide(7)
    sub8 = iota((8, 128), 0)
    grid_y = [sub8.astype(F32) - 7.5, sub8.astype(F32) + 0.5]
    ones = jnp.ones((8, 128), F32)
    zero = jnp.zeros((8, 128), F32)

    def row_of(g, r, j):
        return spread(row_ref[g, r, pl.ds(j, 1), :], 8)

    def forward(j, state):
        reach = list(state[0])
        sums = list(state[1])
        for g in range(2):
            (part_a, part_b, part_c, gv, go, g0, g1, g2) = [row_of(g, r, j) for r in range(8)]
            for h in range(2):
                n = 2 * g + h
                dy = grid_y[h] - gv
                fall = jnp.exp2(part_a + dy * (part_b + part_c * dy))
                alpha = go * fall
                weight = alpha * reach[n]
                alpha_ref[j, n] = alpha
                weight_ref[j, n] = weight
                reach_ref[j, n] = fall * reach[n]
                reach[n] = reach[n] - weight
                sums[3 * n] = sums[3 * n] + weight * g0
                sums[3 * n + 1] = sums[3 * n + 1] + weight * g1
                sums[3 * n + 2] = sums[3 * n + 2] + weight * g2
        return (tuple(reach), tuple(sums))

    unused, sums = lax.fori_loop(
        0, 128, forward, (tuple([ones] * 4), tuple([zero] * 12)), unroll=FORWARD_UNROLL
    )
    chosen = indicator(source == iota((16, 128), 1))
    target = jnp.concatenate(
        [
            jnp.dot(chosen, came[9 + i].astype(BF16), preferred_element_type=F32)
            for i in range(6)
        ],
        axis=1,
    )
    images = []
    for k in range(3):
        image = jnp.concatenate(
            [
                jnp.concatenate(
                    [swap_blocks(sums[6 * g + k]), swap_blocks(sums[6 * g + 3 + k])], axis=1
                )
                for g in range(2)
            ],
            axis=0,
        )
        picture_ref[:, 256 * k : 256 * (k + 1)] = image
        images.append(image)
    loss, slopes = loss_and_slopes(images, target)
    loss_ref[...] = jnp.broadcast_to(loss, (16, 128))
    slope = [
        [
            swap_blocks(slopes[k][8 * g : 8 * g + 8, 128 * h : 128 * h + 128])
            for k in range(3)
        ]
        for g in range(2)
        for h in range(2)
    ]
    grid_yy = [grid_y[h] * grid_y[h] for h in range(2)]

    def fold(first, second, distance):
        bit = (sub8 & distance) != 0
        if distance == 4:
            return jnp.where(bit, second, first) + pltpu.roll(
                jnp.where(bit, first, second), 4, 0
            )
        return jnp.where(
            bit,
            second + pltpu.roll(second, distance, 0),
            first + pltpu.roll(first, 8 - distance, 0),
        )

    def backward(block, state):
        behind = list(state)
        base = pl.multiple_of(120 - 8 * block, 8)
        for g in range(2):
            waiting = {}
            for s in range(7, -1, -1):
                j = base + s
                (g0, g1, g2) = [row_of(g, r, j) for r in (5, 6, 7)]
                pulls = []
                shares = []
                for h in range(2):
                    n = 2 * g + h
                    value = slope[n][0] * g0 + slope[n][1] * g1 + slope[n][2] * g2
                    gap = value - behind[n]
                    pulls.append(reach_ref[j, n] * gap)
                    behind[n] = behind[n] + alpha_ref[j, n] * gap
                    weight = weight_ref[j, n]
                    shares.append([weight * slope[n][k] for k in range(3)])
                found = [
                    pulls[0] + pulls[1],
                    pulls[0] * grid_y[0] + pulls[1] * grid_y[1],
                    pulls[0] * grid_yy[0] + pulls[1] * grid_yy[1],
                    shares[0][0] + shares[1][0],
                    shares[0][1] + shares[1][1],
                    shares[0][2] + shares[1][2],
                ]
                spot = s
                for distance in (1, 2, 4):
                    if spot & distance:
                        break
                    above = waiting.pop((distance, spot + distance))
                    found = [fold(a, b, distance) for a, b in zip(found, above)]
                    if distance == 4:
                        for q in range(6):
                            moment_ref[g, q, pl.ds(base, 8), :] = found[q]
                else:
                    continue
                waiting[(distance, spot)] = found
        return tuple(behind)

    lax.fori_loop(0, 16, backward, tuple([zero] * 4))
    totals = jnp.zeros((16, 1152), F32)
    for g in range(2):
        dx = dx_ref[g]
        gv = row_ref[g, 3]
        m0 = moment_ref[g, 0]
        m1 = moment_ref[g, 1]
        sx = dx * m0
        sy = m1 - gv * m0
        syy = moment_ref[g, 2] - gv * (m1 + sy)
        stack = jnp.concatenate(
            [m0, sx, sy, dx * sx, dx * sy, syy]
            + [moment_ref[g, q] for q in range(3, 6)],
            axis=0,
        )
        tile = iota((16, 256), 0)
        pick = indicator(tile == ((iota((16, 256), 1) >> 4) & 7) + 8 * g)
        totals = totals + contract_lanes(pick, jnp.concatenate(split(stack, 2), axis=1))
    (m0, sx, sy, sxx, sxy, syy, d_red, d_green, d_blue) = [
        totals[:, 128 * c : 128 * c + 128] for c in range(9)
    ]
    (ca, cb, cc) = [ordered_ref[16 * c : 16 * c + 16, :] for c in (2, 3, 4)]
    opacity = ordered_ref[128:144, :]
    results = [
        opacity * (ca * sx + cb * sy),
        opacity * (cb * sx + cc * sy),
        -0.5 * opacity * sxx,
        -opacity * sxy,
        -0.5 * opacity * syy,
        d_red,
        d_green,
        d_blue,
        m0,
    ]
    for c, result in enumerate(results):
        for p, part in enumerate(split(result, 2)):
            part_ref[p, 16 * c : 16 * c + 16, :] = part.astype(F32)
    sub_k = iota((32, 128), 0)
    sub_h = iota((128, 128), 0)

    def give(pair, total):
        hot = []
        left = [[], []]
        for n in range(2):
            tile = 2 * pair + n
            hot.append(indicator(spread(holder_ref[pl.ds(tile, 1), :], 128) == sub_h))
            match = spread(place_ref[pl.ds(tile, 1), :], 32) == sub_k
            for p in range(2):
                left[p].append(
                    jnp.concatenate(
                        [
                            jnp.where(match, part_ref[p, pl.ds(16 * c + tile, 1), :], 0.0)
                            for c in range(9)
                        ],
                        axis=0,
                    ).astype(BF16)
                )
        hot = jnp.concatenate(hot, axis=1)
        for p in range(2):
            total = total + contract_lanes(jnp.concatenate(left[p], axis=1), hot)
        return total

    total = lax.fori_loop(0, 8, give, jnp.zeros((288, 128), F32), unroll=GIVE_UNROLL)
    found_ref[0:288, :] = total
    found_ref[288:, :] = jnp.zeros((96, 128), F32)
    put_rows(out_ref, found_ref)


def update_kernel(
    returned_ref, asked_ref, params_ref, out_hbm,
    high_ref, low_ref, piece_ref, sum_ref, out_ref, sems,
):
    index = asked_ref[...].astype(F32).T[:32, :].astype(I32)
    high_ref[...] = (index >> 7) & 31
    low_ref[...] = (index & 127) + 128 * (index >> 12)
    for i in range(3):
        block = returned_ref[pl.ds(i, 128, stride=3), :].T
        rows = 128 if i < 2 else 32
        block = block[:rows, :]
        upper = block.astype(BF16).astype(F32)
        piece_ref[0, 128 * i : 128 * i + rows, :] = upper
        piece_ref[1, 128 * i : 128 * i + rows, :] = block - upper
    sub_high = iota((32, 128), 0)
    sub_low = iota((256, 256), 0)

    def scatter(pair, total):
        k = 2 * pair
        left = [[], []]
        for n in (k, k + 1):
            match = spread(high_ref[pl.ds(n, 1), :], 32) == sub_high
            for p in range(2):
                left[p].append(
                    jnp.concatenate(
                        [
                            jnp.where(match, piece_ref[p, pl.ds(32 * c + n, 1), :], 0.0)
                            for c in range(9)
                        ],
                        axis=0,
                    ).astype(BF16)
                )
        hot = indicator(pair_rows(low_ref, k, 256) == sub_low)
        for p in range(2):
            total = total + contract_lanes(jnp.concatenate(left[p], axis=1), hot)
        return total

    total = lax.fori_loop(0, 16, scatter, jnp.zeros((288, 256), F32), unroll=SCATTER_UNROLL)
    sum_ref[0] = total[:, :128]
    sum_ref[1] = total[:, 128:]
    early = iota((8, 128), 0) < 3

    def leave(block):
        span = pl.ds(pl.multiple_of(block * 1024, 1024), 1024)
        return pltpu.make_async_copy(out_ref.at[:, span], out_hbm.at[:, span], sems.at[block])

    def pull(place, half):
        block = place + 4 * half
        start = pl.multiple_of(block * 1024, 1024)
        values = params_ref[:, pl.ds(start, 1024)].reshape(59, 8, 128)
        p = [values[i] for i in range(59)]
        g = [
            sum_ref[half, pl.ds(pl.multiple_of(32 * c + 8 * place, 8), 8), :] for c in range(9)
        ]
        unused_conic, pull_conic = jax.vjp(conic, *p[:10])
        unit, pull_unit = jax.vjp(direction, *p[:3])
        basis, pull_basis = jax.vjp(lambda *d: tuple(harmonics(*d)), *unit)
        d_basis = tuple(
            g[5] * p[11 + i] + g[6] * p[27 + i] + g[7] * p[43 + i] for i in range(16)
        )
        first = list(pull_conic((g[2], g[3], g[4])))
        for i, slope in enumerate(pull_unit(pull_basis(d_basis))):
            first[i] = first[i] + slope
        focal_z = FOCAL / p[2]
        opacity = lax.logistic(p[10])
        first[0] = first[0] + g[0] * focal_z
        first[1] = first[1] + g[1] * focal_z
        first[2] = first[2] - focal_z * ((g[0] * p[0] + g[1] * p[1]) / p[2])
        first.append(g[8] * (opacity * (1.0 - opacity)))
        blank = jnp.zeros((8, 128), F32)

        def turn(rows):
            return jnp.stack(rows, axis=0).reshape(8, 1024)

        out_ref[0:8, pl.ds(start, 1024)] = turn(first[:8])
        rest = turn(first[8:] + [blank] * 5)
        ends_all = turn([basis[i] for i in (13, 14, 15, 0, 1, 2, 3, 4)])
        middle_all = turn([basis[i] for i in range(5, 13)])
        for s in range(8):
            column = pl.ds(pl.multiple_of(start + 128 * s, 128), 128)
            ends = ends_all[:, 128 * s : 128 * s + 128]
            middle = middle_all[:, 128 * s : 128 * s + 128]
            (red, green, blue) = [
                spread(sum_ref[half, pl.ds(32 * c + 8 * place + s, 1), :], 8) for c in (5, 6, 7)
            ]
            out_ref[8:16, column] = jnp.where(early, rest[:, 128 * s : 128 * s + 128], ends * red)
            out_ref[16:24, column] = middle * red
            out_ref[24:32, column] = ends * jnp.where(early, red, green)
            out_ref[32:40, column] = middle * green
            out_ref[40:48, column] = ends * jnp.where(early, green, blue)
            out_ref[48:56, column] = middle * blue
            out_ref[56:59, column] = (ends * blue)[:3]
        leave(block).start()

    for half in range(2):
        lax.fori_loop(0, 4, lambda b, unused, half=half: (pull(b, half), unused)[1], 0)
    for block in range(8):
        leave(block).wait()


def vmem():
    return pl.BlockSpec(memory_space=pltpu.VMEM)


def smem():
    return pl.BlockSpec(memory_space=pltpu.SMEM)


def anywhere():
    return pl.BlockSpec(memory_space=pl.ANY)


def shape(dims, dtype=F32):
    return jax.ShapeDtypeStruct(dims, dtype)


PICK_UNROLL = 4
FORWARD_UNROLL = 4
SCATTER_UNROLL = 16
GIVE_UNROLL = 4
WIDE = pltpu.CompilerParams(vmem_limit_bytes=58 * 1024 * 1024)
ROOM = pltpu.CompilerParams(vmem_limit_bytes=40 * 1024 * 1024)


def swap(values):
    return lax.all_to_all(values, "dev", split_axis=0, concat_axis=0, tiled=True)


def swap_rows(values, rows):
    return swap(values.reshape(128, rows, 128)).reshape(128 * rows, 128)


def body(
    params, entry_shard, entry_row, depth_order, live_count, tile_of_slot, prev_slot, gt_image
):
    request, holder, place = pl.pallas_call(
        route_kernel,
        out_shape=(shape((128, 128), I32), shape((16, 128), I32), shape((16, 128), I32)),
        in_specs=[anywhere()] * 5,
        out_specs=(vmem(),) * 3,
        scratch_shapes=[pltpu.VMEM((16, 128), I32)] * 3
        + [pltpu.SMEM((16,), I32)] * 2
        + [pltpu.SemaphoreType.DMA((5,))],
        compiler_params=WIDE,
        name="route",
    )(entry_shard, entry_row, depth_order, live_count, prev_slot)
    asked = swap(request)
    table = pl.pallas_call(
        project_kernel,
        out_shape=shape((864, 256), BF16),
        in_specs=[vmem()],
        out_specs=vmem(),
        scratch_shapes=[pltpu.VMEM((288, 256), F32)],
        compiler_params=ROOM,
        cost_estimate=pl.CostEstimate(
            flops=20_000_000, bytes_accessed=20_000_000, transcendentals=100_000
        ),
        name="project",
    )(params)
    picked = pl.pallas_call(
        pick_kernel,
        out_shape=shape((2048, 128), BF16),
        in_specs=[vmem(), vmem(), vmem()],
        out_specs=vmem(),
        scratch_shapes=[
            pltpu.VMEM((32, 128), I32),
            pltpu.VMEM((32, 128), I32),
            pltpu.VMEM((384, 128), F32),
            pltpu.VMEM((2048, 128), F32),
        ],
        compiler_params=ROOM,
        name="pick",
    )(asked, table, gt_image)
    arrived = swap_rows(picked, 16)
    picture, loss, outgoing = pl.pallas_call(
        render_kernel,
        out_shape=(shape((16, 768)), shape((16, 128)), shape((384, 128))),
        in_specs=[vmem()] * 3 + [smem(), smem()],
        out_specs=(vmem(),) * 3,
        scratch_shapes=[
            pltpu.VMEM((2048, 128), F32),
            pltpu.VMEM((256, 128), F32),
            pltpu.VMEM((2, 8, 128, 128), F32),
            pltpu.VMEM((2, 128, 128), F32),
            pltpu.VMEM((128, 4, 8, 128), F32),
            pltpu.VMEM((128, 4, 8, 128), F32),
            pltpu.VMEM((128, 4, 8, 128), F32),
            pltpu.VMEM((2, 6, 128, 128), F32),
            pltpu.VMEM((384, 128), F32),
            pltpu.VMEM((16, 128), I32),
            pltpu.VMEM((16, 128), I32),
            pltpu.VMEM((2, 144, 128), F32),
        ],
        compiler_params=ROOM,
        name="render",
    )(arrived, holder, place, tile_of_slot, prev_slot)
    returned = swap(outgoing.reshape(128, 1, 384)).reshape(384, 128)
    gradients = pl.pallas_call(
        update_kernel,
        out_shape=shape((59, 8192)),
        in_specs=[vmem(), vmem(), vmem()],
        out_specs=anywhere(),
        scratch_shapes=[
            pltpu.VMEM((32, 128), I32),
            pltpu.VMEM((32, 128), I32),
            pltpu.VMEM((2, 288, 128), F32),
            pltpu.VMEM((2, 288, 128), F32),
            pltpu.VMEM((59, 8192), F32),
            pltpu.SemaphoreType.DMA((8,)),
        ],
        compiler_params=ROOM,
        name="update",
    )(returned, asked, params)
    return (gradients, picture, loss[:, 0])


def solution(mesh):
    return jax.shard_map(
        body,
        mesh=mesh,
        in_specs=(
            P(None, "dev"),
            P("dev", None),
            P("dev", None),
            P("dev", None),
            P("dev"),
            P("dev"),
            P("dev"),
            P("dev", None),
        ),
        out_specs=(P(None, "dev"), P("dev", None), P("dev")),
        check_vma=False,
    )
```

```python
import jax
import jax.numpy as jnp
from jax import lax
from jax.experimental import pallas as pl
from jax.experimental.pallas import tpu as pltpu
from jax.sharding import PartitionSpec as P

TW = 240
TH = 135
FOCAL = 1200.0
LOG2E = 1.4426950408889634
F32 = jnp.float32
BF16 = jnp.bfloat16
I32 = jnp.int32


def iota(shape, axis):
    return lax.broadcasted_iota(I32, shape, axis)


def take_lane(table, index):
    return jnp.take_along_axis(table, index, axis=1, mode="promise_in_bounds")


def conic(pos_x, pos_y, depth, ls0, ls1, ls2, q0, q1, q2, q3):
    scales = [jnp.exp(ls0), jnp.exp(ls1), jnp.exp(ls2)]
    inverse_q = lax.rsqrt(q0 * q0 + q1 * q1 + q2 * q2 + q3 * q3)
    w_part = q0 * inverse_q
    x_part = q1 * inverse_q
    y_part = q2 * inverse_q
    z_part = q3 * inverse_q
    rotation = [
        [
            1.0 - 2.0 * (y_part * y_part + z_part * z_part),
            2.0 * (x_part * y_part - w_part * z_part),
            2.0 * (x_part * z_part + w_part * y_part),
        ],
        [
            2.0 * (x_part * y_part + w_part * z_part),
            1.0 - 2.0 * (x_part * x_part + z_part * z_part),
            2.0 * (y_part * z_part - w_part * x_part),
        ],
        [
            2.0 * (x_part * z_part - w_part * y_part),
            2.0 * (y_part * z_part + w_part * x_part),
            1.0 - 2.0 * (x_part * x_part + y_part * y_part),
        ],
    ]
    inverse_z = 1.0 / depth
    focal_z = FOCAL * inverse_z
    ratio_x = pos_x * inverse_z
    ratio_y = pos_y * inverse_z
    slope_x = -focal_z * ratio_x
    slope_y = -focal_z * ratio_y
    first = [(focal_z * rotation[0][i] + slope_x * rotation[2][i]) * scales[i] for i in range(3)]
    second = [(focal_z * rotation[1][i] + slope_y * rotation[2][i]) * scales[i] for i in range(3)]
    spread_xx = first[0] * first[0] + first[1] * first[1] + first[2] * first[2] + 0.3
    spread_xy = first[0] * second[0] + first[1] * second[1] + first[2] * second[2]
    spread_yy = second[0] * second[0] + second[1] * second[1] + second[2] * second[2] + 0.3
    inverse_det = 1.0 / (spread_xx * spread_yy - spread_xy * spread_xy)
    return (spread_yy * inverse_det, -spread_xy * inverse_det, spread_xx * inverse_det)


def direction(pos_x, pos_y, depth):
    inverse_norm = lax.rsqrt(pos_x * pos_x + pos_y * pos_y + depth * depth)
    return (pos_x * inverse_norm, pos_y * inverse_norm, depth * inverse_norm)


def harmonics(unit_x, unit_y, unit_z):
    square_x = unit_x * unit_x
    square_y = unit_y * unit_y
    square_z = unit_z * unit_z
    return [
        0.28209479177387814 * jnp.ones_like(unit_x),
        -0.4886025119029199 * unit_y,
        0.4886025119029199 * unit_z,
        -0.4886025119029199 * unit_x,
        1.0925484305920792 * unit_x * unit_y,
        -1.0925484305920792 * unit_y * unit_z,
        0.31539156525252005 * (2.0 * square_z - square_x - square_y),
        -1.0925484305920792 * unit_x * unit_z,
        0.5462742152960396 * (square_x - square_y),
        -0.5900435899266435 * unit_y * (3.0 * square_x - square_y),
        2.890611442640554 * unit_x * unit_y * unit_z,
        -0.4570457994644658 * unit_y * (4.0 * square_z - square_x - square_y),
        0.3731763325901154 * unit_z * (2.0 * square_z - 3.0 * square_x - 3.0 * square_y),
        -0.4570457994644658 * unit_x * (4.0 * square_z - square_x - square_y),
        1.445305721320277 * unit_z * (square_x - square_y),
        -0.5900435899266435 * unit_x * (square_x - 3.0 * square_y),
    ]


def split(value, pieces):
    parts = []
    for _ in range(pieces - 1):
        part = value.astype(BF16)
        parts.append(part)
        value = value - part.astype(F32)
    parts.append(value.astype(BF16))
    return parts


def contract_lanes(left, right):
    return lax.dot_general(left, right, (((1,), (1,)), ((), ())), preferred_element_type=F32)


def indicator(condition):
    return jnp.where(condition, 1.0, 0.0).astype(BF16)


def spread(row, count):
    return jnp.broadcast_to(row, (count, row.shape[1]))


def pair_rows(ref, row, count):
    return jnp.concatenate(
        [spread(ref[pl.ds(row + n, 1), :], count) for n in range(2)], axis=1
    )


def route_kernel(
    shard_hbm, row_hbm, order_hbm, live_hbm, prev_hbm, request_ref, holder_ref, place_ref,
    shard_ref, row_ref, order_ref, live_ref, prev_ref, sems,
):
    tiles, length = shard_ref.shape
    copies = [
        pltpu.make_async_copy(source, target, sems.at[n])
        for n, (source, target) in enumerate(
            [
                (order_hbm, order_ref),
                (shard_hbm, shard_ref),
                (row_hbm, row_ref),
                (live_hbm, live_ref),
                (prev_hbm, prev_ref),
            ]
        )
    ]
    for copy in copies:
        copy.start()
    for copy in copies:
        copy.wait()
    order = order_ref[...]
    shards = take_lane(shard_ref[...], order)
    rows = take_lane(row_ref[...], order)
    sub = iota((128, 128), 0)
    lane = iota((128, 128), 1)
    wide_row = iota((128, 256), 0)
    wide_lane = iota((128, 256), 1)
    counter = indicator((wide_lane >= 128) | (wide_row < wide_lane))
    sub_k = iota((32, 128), 0)
    carry = jnp.zeros((128, 128), F32)
    request = jnp.zeros((128, 32), F32)
    truth = jnp.zeros((128, 128), I32)
    for t in range(tiles):
        live = order[t : t + 1, :] < live_ref[t]
        holder = jnp.where(live, shards[t : t + 1, :], -1)
        match = spread(holder, 128) == sub
        hot = indicator(match)
        counted = jnp.dot(hot, counter, preferred_element_type=F32)
        place = jnp.sum(
            jnp.where(match, counted[:, :128] + carry, 0.0), axis=0, keepdims=True
        ).astype(I32)
        carry = carry + counted[:, 128:]
        holder_ref[t : t + 1, :] = holder
        place_ref[t : t + 1, :] = jnp.where(live, place, -1)
        match_k = spread(place, 32) == sub_k
        row = rows[t : t + 1, :]
        high = jnp.where(match_k, ((row >> 7) * 128).astype(F32), 0.0)
        low = jnp.where(match_k, (row & 127).astype(F32), 0.0)
        asked = jnp.concatenate([high, low], axis=1).astype(BF16)
        request = request + contract_lanes(jnp.concatenate([hot, hot], axis=1), asked)
        previous = prev_ref[t]
        truth = jnp.where(sub == lax.shift_right_logical(previous, 4), previous & 15, truth)
    wide = jnp.concatenate([request.astype(I32), jnp.zeros((128, 96), I32)], axis=1)
    request_ref[...] = jnp.where(lane == 32, truth, wide)


def project_kernel(params_ref, out_ref, table_ref):
    def step(block, half):
        start = pl.multiple_of(half * 4096 + block * 1024, 1024)
        values = params_ref[:, pl.ds(start, 1024)].reshape(59, 8, 128)
        p = [values[i] for i in range(59)]
        (ca, cb, cc) = conic(*p[:10])
        u = FOCAL * p[0] / p[2] + 8.0 * TW
        v = FOCAL * p[1] / p[2] + 8.0 * TH
        opacity = lax.logistic(p[10])
        basis = harmonics(*direction(*p[:3]))
        colors = []
        for channel in range(3):
            color = 0.5 + basis[0] * p[11 + 16 * channel]
            for degree in range(1, 16):
                color = color + basis[degree] * p[11 + 16 * channel + degree]
            colors.append(color)
        for c, value in enumerate([u, v, ca, cb, cc] + colors + [opacity]):
            spot = pl.ds(pl.multiple_of(32 * c + 8 * block, 8), 8)
            table_ref[spot, 128 * half : 128 * half + 128] = value

    for half in range(2):
        lax.fori_loop(0, 4, lambda b, unused, half=half: (step(b, half), unused)[1], 0)
    for n, part in enumerate(split(table_ref[...], 3)):
        out_ref[288 * n : 288 * (n + 1), :] = part


def pick_kernel(
    asked_ref, table_ref, image_ref, out_ref, high_ref, low_ref, found_ref, stage_ref
):
    asked = asked_ref[...]
    index = asked.astype(F32).T[:32, :].astype(I32)
    high_ref[...] = (index >> 7) & 31
    low_ref[...] = (index & 127) + 128 * (index >> 12)
    sub_high = iota((32, 256), 0)
    sub_low = iota((256, 256), 0)
    for k in range(0, 32, 2):
        hot = indicator(pair_rows(low_ref, k, 256) == sub_low)
        parts = jnp.dot(table_ref[...], hot, preferred_element_type=F32)
        whole = parts[:288] + parts[288:576] + parts[576:]
        match = pair_rows(high_ref, k, 32) == sub_high
        for c in range(9):
            row = jnp.sum(
                jnp.where(match, whole[32 * c : 32 * c + 32], 0.0), axis=0, keepdims=True
            )
            found_ref[32 * c + k : 32 * c + k + 1, :] = row[:, :128]
            found_ref[32 * c + k + 1 : 32 * c + k + 2, :] = row[:, 128:]
    upper, middle, lower = split(found_ref[128:160, :], 3)
    found_ref[320:352, :] = lower.astype(F32)
    found_ref[352:, :] = jnp.zeros((32, 128), F32)
    upper, lower = split(found_ref[256:288, :], 2)
    found_ref[256:288, :] = upper.astype(F32)
    found_ref[288:320, :] = lower.astype(F32)
    truth = jnp.dot(
        indicator(asked[:, 32:33] == iota((128, 16), 1)), image_ref[...],
        preferred_element_type=F32,
    )
    spot = 0
    for i in range(3):
        block = found_ref[128 * i : 128 * (i + 1), :].T
        for part in split(block, 3 - i):
            stage_ref[pl.ds(spot, 128, stride=12), :] = part.astype(F32)
            spot += 1
    for i in range(6):
        stage_ref[pl.ds(6 + i, 128, stride=12), :] = truth[:, 128 * i : 128 * (i + 1)]
    out_ref[...] = stage_ref[...].astype(BF16)


def put_rows(out_ref, found_ref):
    for i in range(3):
        out_ref[pl.ds(i, 128, stride=3), :] = found_ref[128 * i : 128 * (i + 1), :].T


def swap_blocks(value):
    sub = iota((8, 128), 0)
    block = iota((8, 128), 1) >> 4
    for s in (4, 2, 1):
        up = pltpu.roll(pltpu.roll(value, 8 - s, 0), 16 * s, 1)
        down = up if s == 4 else pltpu.roll(pltpu.roll(value, s, 0), 128 - 16 * s, 1)
        sub_bit = sub & s
        block_bit = block & s
        value = jnp.where(
            sub_bit == block_bit, value, jnp.where(sub_bit < block_bit, up, down)
        )
    return value


def loss_and_slopes(images, target):
    loss = jnp.zeros((16, 1), F32)
    slopes = []
    for k in range(3):
        image = images[k]
        wanted = target[:, 256 * k : 256 * (k + 1)]
        difference = image - wanted
        smooth = jnp.sqrt(difference * difference + 0.0001)
        mean_r = jnp.sum(image, axis=1, keepdims=True) / 256.0
        mean_t = jnp.sum(wanted, axis=1, keepdims=True) / 256.0
        centered_r = image - mean_r
        centered_t = wanted - mean_t
        var_r = jnp.sum(centered_r * centered_r, axis=1, keepdims=True) / 256.0
        var_t = jnp.sum(centered_t * centered_t, axis=1, keepdims=True) / 256.0
        cov = jnp.sum(centered_r * centered_t, axis=1, keepdims=True) / 256.0
        top_m = 2.0 * mean_r * mean_t + 0.0001
        top_c = 2.0 * cov + 0.0009
        low_m = mean_r * mean_r + mean_t * mean_t + 0.0001
        low_v = var_r + var_t + 0.0009
        below = 1.0 / (low_m * low_v)
        similarity = top_m * top_c * below
        loss = loss + (0.8 / 3.0) * jnp.sum(smooth, axis=1, keepdims=True)
        loss = loss + (0.2 * 256.0 / 3.0) * (1.0 - similarity)
        by_mean = 2.0 * mean_t * top_c * below - similarity * 2.0 * mean_r / low_m
        by_cov = 2.0 * top_m * below
        by_var = -similarity / low_v
        slopes.append(
            (0.8 / 3.0) * difference / smooth
            - (0.2 / 3.0) * (by_mean + 2.0 * by_var * centered_r + by_cov * centered_t)
        )
    return loss, slopes


def render_kernel(
    arrived_ref, holder_ref, place_ref, tile_ref, prev_ref,
    picture_ref, loss_ref, out_ref, stage_ref,
    ordered_ref, row_ref, dx_ref, alpha_ref, weight_ref, reach_ref, moment_ref, found_ref,
    code_ref, low_ref, part_ref,
):
    code_ref[...] = (place_ref[...] >> 4) * 128 + holder_ref[...]
    low_ref[...] = place_ref[...] & 15
    stage_ref[...] = arrived_ref[...].astype(F32)
    came = [stage_ref[pl.ds(i, 128, stride=12), :] for i in range(12)]
    table = [(came[0] + came[1] + came[2]).T, (came[3] + came[4]).T, came[5].T]
    folded = []
    for c in range(9):
        part = table[c // 4][32 * (c % 4) : 32 * (c % 4) + 32, :]
        if c == 4:
            part = part + table[2][64:96, :]
        if c == 8:
            part = part + table[2][32:64, :]
        folded.append(jnp.concatenate([part[:16], part[16:]], axis=1))
    pieces = jnp.concatenate(split(jnp.concatenate(folded, axis=0), 3), axis=0)
    sub_slot = iota((256, 256), 0)
    sub_place = iota((16, 256), 0)

    def pick(pair, unused):
        t = 2 * pair
        hot = indicator(pair_rows(code_ref, t, 256) == sub_slot)
        parts = jnp.dot(pieces, hot, preferred_element_type=F32)
        whole = parts[:144] + parts[144:288] + parts[288:]
        match = pair_rows(low_ref, t, 16) == sub_place
        for c in range(9):
            row = jnp.sum(
                jnp.where(match, whole[16 * c : 16 * c + 16], 0.0), axis=0, keepdims=True
            )
            ordered_ref[pl.ds(16 * c + t, 1), :] = row[:, :128]
            ordered_ref[pl.ds(16 * c + t + 1, 1), :] = row[:, 128:]
        return unused

    lax.fori_loop(0, 8, pick, 0, unroll=PICK_UNROLL)
    sub = iota((16, 128), 0)
    base_x = jnp.zeros((16, 128), F32)
    base_y = jnp.zeros((16, 128), F32)
    source = jnp.zeros((16, 128), I32)
    for t in range(16):
        number = tile_ref[t]
        tile_row = number // TW
        tile_column = number - tile_row * TW
        base_x = jnp.where(sub == t, (16 * tile_column + 8).astype(F32), base_x)
        base_y = jnp.where(sub == t, (16 * tile_row + 8).astype(F32), base_y)
        source = jnp.where(sub == t, lax.shift_right_logical(prev_ref[t], 4), source)
    ordered_ref[0:16, :] = ordered_ref[0:16, :] - base_x
    ordered_ref[16:32, :] = ordered_ref[16:32, :] - base_y
    ordered_ref[144:, :] = jnp.zeros((112, 128), F32)
    turned = [ordered_ref[0:128, :].T, ordered_ref[128:256, :].T]
    lane = iota((128, 128), 1)
    grid_x = (lane & 15).astype(F32) - 7.5
    for g in range(2):
        owner = (lane >> 4) + 8 * g

        def wide(c):
            return take_lane(turned[c // 8], owner + 16 * (c % 8))

        dx = grid_x - wide(0)
        dx_ref[g] = dx
        row_ref[g, 0] = (-0.5 * LOG2E) * wide(2) * dx * dx
        row_ref[g, 1] = (-LOG2E) * wide(3) * dx
        row_ref[g, 2] = (-0.5 * LOG2E) * wide(4)
        row_ref[g, 3] = wide(1)
        row_ref[g, 4] = wide(8)
        row_ref[g, 5] = wide(5)
        row_ref[g, 6] = wide(6)
        row_ref[g, 7] = wide(7)
    sub8 = iota((8, 128), 0)
    grid_y = [sub8.astype(F32) - 7.5, sub8.astype(F32) + 0.5]
    ones = jnp.ones((8, 128), F32)
    zero = jnp.zeros((8, 128), F32)

    def row_of(g, r, j):
        return spread(row_ref[g, r, pl.ds(j, 1), :], 8)

    def forward(j, state):
        reach = list(state[0])
        sums = list(state[1])
        for g in range(2):
            (part_a, part_b, part_c, gv, go, g0, g1, g2) = [row_of(g, r, j) for r in range(8)]
            for h in range(2):
                n = 2 * g + h
                dy = grid_y[h] - gv
                fall = jnp.exp2(part_a + dy * (part_b + part_c * dy))
                alpha = go * fall
                weight = alpha * reach[n]
                alpha_ref[j, n] = alpha
                weight_ref[j, n] = weight
                reach_ref[j, n] = fall * reach[n]
                reach[n] = reach[n] - weight
                sums[3 * n] = sums[3 * n] + weight * g0
                sums[3 * n + 1] = sums[3 * n + 1] + weight * g1
                sums[3 * n + 2] = sums[3 * n + 2] + weight * g2
        return (tuple(reach), tuple(sums))

    unused, sums = lax.fori_loop(
        0, 128, forward, (tuple([ones] * 4), tuple([zero] * 12)), unroll=FORWARD_UNROLL
    )
    chosen = indicator(source == iota((16, 128), 1))
    target = jnp.concatenate(
        [
            jnp.dot(chosen, came[6 + i].astype(BF16), preferred_element_type=F32)
            for i in range(6)
        ],
        axis=1,
    )
    images = []
    for k in range(3):
        image = jnp.concatenate(
            [
                jnp.concatenate(
                    [swap_blocks(sums[6 * g + k]), swap_blocks(sums[6 * g + 3 + k])], axis=1
                )
                for g in range(2)
            ],
            axis=0,
        )
        picture_ref[:, 256 * k : 256 * (k + 1)] = image
        images.append(image)
    loss, slopes = loss_and_slopes(images, target)
    loss_ref[...] = jnp.broadcast_to(loss, (16, 128))
    slope = [
        [
            swap_blocks(slopes[k][8 * g : 8 * g + 8, 128 * h : 128 * h + 128])
            for k in range(3)
        ]
        for g in range(2)
        for h in range(2)
    ]
    grid_yy = [grid_y[h] * grid_y[h] for h in range(2)]

    def fold(first, second, distance):
        bit = (sub8 & distance) != 0
        if distance == 4:
            return jnp.where(bit, second, first) + pltpu.roll(
                jnp.where(bit, first, second), 4, 0
            )
        return jnp.where(
            bit,
            second + pltpu.roll(second, distance, 0),
            first + pltpu.roll(first, 8 - distance, 0),
        )

    def backward(block, state):
        behind = list(state)
        base = pl.multiple_of(120 - 8 * block, 8)
        for g in range(2):
            waiting = {}
            for s in range(7, -1, -1):
                j = base + s
                (g0, g1, g2) = [row_of(g, r, j) for r in (5, 6, 7)]
                pulls = []
                shares = []
                for h in range(2):
                    n = 2 * g + h
                    value = slope[n][0] * g0 + slope[n][1] * g1 + slope[n][2] * g2
                    gap = value - behind[n]
                    pulls.append(reach_ref[j, n] * gap)
                    behind[n] = behind[n] + alpha_ref[j, n] * gap
                    weight = weight_ref[j, n]
                    shares.append([weight * slope[n][k] for k in range(3)])
                found = [
                    pulls[0] + pulls[1],
                    pulls[0] * grid_y[0] + pulls[1] * grid_y[1],
                    pulls[0] * grid_yy[0] + pulls[1] * grid_yy[1],
                    shares[0][0] + shares[1][0],
                    shares[0][1] + shares[1][1],
                    shares[0][2] + shares[1][2],
                ]
                spot = s
                for distance in (1, 2, 4):
                    if spot & distance:
                        break
                    above = waiting.pop((distance, spot + distance))
                    found = [fold(a, b, distance) for a, b in zip(found, above)]
                    if distance == 4:
                        for q in range(6):
                            moment_ref[g, q, pl.ds(base, 8), :] = found[q]
                else:
                    continue
                waiting[(distance, spot)] = found
        return tuple(behind)

    lax.fori_loop(0, 16, backward, tuple([zero] * 4))
    totals = jnp.zeros((16, 1152), F32)
    for g in range(2):
        dx = dx_ref[g]
        gv = row_ref[g, 3]
        m0 = moment_ref[g, 0]
        m1 = moment_ref[g, 1]
        sx = dx * m0
        sy = m1 - gv * m0
        syy = moment_ref[g, 2] - gv * (m1 + sy)
        stack = jnp.concatenate(
            [m0, sx, sy, dx * sx, dx * sy, syy]
            + [moment_ref[g, q] for q in range(3, 6)],
            axis=0,
        )
        tile = iota((16, 256), 0)
        pick = indicator(tile == ((iota((16, 256), 1) >> 4) & 7) + 8 * g)
        totals = totals + contract_lanes(pick, jnp.concatenate(split(stack, 2), axis=1))
    (m0, sx, sy, sxx, sxy, syy, d_red, d_green, d_blue) = [
        totals[:, 128 * c : 128 * c + 128] for c in range(9)
    ]
    (ca, cb, cc) = [ordered_ref[16 * c : 16 * c + 16, :] for c in (2, 3, 4)]
    opacity = ordered_ref[128:144, :]
    results = [
        opacity * (ca * sx + cb * sy),
        opacity * (cb * sx + cc * sy),
        -0.5 * opacity * sxx,
        -opacity * sxy,
        -0.5 * opacity * syy,
        d_red,
        d_green,
        d_blue,
        m0,
    ]
    for c, result in enumerate(results):
        for p, part in enumerate(split(result, 2)):
            part_ref[p, 16 * c : 16 * c + 16, :] = part.astype(F32)
    sub_k = iota((32, 128), 0)
    sub_h = iota((128, 128), 0)

    def give(pair, total):
        hot = []
        left = [[], []]
        for n in range(2):
            tile = 2 * pair + n
            hot.append(indicator(spread(holder_ref[pl.ds(tile, 1), :], 128) == sub_h))
            match = spread(place_ref[pl.ds(tile, 1), :], 32) == sub_k
            for p in range(2):
                left[p].append(
                    jnp.concatenate(
                        [
                            jnp.where(match, part_ref[p, pl.ds(16 * c + tile, 1), :], 0.0)
                            for c in range(9)
                        ],
                        axis=0,
                    ).astype(BF16)
                )
        hot = jnp.concatenate(hot, axis=1)
        for p in range(2):
            total = total + contract_lanes(jnp.concatenate(left[p], axis=1), hot)
        return total

    total = lax.fori_loop(0, 8, give, jnp.zeros((288, 128), F32), unroll=GIVE_UNROLL)
    found_ref[0:288, :] = total
    found_ref[288:, :] = jnp.zeros((96, 128), F32)
    put_rows(out_ref, found_ref)


def update_kernel(
    returned_ref, asked_ref, params_ref, out_hbm,
    high_ref, low_ref, piece_ref, sum_ref, out_ref, sems,
):
    index = asked_ref[...].astype(F32).T[:32, :].astype(I32)
    high_ref[...] = (index >> 7) & 31
    low_ref[...] = (index & 127) + 128 * (index >> 12)
    for i in range(3):
        block = returned_ref[pl.ds(i, 128, stride=3), :].T
        rows = 128 if i < 2 else 32
        block = block[:rows, :]
        upper = block.astype(BF16).astype(F32)
        piece_ref[0, 128 * i : 128 * i + rows, :] = upper
        piece_ref[1, 128 * i : 128 * i + rows, :] = block - upper
    sub_high = iota((32, 128), 0)
    sub_low = iota((256, 256), 0)

    def scatter(pair, total):
        k = 2 * pair
        left = [[], []]
        for n in (k, k + 1):
            match = spread(high_ref[pl.ds(n, 1), :], 32) == sub_high
            for p in range(2):
                left[p].append(
                    jnp.concatenate(
                        [
                            jnp.where(match, piece_ref[p, pl.ds(32 * c + n, 1), :], 0.0)
                            for c in range(9)
                        ],
                        axis=0,
                    ).astype(BF16)
                )
        hot = indicator(pair_rows(low_ref, k, 256) == sub_low)
        for p in range(2):
            total = total + contract_lanes(jnp.concatenate(left[p], axis=1), hot)
        return total

    total = lax.fori_loop(0, 16, scatter, jnp.zeros((288, 256), F32), unroll=SCATTER_UNROLL)
    sum_ref[0] = total[:, :128]
    sum_ref[1] = total[:, 128:]
    early = iota((8, 128), 0) < 3

    def leave(block):
        span = pl.ds(pl.multiple_of(block * 1024, 1024), 1024)
        return pltpu.make_async_copy(out_ref.at[:, span], out_hbm.at[:, span], sems.at[block])

    def pull(place, half):
        block = place + 4 * half
        start = pl.multiple_of(block * 1024, 1024)
        values = params_ref[:, pl.ds(start, 1024)].reshape(59, 8, 128)
        p = [values[i] for i in range(59)]
        g = [
            sum_ref[half, pl.ds(pl.multiple_of(32 * c + 8 * place, 8), 8), :] for c in range(9)
        ]
        unused_conic, pull_conic = jax.vjp(conic, *p[:10])
        unit, pull_unit = jax.vjp(direction, *p[:3])
        basis, pull_basis = jax.vjp(lambda *d: tuple(harmonics(*d)), *unit)
        d_basis = tuple(
            g[5] * p[11 + i] + g[6] * p[27 + i] + g[7] * p[43 + i] for i in range(16)
        )
        first = list(pull_conic((g[2], g[3], g[4])))
        for i, slope in enumerate(pull_unit(pull_basis(d_basis))):
            first[i] = first[i] + slope
        focal_z = FOCAL / p[2]
        opacity = lax.logistic(p[10])
        first[0] = first[0] + g[0] * focal_z
        first[1] = first[1] + g[1] * focal_z
        first[2] = first[2] - focal_z * ((g[0] * p[0] + g[1] * p[1]) / p[2])
        first.append(g[8] * (opacity * (1.0 - opacity)))
        blank = jnp.zeros((8, 128), F32)

        def turn(rows):
            return jnp.stack(rows, axis=0).reshape(8, 1024)

        out_ref[0:8, pl.ds(start, 1024)] = turn(first[:8])
        rest = turn(first[8:] + [blank] * 5)
        ends_all = turn([basis[i] for i in (13, 14, 15, 0, 1, 2, 3, 4)])
        middle_all = turn([basis[i] for i in range(5, 13)])
        for s in range(8):
            column = pl.ds(pl.multiple_of(start + 128 * s, 128), 128)
            ends = ends_all[:, 128 * s : 128 * s + 128]
            middle = middle_all[:, 128 * s : 128 * s + 128]
            (red, green, blue) = [
                spread(sum_ref[half, pl.ds(32 * c + 8 * place + s, 1), :], 8) for c in (5, 6, 7)
            ]
            out_ref[8:16, column] = jnp.where(early, rest[:, 128 * s : 128 * s + 128], ends * red)
            out_ref[16:24, column] = middle * red
            out_ref[24:32, column] = ends * jnp.where(early, red, green)
            out_ref[32:40, column] = middle * green
            out_ref[40:48, column] = ends * jnp.where(early, green, blue)
            out_ref[48:56, column] = middle * blue
            out_ref[56:59, column] = (ends * blue)[:3]
        leave(block).start()

    for half in range(2):
        lax.fori_loop(0, 4, lambda b, unused, half=half: (pull(b, half), unused)[1], 0)
    for block in range(8):
        leave(block).wait()


def vmem():
    return pl.BlockSpec(memory_space=pltpu.VMEM)


def smem():
    return pl.BlockSpec(memory_space=pltpu.SMEM)


def anywhere():
    return pl.BlockSpec(memory_space=pl.ANY)


def shape(dims, dtype=F32):
    return jax.ShapeDtypeStruct(dims, dtype)


PICK_UNROLL = 4
FORWARD_UNROLL = 4
SCATTER_UNROLL = 16
GIVE_UNROLL = 4
WIDE = pltpu.CompilerParams(vmem_limit_bytes=58 * 1024 * 1024)
ROOM = pltpu.CompilerParams(vmem_limit_bytes=40 * 1024 * 1024)


def swap(values):
    return lax.all_to_all(values, "dev", split_axis=0, concat_axis=0, tiled=True)


def body(
    params, entry_shard, entry_row, depth_order, live_count, tile_of_slot, prev_slot, gt_image
):
    request, holder, place = pl.pallas_call(
        route_kernel,
        out_shape=(shape((128, 128), I32), shape((16, 128), I32), shape((16, 128), I32)),
        in_specs=[anywhere()] * 5,
        out_specs=(vmem(),) * 3,
        scratch_shapes=[pltpu.VMEM((16, 128), I32)] * 3
        + [pltpu.SMEM((16,), I32)] * 2
        + [pltpu.SemaphoreType.DMA((5,))],
        compiler_params=WIDE,
        name="route",
    )(entry_shard, entry_row, depth_order, live_count, prev_slot)
    asked = swap(request)
    table = pl.pallas_call(
        project_kernel,
        out_shape=shape((864, 256), BF16),
        in_specs=[vmem()],
        out_specs=vmem(),
        scratch_shapes=[pltpu.VMEM((288, 256), F32)],
        compiler_params=ROOM,
        cost_estimate=pl.CostEstimate(
            flops=20_000_000, bytes_accessed=20_000_000, transcendentals=100_000
        ),
        name="project",
    )(params)
    picked = pl.pallas_call(
        pick_kernel,
        out_shape=shape((1536, 128), BF16),
        in_specs=[vmem(), vmem(), vmem()],
        out_specs=vmem(),
        scratch_shapes=[
            pltpu.VMEM((32, 128), I32),
            pltpu.VMEM((32, 128), I32),
            pltpu.VMEM((384, 128), F32),
            pltpu.VMEM((1536, 128), F32),
        ],
        compiler_params=ROOM,
        name="pick",
    )(asked, table, gt_image)
    arrived = swap(picked.reshape(128, 3, 4, 128)).reshape(1536, 128)
    picture, loss, outgoing = pl.pallas_call(
        render_kernel,
        out_shape=(shape((16, 768)), shape((16, 128)), shape((384, 128))),
        in_specs=[vmem()] * 3 + [smem(), smem()],
        out_specs=(vmem(),) * 3,
        scratch_shapes=[
            pltpu.VMEM((1536, 128), F32),
            pltpu.VMEM((256, 128), F32),
            pltpu.VMEM((2, 8, 128, 128), F32),
            pltpu.VMEM((2, 128, 128), F32),
            pltpu.VMEM((128, 4, 8, 128), F32),
            pltpu.VMEM((128, 4, 8, 128), F32),
            pltpu.VMEM((128, 4, 8, 128), F32),
            pltpu.VMEM((2, 6, 128, 128), F32),
            pltpu.VMEM((384, 128), F32),
            pltpu.VMEM((16, 128), I32),
            pltpu.VMEM((16, 128), I32),
            pltpu.VMEM((2, 144, 128), F32),
        ],
        compiler_params=ROOM,
        name="render",
    )(arrived, holder, place, tile_of_slot, prev_slot)
    returned = swap(outgoing.reshape(128, 1, 384)).reshape(384, 128)
    gradients = pl.pallas_call(
        update_kernel,
        out_shape=shape((59, 8192)),
        in_specs=[vmem(), vmem(), vmem()],
        out_specs=anywhere(),
        scratch_shapes=[
            pltpu.VMEM((32, 128), I32),
            pltpu.VMEM((32, 128), I32),
            pltpu.VMEM((2, 288, 128), F32),
            pltpu.VMEM((2, 288, 128), F32),
            pltpu.VMEM((59, 8192), F32),
            pltpu.SemaphoreType.DMA((8,)),
        ],
        compiler_params=ROOM,
        name="update",
    )(returned, asked, params)
    return (gradients, picture, loss[:, 0])


def solution(mesh):
    return jax.shard_map(
        body,
        mesh=mesh,
        in_specs=(
            P(None, "dev"),
            P("dev", None),
            P("dev", None),
            P("dev", None),
            P("dev"),
            P("dev"),
            P("dev"),
            P("dev", None),
        ),
        out_specs=(P(None, "dev"), P("dev", None), P("dev")),
        check_vma=False,
    )
```

```python
import jax
import jax.numpy as jnp
from jax import lax
from jax.experimental import pallas as pl
from jax.experimental.pallas import tpu as pltpu
from jax.sharding import PartitionSpec as P

TW = 240
TH = 135
FOCAL = 1200.0
LOG2E = 1.4426950408889634
F32 = jnp.float32
BF16 = jnp.bfloat16
I32 = jnp.int32


def iota(shape, axis):
    return lax.broadcasted_iota(I32, shape, axis)


def take_lane(table, index):
    return jnp.take_along_axis(table, index, axis=1, mode="promise_in_bounds")


def conic(pos_x, pos_y, depth, ls0, ls1, ls2, q0, q1, q2, q3):
    scales = [jnp.exp(ls0), jnp.exp(ls1), jnp.exp(ls2)]
    inverse_q = lax.rsqrt(q0 * q0 + q1 * q1 + q2 * q2 + q3 * q3)
    w_part = q0 * inverse_q
    x_part = q1 * inverse_q
    y_part = q2 * inverse_q
    z_part = q3 * inverse_q
    rotation = [
        [
            1.0 - 2.0 * (y_part * y_part + z_part * z_part),
            2.0 * (x_part * y_part - w_part * z_part),
            2.0 * (x_part * z_part + w_part * y_part),
        ],
        [
            2.0 * (x_part * y_part + w_part * z_part),
            1.0 - 2.0 * (x_part * x_part + z_part * z_part),
            2.0 * (y_part * z_part - w_part * x_part),
        ],
        [
            2.0 * (x_part * z_part - w_part * y_part),
            2.0 * (y_part * z_part + w_part * x_part),
            1.0 - 2.0 * (x_part * x_part + y_part * y_part),
        ],
    ]
    inverse_z = 1.0 / depth
    focal_z = FOCAL * inverse_z
    ratio_x = pos_x * inverse_z
    ratio_y = pos_y * inverse_z
    slope_x = -focal_z * ratio_x
    slope_y = -focal_z * ratio_y
    first = [(focal_z * rotation[0][i] + slope_x * rotation[2][i]) * scales[i] for i in range(3)]
    second = [(focal_z * rotation[1][i] + slope_y * rotation[2][i]) * scales[i] for i in range(3)]
    spread_xx = first[0] * first[0] + first[1] * first[1] + first[2] * first[2] + 0.3
    spread_xy = first[0] * second[0] + first[1] * second[1] + first[2] * second[2]
    spread_yy = second[0] * second[0] + second[1] * second[1] + second[2] * second[2] + 0.3
    inverse_det = 1.0 / (spread_xx * spread_yy - spread_xy * spread_xy)
    return (spread_yy * inverse_det, -spread_xy * inverse_det, spread_xx * inverse_det)


def direction(pos_x, pos_y, depth):
    inverse_norm = lax.rsqrt(pos_x * pos_x + pos_y * pos_y + depth * depth)
    return (pos_x * inverse_norm, pos_y * inverse_norm, depth * inverse_norm)


def harmonics(unit_x, unit_y, unit_z):
    square_x = unit_x * unit_x
    square_y = unit_y * unit_y
    square_z = unit_z * unit_z
    return [
        0.28209479177387814 * jnp.ones_like(unit_x),
        -0.4886025119029199 * unit_y,
        0.4886025119029199 * unit_z,
        -0.4886025119029199 * unit_x,
        1.0925484305920792 * unit_x * unit_y,
        -1.0925484305920792 * unit_y * unit_z,
        0.31539156525252005 * (2.0 * square_z - square_x - square_y),
        -1.0925484305920792 * unit_x * unit_z,
        0.5462742152960396 * (square_x - square_y),
        -0.5900435899266435 * unit_y * (3.0 * square_x - square_y),
        2.890611442640554 * unit_x * unit_y * unit_z,
        -0.4570457994644658 * unit_y * (4.0 * square_z - square_x - square_y),
        0.3731763325901154 * unit_z * (2.0 * square_z - 3.0 * square_x - 3.0 * square_y),
        -0.4570457994644658 * unit_x * (4.0 * square_z - square_x - square_y),
        1.445305721320277 * unit_z * (square_x - square_y),
        -0.5900435899266435 * unit_x * (square_x - 3.0 * square_y),
    ]


def split(value, pieces):
    parts = []
    for _ in range(pieces - 1):
        part = value.astype(BF16)
        parts.append(part)
        value = value - part.astype(F32)
    parts.append(value.astype(BF16))
    return parts


def contract_lanes(left, right):
    return lax.dot_general(left, right, (((1,), (1,)), ((), ())), preferred_element_type=F32)


def indicator(condition):
    return jnp.where(condition, 1.0, 0.0).astype(BF16)


def spread(row, count):
    return jnp.broadcast_to(row, (count, row.shape[1]))


def pair_rows(ref, row, count):
    return jnp.concatenate(
        [spread(ref[pl.ds(row + n, 1), :], count) for n in range(2)], axis=1
    )


def route_kernel(
    shard_hbm, row_hbm, order_hbm, live_hbm, prev_hbm, request_ref, holder_ref, place_ref,
    shard_ref, row_ref, order_ref, live_ref, prev_ref, sems,
):
    tiles, length = shard_ref.shape
    copies = [
        pltpu.make_async_copy(source, target, sems.at[n])
        for n, (source, target) in enumerate(
            [
                (order_hbm, order_ref),
                (shard_hbm, shard_ref),
                (row_hbm, row_ref),
                (live_hbm, live_ref),
                (prev_hbm, prev_ref),
            ]
        )
    ]
    for copy in copies:
        copy.start()
    for copy in copies:
        copy.wait()
    order = order_ref[...]
    shards = take_lane(shard_ref[...], order)
    rows = take_lane(row_ref[...], order)
    sub = iota((128, 128), 0)
    lane = iota((128, 128), 1)
    wide_row = iota((128, 256), 0)
    wide_lane = iota((128, 256), 1)
    counter = indicator((wide_lane >= 128) | (wide_row < wide_lane))
    sub_k = iota((32, 128), 0)
    carry = jnp.zeros((128, 128), F32)
    request = jnp.zeros((128, 32), F32)
    truth = jnp.zeros((128, 128), I32)
    for t in range(tiles):
        live = order[t : t + 1, :] < live_ref[t]
        holder = jnp.where(live, shards[t : t + 1, :], -1)
        match = spread(holder, 128) == sub
        hot = indicator(match)
        counted = jnp.dot(hot, counter, preferred_element_type=F32)
        place = jnp.sum(
            jnp.where(match, counted[:, :128] + carry, 0.0), axis=0, keepdims=True
        ).astype(I32)
        carry = carry + counted[:, 128:]
        holder_ref[t : t + 1, :] = holder
        place_ref[t : t + 1, :] = jnp.where(live, place, -1)
        match_k = spread(place, 32) == sub_k
        row = rows[t : t + 1, :]
        high = jnp.where(match_k, ((row >> 7) * 128).astype(F32), 0.0)
        low = jnp.where(match_k, (row & 127).astype(F32), 0.0)
        asked = jnp.concatenate([high, low], axis=1).astype(BF16)
        request = request + contract_lanes(jnp.concatenate([hot, hot], axis=1), asked)
        previous = prev_ref[t]
        truth = jnp.where(sub == lax.shift_right_logical(previous, 4), previous & 15, truth)
    wide = jnp.concatenate([request.astype(I32), jnp.zeros((128, 96), I32)], axis=1)
    request_ref[...] = jnp.where(lane == 32, truth, wide)


def project_kernel(params_ref, out_ref, table_ref):
    def step(block, half):
        start = pl.multiple_of(half * 4096 + block * 1024, 1024)
        values = params_ref[:, pl.ds(start, 1024)].reshape(59, 8, 128)
        p = [values[i] for i in range(59)]
        (ca, cb, cc) = conic(*p[:10])
        u = FOCAL * p[0] / p[2] + 8.0 * TW
        v = FOCAL * p[1] / p[2] + 8.0 * TH
        opacity = lax.logistic(p[10])
        basis = harmonics(*direction(*p[:3]))
        colors = []
        for channel in range(3):
            color = 0.5 + basis[0] * p[11 + 16 * channel]
            for degree in range(1, 16):
                color = color + basis[degree] * p[11 + 16 * channel + degree]
            colors.append(color)
        for c, value in enumerate([u, v, ca, cb, cc] + colors + [opacity]):
            spot = pl.ds(pl.multiple_of(32 * c + 8 * block, 8), 8)
            table_ref[spot, 128 * half : 128 * half + 128] = value

    for half in range(2):
        lax.fori_loop(0, 4, lambda b, unused, half=half: (step(b, half), unused)[1], 0)
    upper, middle, lower = split(table_ref[...], 3)
    out_ref[0:288, :] = upper
    out_ref[288:576, :] = middle
    out_ref[576:736, :] = lower[:160]


def pick_kernel(
    asked_ref, table_ref, image_ref, out_ref, high_ref, low_ref, found_ref, stage_ref
):
    asked = asked_ref[...]
    index = asked.astype(F32).T[:32, :].astype(I32)
    high_ref[...] = (index >> 7) & 31
    low_ref[...] = (index & 127) + 128 * (index >> 12)
    sub_high = iota((32, 256), 0)
    sub_low = iota((256, 256), 0)
    for k in range(0, 32, 2):
        hot = indicator(pair_rows(low_ref, k, 256) == sub_low)
        parts = jnp.dot(table_ref[...], hot, preferred_element_type=F32)
        both = parts[:288] + parts[288:576]
        whole = jnp.concatenate([both[:160] + parts[576:], both[160:]], axis=0)
        match = pair_rows(high_ref, k, 32) == sub_high
        for c in range(9):
            row = jnp.sum(
                jnp.where(match, whole[32 * c : 32 * c + 32], 0.0), axis=0, keepdims=True
            )
            found_ref[32 * c + k : 32 * c + k + 1, :] = row[:, :128]
            found_ref[32 * c + k + 1 : 32 * c + k + 2, :] = row[:, 128:]
    upper, middle, lower = split(found_ref[128:160, :], 3)
    found_ref[320:352, :] = lower.astype(F32)
    found_ref[352:, :] = jnp.zeros((32, 128), F32)
    upper, lower = split(found_ref[256:288, :], 2)
    found_ref[256:288, :] = upper.astype(F32)
    found_ref[288:320, :] = lower.astype(F32)
    truth = jnp.dot(
        indicator(asked[:, 32:33] == iota((128, 16), 1)), image_ref[...],
        preferred_element_type=F32,
    )
    spot = 0
    for i in range(3):
        block = found_ref[128 * i : 128 * (i + 1), :].T
        for part in split(block, 3 - i):
            stage_ref[pl.ds(spot, 128, stride=12), :] = part.astype(F32)
            spot += 1
    for i in range(6):
        stage_ref[pl.ds(6 + i, 128, stride=12), :] = truth[:, 128 * i : 128 * (i + 1)]
    out_ref[...] = stage_ref[...].astype(BF16)


def put_rows(out_ref, found_ref):
    for i in range(3):
        out_ref[pl.ds(i, 128, stride=3), :] = found_ref[128 * i : 128 * (i + 1), :].T


def swap_blocks(value):
    sub = iota((8, 128), 0)
    block = iota((8, 128), 1) >> 4
    for s in (4, 2, 1):
        up = pltpu.roll(pltpu.roll(value, 8 - s, 0), 16 * s, 1)
        down = up if s == 4 else pltpu.roll(pltpu.roll(value, s, 0), 128 - 16 * s, 1)
        sub_bit = sub & s
        block_bit = block & s
        value = jnp.where(
            sub_bit == block_bit, value, jnp.where(sub_bit < block_bit, up, down)
        )
    return value


def loss_and_slopes(images, target):
    loss = jnp.zeros((16, 1), F32)
    slopes = []
    for k in range(3):
        image = images[k]
        wanted = target[:, 256 * k : 256 * (k + 1)]
        difference = image - wanted
        smooth = jnp.sqrt(difference * difference + 0.0001)
        mean_r = jnp.sum(image, axis=1, keepdims=True) / 256.0
        mean_t = jnp.sum(wanted, axis=1, keepdims=True) / 256.0
        centered_r = image - mean_r
        centered_t = wanted - mean_t
        var_r = jnp.sum(centered_r * centered_r, axis=1, keepdims=True) / 256.0
        var_t = jnp.sum(centered_t * centered_t, axis=1, keepdims=True) / 256.0
        cov = jnp.sum(centered_r * centered_t, axis=1, keepdims=True) / 256.0
        top_m = 2.0 * mean_r * mean_t + 0.0001
        top_c = 2.0 * cov + 0.0009
        low_m = mean_r * mean_r + mean_t * mean_t + 0.0001
        low_v = var_r + var_t + 0.0009
        below = 1.0 / (low_m * low_v)
        similarity = top_m * top_c * below
        loss = loss + (0.8 / 3.0) * jnp.sum(smooth, axis=1, keepdims=True)
        loss = loss + (0.2 * 256.0 / 3.0) * (1.0 - similarity)
        by_mean = 2.0 * mean_t * top_c * below - similarity * 2.0 * mean_r / low_m
        by_cov = 2.0 * top_m * below
        by_var = -similarity / low_v
        slopes.append(
            (0.8 / 3.0) * difference / smooth
            - (0.2 / 3.0) * (by_mean + 2.0 * by_var * centered_r + by_cov * centered_t)
        )
    return loss, slopes


def render_kernel(
    arrived_ref, holder_ref, place_ref, tile_ref, prev_ref,
    picture_ref, loss_ref, out_ref, stage_ref,
    ordered_ref, row_ref, dx_ref, alpha_ref, weight_ref, reach_ref, moment_ref, found_ref,
    code_ref, low_ref, part_ref,
):
    code_ref[...] = (place_ref[...] >> 4) * 128 + holder_ref[...]
    low_ref[...] = place_ref[...] & 15
    stage_ref[...] = arrived_ref[...].astype(F32)
    came = [stage_ref[pl.ds(i, 128, stride=12), :] for i in range(12)]
    table = [(came[0] + came[1] + came[2]).T, (came[3] + came[4]).T, came[5].T]
    folded = []
    for c in range(9):
        part = table[c // 4][32 * (c % 4) : 32 * (c % 4) + 32, :]
        if c == 4:
            part = part + table[2][64:96, :]
        if c == 8:
            part = part + table[2][32:64, :]
        folded.append(jnp.concatenate([part[:16], part[16:]], axis=1))
    pieces = jnp.concatenate(split(jnp.concatenate(folded, axis=0), 3), axis=0)
    sub_slot = iota((256, 256), 0)
    sub_place = iota((16, 256), 0)

    def pick(pair, unused):
        t = 2 * pair
        hot = indicator(pair_rows(code_ref, t, 256) == sub_slot)
        parts = jnp.dot(pieces, hot, preferred_element_type=F32)
        whole = parts[:144] + parts[144:288] + parts[288:]
        match = pair_rows(low_ref, t, 16) == sub_place
        for c in range(9):
            row = jnp.sum(
                jnp.where(match, whole[16 * c : 16 * c + 16], 0.0), axis=0, keepdims=True
            )
            ordered_ref[pl.ds(16 * c + t, 1), :] = row[:, :128]
            ordered_ref[pl.ds(16 * c + t + 1, 1), :] = row[:, 128:]
        return unused

    lax.fori_loop(0, 8, pick, 0, unroll=PICK_UNROLL)
    sub = iota((16, 128), 0)
    base_x = jnp.zeros((16, 128), F32)
    base_y = jnp.zeros((16, 128), F32)
    source = jnp.zeros((16, 128), I32)
    for t in range(16):
        number = tile_ref[t]
        tile_row = number // TW
        tile_column = number - tile_row * TW
        base_x = jnp.where(sub == t, (16 * tile_column + 8).astype(F32), base_x)
        base_y = jnp.where(sub == t, (16 * tile_row + 8).astype(F32), base_y)
        source = jnp.where(sub == t, lax.shift_right_logical(prev_ref[t], 4), source)
    ordered_ref[0:16, :] = ordered_ref[0:16, :] - base_x
    ordered_ref[16:32, :] = ordered_ref[16:32, :] - base_y
    ordered_ref[144:, :] = jnp.zeros((112, 128), F32)
    turned = [ordered_ref[0:128, :].T, ordered_ref[128:256, :].T]
    lane = iota((128, 128), 1)
    grid_x = (lane & 15).astype(F32) - 7.5
    for g in range(2):
        owner = (lane >> 4) + 8 * g

        def wide(c):
            return take_lane(turned[c // 8], owner + 16 * (c % 8))

        dx = grid_x - wide(0)
        dx_ref[g] = dx
        row_ref[g, 0] = (-0.5 * LOG2E) * wide(2) * dx * dx
        row_ref[g, 1] = (-LOG2E) * wide(3) * dx
        row_ref[g, 2] = (-0.5 * LOG2E) * wide(4)
        row_ref[g, 3] = wide(1)
        row_ref[g, 4] = wide(8)
        row_ref[g, 5] = wide(5)
        row_ref[g, 6] = wide(6)
        row_ref[g, 7] = wide(7)
    sub8 = iota((8, 128), 0)
    grid_y = [sub8.astype(F32) - 7.5, sub8.astype(F32) + 0.5]
    ones = jnp.ones((8, 128), F32)
    zero = jnp.zeros((8, 128), F32)

    def row_of(g, r, j):
        return spread(row_ref[g, r, pl.ds(j, 1), :], 8)

    def forward(j, state):
        reach = list(state[0])
        sums = list(state[1])
        for g in range(2):
            (part_a, part_b, part_c, gv, go, g0, g1, g2) = [row_of(g, r, j) for r in range(8)]
            for h in range(2):
                n = 2 * g + h
                dy = grid_y[h] - gv
                fall = jnp.exp2(part_a + dy * (part_b + part_c * dy))
                alpha = go * fall
                weight = alpha * reach[n]
                alpha_ref[j, n] = alpha
                weight_ref[j, n] = weight
                reach_ref[j, n] = fall * reach[n]
                reach[n] = reach[n] - weight
                sums[3 * n] = sums[3 * n] + weight * g0
                sums[3 * n + 1] = sums[3 * n + 1] + weight * g1
                sums[3 * n + 2] = sums[3 * n + 2] + weight * g2
        return (tuple(reach), tuple(sums))

    unused, sums = lax.fori_loop(
        0, 128, forward, (tuple([ones] * 4), tuple([zero] * 12)), unroll=FORWARD_UNROLL
    )
    chosen = indicator(source == iota((16, 128), 1))
    target = jnp.concatenate(
        [
            jnp.dot(chosen, came[6 + i].astype(BF16), preferred_element_type=F32)
            for i in range(6)
        ],
        axis=1,
    )
    images = []
    for k in range(3):
        image = jnp.concatenate(
            [
                jnp.concatenate(
                    [swap_blocks(sums[6 * g + k]), swap_blocks(sums[6 * g + 3 + k])], axis=1
                )
                for g in range(2)
            ],
            axis=0,
        )
        picture_ref[:, 256 * k : 256 * (k + 1)] = image
        images.append(image)
    loss, slopes = loss_and_slopes(images, target)
    loss_ref[...] = jnp.broadcast_to(loss, (16, 128))
    slope = [
        [
            swap_blocks(slopes[k][8 * g : 8 * g + 8, 128 * h : 128 * h + 128])
            for k in range(3)
        ]
        for g in range(2)
        for h in range(2)
    ]
    grid_yy = [grid_y[h] * grid_y[h] for h in range(2)]

    def fold(first, second, distance):
        bit = (sub8 & distance) != 0
        if distance == 4:
            return jnp.where(bit, second, first) + pltpu.roll(
                jnp.where(bit, first, second), 4, 0
            )
        return jnp.where(
            bit,
            second + pltpu.roll(second, distance, 0),
            first + pltpu.roll(first, 8 - distance, 0),
        )

    def backward(block, state):
        behind = list(state)
        base = pl.multiple_of(120 - 8 * block, 8)
        for g in range(2):
            waiting = {}
            for s in range(7, -1, -1):
                j = base + s
                (g0, g1, g2) = [row_of(g, r, j) for r in (5, 6, 7)]
                pulls = []
                shares = []
                for h in range(2):
                    n = 2 * g + h
                    value = slope[n][0] * g0 + slope[n][1] * g1 + slope[n][2] * g2
                    gap = value - behind[n]
                    pulls.append(reach_ref[j, n] * gap)
                    behind[n] = behind[n] + alpha_ref[j, n] * gap
                    weight = weight_ref[j, n]
                    shares.append([weight * slope[n][k] for k in range(3)])
                found = [
                    pulls[0] + pulls[1],
                    pulls[0] * grid_y[0] + pulls[1] * grid_y[1],
                    pulls[0] * grid_yy[0] + pulls[1] * grid_yy[1],
                    shares[0][0] + shares[1][0],
                    shares[0][1] + shares[1][1],
                    shares[0][2] + shares[1][2],
                ]
                spot = s
                for distance in (1, 2, 4):
                    if spot & distance:
                        break
                    above = waiting.pop((distance, spot + distance))
                    found = [fold(a, b, distance) for a, b in zip(found, above)]
                    if distance == 4:
                        for q in range(6):
                            moment_ref[g, q, pl.ds(base, 8), :] = found[q]
                else:
                    continue
                waiting[(distance, spot)] = found
        return tuple(behind)

    lax.fori_loop(0, 16, backward, tuple([zero] * 4))
    totals = jnp.zeros((16, 1152), F32)
    for g in range(2):
        dx = dx_ref[g]
        gv = row_ref[g, 3]
        m0 = moment_ref[g, 0]
        m1 = moment_ref[g, 1]
        sx = dx * m0
        sy = m1 - gv * m0
        syy = moment_ref[g, 2] - gv * (m1 + sy)
        stack = jnp.concatenate(
            [m0, sx, sy, dx * sx, dx * sy, syy]
            + [moment_ref[g, q] for q in range(3, 6)],
            axis=0,
        )
        tile = iota((16, 256), 0)
        pick = indicator(tile == ((iota((16, 256), 1) >> 4) & 7) + 8 * g)
        totals = totals + contract_lanes(pick, jnp.concatenate(split(stack, 2), axis=1))
    (m0, sx, sy, sxx, sxy, syy, d_red, d_green, d_blue) = [
        totals[:, 128 * c : 128 * c + 128] for c in range(9)
    ]
    (ca, cb, cc) = [ordered_ref[16 * c : 16 * c + 16, :] for c in (2, 3, 4)]
    opacity = ordered_ref[128:144, :]
    results = [
        opacity * (ca * sx + cb * sy),
        opacity * (cb * sx + cc * sy),
        -0.5 * opacity * sxx,
        -opacity * sxy,
        -0.5 * opacity * syy,
        d_red,
        d_green,
        d_blue,
        m0,
    ]
    for c, result in enumerate(results):
        for p, part in enumerate(split(result, 2)):
            part_ref[p, 16 * c : 16 * c + 16, :] = part.astype(F32)
    sub_k = iota((32, 128), 0)
    sub_h = iota((128, 128), 0)

    def give(pair, total):
        hot = []
        left = [[], []]
        for n in range(2):
            tile = 2 * pair + n
            hot.append(indicator(spread(holder_ref[pl.ds(tile, 1), :], 128) == sub_h))
            match = spread(place_ref[pl.ds(tile, 1), :], 32) == sub_k
            for p in range(2):
                left[p].append(
                    jnp.concatenate(
                        [
                            jnp.where(match, part_ref[p, pl.ds(16 * c + tile, 1), :], 0.0)
                            for c in range(9)
                        ],
                        axis=0,
                    ).astype(BF16)
                )
        hot = jnp.concatenate(hot, axis=1)
        for p in range(2):
            total = total + contract_lanes(jnp.concatenate(left[p], axis=1), hot)
        return total

    total = lax.fori_loop(0, 8, give, jnp.zeros((288, 128), F32), unroll=GIVE_UNROLL)
    found_ref[0:288, :] = total
    found_ref[288:, :] = jnp.zeros((96, 128), F32)
    put_rows(out_ref, found_ref)


def update_kernel(
    returned_ref, asked_ref, params_ref, out_hbm,
    high_ref, low_ref, piece_ref, sum_ref, out_ref, sems,
):
    index = asked_ref[...].astype(F32).T[:32, :].astype(I32)
    high_ref[...] = (index >> 7) & 31
    low_ref[...] = (index & 127) + 128 * (index >> 12)
    for i in range(3):
        block = returned_ref[pl.ds(i, 128, stride=3), :].T
        rows = 128 if i < 2 else 32
        block = block[:rows, :]
        upper = block.astype(BF16).astype(F32)
        piece_ref[0, 128 * i : 128 * i + rows, :] = upper
        piece_ref[1, 128 * i : 128 * i + rows, :] = block - upper
    sub_high = iota((32, 128), 0)
    sub_low = iota((256, 256), 0)

    def scatter(pair, total):
        k = 2 * pair
        left = [[], []]
        for n in (k, k + 1):
            match = spread(high_ref[pl.ds(n, 1), :], 32) == sub_high
            for p in range(2):
                left[p].append(
                    jnp.concatenate(
                        [
                            jnp.where(match, piece_ref[p, pl.ds(32 * c + n, 1), :], 0.0)
                            for c in range(9)
                        ],
                        axis=0,
                    ).astype(BF16)
                )
        hot = indicator(pair_rows(low_ref, k, 256) == sub_low)
        for p in range(2):
            total = total + contract_lanes(jnp.concatenate(left[p], axis=1), hot)
        return total

    total = lax.fori_loop(0, 16, scatter, jnp.zeros((288, 256), F32), unroll=SCATTER_UNROLL)
    sum_ref[0] = total[:, :128]
    sum_ref[1] = total[:, 128:]
    early = iota((8, 128), 0) < 3

    def leave(block):
        span = pl.ds(pl.multiple_of(block * 1024, 1024), 1024)
        return pltpu.make_async_copy(out_ref.at[:, span], out_hbm.at[:, span], sems.at[block])

    def pull(place, half):
        block = place + 4 * half
        start = pl.multiple_of(block * 1024, 1024)
        values = params_ref[:, pl.ds(start, 1024)].reshape(59, 8, 128)
        p = [values[i] for i in range(59)]
        g = [
            sum_ref[half, pl.ds(pl.multiple_of(32 * c + 8 * place, 8), 8), :] for c in range(9)
        ]
        unused_conic, pull_conic = jax.vjp(conic, *p[:10])
        unit, pull_unit = jax.vjp(direction, *p[:3])
        basis, pull_basis = jax.vjp(lambda *d: tuple(harmonics(*d)), *unit)
        d_basis = tuple(
            g[5] * p[11 + i] + g[6] * p[27 + i] + g[7] * p[43 + i] for i in range(16)
        )
        first = list(pull_conic((g[2], g[3], g[4])))
        for i, slope in enumerate(pull_unit(pull_basis(d_basis))):
            first[i] = first[i] + slope
        focal_z = FOCAL / p[2]
        opacity = lax.logistic(p[10])
        first[0] = first[0] + g[0] * focal_z
        first[1] = first[1] + g[1] * focal_z
        first[2] = first[2] - focal_z * ((g[0] * p[0] + g[1] * p[1]) / p[2])
        first.append(g[8] * (opacity * (1.0 - opacity)))
        blank = jnp.zeros((8, 128), F32)

        def turn(rows):
            return jnp.stack(rows, axis=0).reshape(8, 1024)

        out_ref[0:8, pl.ds(start, 1024)] = turn(first[:8])
        rest = turn(first[8:] + [blank] * 5)
        ends_all = turn([basis[i] for i in (13, 14, 15, 0, 1, 2, 3, 4)])
        middle_all = turn([basis[i] for i in range(5, 13)])
        for s in range(8):
            column = pl.ds(pl.multiple_of(start + 128 * s, 128), 128)
            ends = ends_all[:, 128 * s : 128 * s + 128]
            middle = middle_all[:, 128 * s : 128 * s + 128]
            (red, green, blue) = [
                spread(sum_ref[half, pl.ds(32 * c + 8 * place + s, 1), :], 8) for c in (5, 6, 7)
            ]
            out_ref[8:16, column] = jnp.where(early, rest[:, 128 * s : 128 * s + 128], ends * red)
            out_ref[16:24, column] = middle * red
            out_ref[24:32, column] = ends * jnp.where(early, red, green)
            out_ref[32:40, column] = middle * green
            out_ref[40:48, column] = ends * jnp.where(early, green, blue)
            out_ref[48:56, column] = middle * blue
            out_ref[56:59, column] = (ends * blue)[:3]
        leave(block).start()

    for half in range(2):
        lax.fori_loop(0, 4, lambda b, unused, half=half: (pull(b, half), unused)[1], 0)
    for block in range(8):
        leave(block).wait()


def vmem():
    return pl.BlockSpec(memory_space=pltpu.VMEM)


def smem():
    return pl.BlockSpec(memory_space=pltpu.SMEM)


def anywhere():
    return pl.BlockSpec(memory_space=pl.ANY)


def shape(dims, dtype=F32):
    return jax.ShapeDtypeStruct(dims, dtype)


PICK_UNROLL = 4
FORWARD_UNROLL = 4
SCATTER_UNROLL = 16
GIVE_UNROLL = 4
WIDE = pltpu.CompilerParams(vmem_limit_bytes=58 * 1024 * 1024)
ROOM = pltpu.CompilerParams(vmem_limit_bytes=40 * 1024 * 1024)


def swap(values):
    return lax.all_to_all(values, "dev", split_axis=0, concat_axis=0, tiled=True)


def body(
    params, entry_shard, entry_row, depth_order, live_count, tile_of_slot, prev_slot, gt_image
):
    request, holder, place = pl.pallas_call(
        route_kernel,
        out_shape=(shape((128, 128), I32), shape((16, 128), I32), shape((16, 128), I32)),
        in_specs=[anywhere()] * 5,
        out_specs=(vmem(),) * 3,
        scratch_shapes=[pltpu.VMEM((16, 128), I32)] * 3
        + [pltpu.SMEM((16,), I32)] * 2
        + [pltpu.SemaphoreType.DMA((5,))],
        compiler_params=WIDE,
        name="route",
    )(entry_shard, entry_row, depth_order, live_count, prev_slot)
    asked = swap(request)
    table = pl.pallas_call(
        project_kernel,
        out_shape=shape((736, 256), BF16),
        in_specs=[vmem()],
        out_specs=vmem(),
        scratch_shapes=[pltpu.VMEM((288, 256), F32)],
        compiler_params=ROOM,
        cost_estimate=pl.CostEstimate(
            flops=20_000_000, bytes_accessed=20_000_000, transcendentals=100_000
        ),
        name="project",
    )(params)
    picked = pl.pallas_call(
        pick_kernel,
        out_shape=shape((1536, 128), BF16),
        in_specs=[vmem(), vmem(), vmem()],
        out_specs=vmem(),
        scratch_shapes=[
            pltpu.VMEM((32, 128), I32),
            pltpu.VMEM((32, 128), I32),
            pltpu.VMEM((384, 128), F32),
            pltpu.VMEM((1536, 128), F32),
        ],
        compiler_params=ROOM,
        name="pick",
    )(asked, table, gt_image)
    arrived = swap(picked.reshape(128, 3, 4, 128)).reshape(1536, 128)
    picture, loss, outgoing = pl.pallas_call(
        render_kernel,
        out_shape=(shape((16, 768)), shape((16, 128)), shape((384, 128))),
        in_specs=[vmem()] * 3 + [smem(), smem()],
        out_specs=(vmem(),) * 3,
        scratch_shapes=[
            pltpu.VMEM((1536, 128), F32),
            pltpu.VMEM((256, 128), F32),
            pltpu.VMEM((2, 8, 128, 128), F32),
            pltpu.VMEM((2, 128, 128), F32),
            pltpu.VMEM((128, 4, 8, 128), F32),
            pltpu.VMEM((128, 4, 8, 128), F32),
            pltpu.VMEM((128, 4, 8, 128), F32),
            pltpu.VMEM((2, 6, 128, 128), F32),
            pltpu.VMEM((384, 128), F32),
            pltpu.VMEM((16, 128), I32),
            pltpu.VMEM((16, 128), I32),
            pltpu.VMEM((2, 144, 128), F32),
        ],
        compiler_params=ROOM,
        name="render",
    )(arrived, holder, place, tile_of_slot, prev_slot)
    returned = swap(outgoing.reshape(128, 1, 384)).reshape(384, 128)
    gradients = pl.pallas_call(
        update_kernel,
        out_shape=shape((59, 8192)),
        in_specs=[vmem(), vmem(), vmem()],
        out_specs=anywhere(),
        scratch_shapes=[
            pltpu.VMEM((32, 128), I32),
            pltpu.VMEM((32, 128), I32),
            pltpu.VMEM((2, 288, 128), F32),
            pltpu.VMEM((2, 288, 128), F32),
            pltpu.VMEM((59, 8192), F32),
            pltpu.SemaphoreType.DMA((8,)),
        ],
        compiler_params=ROOM,
        name="update",
    )(returned, asked, params)
    return (gradients, picture, loss[:, 0])


def solution(mesh):
    return jax.shard_map(
        body,
        mesh=mesh,
        in_specs=(
            P(None, "dev"),
            P("dev", None),
            P("dev", None),
            P("dev", None),
            P("dev"),
            P("dev"),
            P("dev"),
            P("dev", None),
        ),
        out_specs=(P(None, "dev"), P("dev", None), P("dev")),
        check_vma=False,
    )
```

```python
import jax
import jax.numpy as jnp
from jax import lax
from jax.experimental import pallas as pl
from jax.experimental.pallas import tpu as pltpu
from jax.sharding import PartitionSpec as P

TW = 240
TH = 135
FOCAL = 1200.0
LOG2E = 1.4426950408889634
F32 = jnp.float32
BF16 = jnp.bfloat16
I32 = jnp.int32


def iota(shape, axis):
    return lax.broadcasted_iota(I32, shape, axis)


def take_lane(table, index):
    return jnp.take_along_axis(table, index, axis=1, mode="promise_in_bounds")


def conic(pos_x, pos_y, depth, ls0, ls1, ls2, q0, q1, q2, q3):
    scales = [jnp.exp(ls0), jnp.exp(ls1), jnp.exp(ls2)]
    inverse_q = lax.rsqrt(q0 * q0 + q1 * q1 + q2 * q2 + q3 * q3)
    w_part = q0 * inverse_q
    x_part = q1 * inverse_q
    y_part = q2 * inverse_q
    z_part = q3 * inverse_q
    rotation = [
        [
            1.0 - 2.0 * (y_part * y_part + z_part * z_part),
            2.0 * (x_part * y_part - w_part * z_part),
            2.0 * (x_part * z_part + w_part * y_part),
        ],
        [
            2.0 * (x_part * y_part + w_part * z_part),
            1.0 - 2.0 * (x_part * x_part + z_part * z_part),
            2.0 * (y_part * z_part - w_part * x_part),
        ],
        [
            2.0 * (x_part * z_part - w_part * y_part),
            2.0 * (y_part * z_part + w_part * x_part),
            1.0 - 2.0 * (x_part * x_part + y_part * y_part),
        ],
    ]
    inverse_z = 1.0 / depth
    focal_z = FOCAL * inverse_z
    ratio_x = pos_x * inverse_z
    ratio_y = pos_y * inverse_z
    slope_x = -focal_z * ratio_x
    slope_y = -focal_z * ratio_y
    first = [(focal_z * rotation[0][i] + slope_x * rotation[2][i]) * scales[i] for i in range(3)]
    second = [(focal_z * rotation[1][i] + slope_y * rotation[2][i]) * scales[i] for i in range(3)]
    spread_xx = first[0] * first[0] + first[1] * first[1] + first[2] * first[2] + 0.3
    spread_xy = first[0] * second[0] + first[1] * second[1] + first[2] * second[2]
    spread_yy = second[0] * second[0] + second[1] * second[1] + second[2] * second[2] + 0.3
    inverse_det = 1.0 / (spread_xx * spread_yy - spread_xy * spread_xy)
    return (spread_yy * inverse_det, -spread_xy * inverse_det, spread_xx * inverse_det)


def direction(pos_x, pos_y, depth):
    inverse_norm = lax.rsqrt(pos_x * pos_x + pos_y * pos_y + depth * depth)
    return (pos_x * inverse_norm, pos_y * inverse_norm, depth * inverse_norm)


def harmonics(unit_x, unit_y, unit_z):
    square_x = unit_x * unit_x
    square_y = unit_y * unit_y
    square_z = unit_z * unit_z
    return [
        0.28209479177387814 * jnp.ones_like(unit_x),
        -0.4886025119029199 * unit_y,
        0.4886025119029199 * unit_z,
        -0.4886025119029199 * unit_x,
        1.0925484305920792 * unit_x * unit_y,
        -1.0925484305920792 * unit_y * unit_z,
        0.31539156525252005 * (2.0 * square_z - square_x - square_y),
        -1.0925484305920792 * unit_x * unit_z,
        0.5462742152960396 * (square_x - square_y),
        -0.5900435899266435 * unit_y * (3.0 * square_x - square_y),
        2.890611442640554 * unit_x * unit_y * unit_z,
        -0.4570457994644658 * unit_y * (4.0 * square_z - square_x - square_y),
        0.3731763325901154 * unit_z * (2.0 * square_z - 3.0 * square_x - 3.0 * square_y),
        -0.4570457994644658 * unit_x * (4.0 * square_z - square_x - square_y),
        1.445305721320277 * unit_z * (square_x - square_y),
        -0.5900435899266435 * unit_x * (square_x - 3.0 * square_y),
    ]


def split(value, pieces):
    parts = []
    for _ in range(pieces - 1):
        part = value.astype(BF16)
        parts.append(part)
        value = value - part.astype(F32)
    parts.append(value.astype(BF16))
    return parts


def contract_lanes(left, right):
    return lax.dot_general(left, right, (((1,), (1,)), ((), ())), preferred_element_type=F32)


def indicator(condition):
    return jnp.where(condition, 1.0, 0.0).astype(BF16)


def spread(row, count):
    return jnp.broadcast_to(row, (count, row.shape[1]))


def pair_rows(ref, row, count):
    return jnp.concatenate(
        [spread(ref[pl.ds(row + n, 1), :], count) for n in range(2)], axis=1
    )


def route_kernel(
    shard_hbm, row_hbm, order_hbm, live_hbm, prev_hbm, request_ref, holder_ref, place_ref,
    shard_ref, row_ref, order_ref, live_ref, prev_ref, sems,
):
    tiles, length = shard_ref.shape
    copies = [
        pltpu.make_async_copy(source, target, sems.at[n])
        for n, (source, target) in enumerate(
            [
                (order_hbm, order_ref),
                (shard_hbm, shard_ref),
                (row_hbm, row_ref),
                (live_hbm, live_ref),
                (prev_hbm, prev_ref),
            ]
        )
    ]
    for copy in copies:
        copy.start()
    for copy in copies:
        copy.wait()
    order = order_ref[...]
    shards = take_lane(shard_ref[...], order)
    rows = take_lane(row_ref[...], order)
    sub = iota((128, 128), 0)
    lane = iota((128, 128), 1)
    wide_row = iota((128, 256), 0)
    wide_lane = iota((128, 256), 1)
    counter = indicator((wide_lane >= 128) | (wide_row < wide_lane))
    sub_k = iota((32, 128), 0)
    carry = jnp.zeros((128, 128), F32)
    request = jnp.zeros((128, 32), F32)
    truth = jnp.zeros((128, 128), I32)
    for t in range(tiles):
        live = order[t : t + 1, :] < live_ref[t]
        holder = jnp.where(live, shards[t : t + 1, :], -1)
        match = spread(holder, 128) == sub
        hot = indicator(match)
        counted = jnp.dot(hot, counter, preferred_element_type=F32)
        place = jnp.sum(
            jnp.where(match, counted[:, :128] + carry, 0.0), axis=0, keepdims=True
        ).astype(I32)
        carry = carry + counted[:, 128:]
        holder_ref[t : t + 1, :] = holder
        place_ref[t : t + 1, :] = jnp.where(live, place, -1)
        match_k = spread(place, 32) == sub_k
        row = rows[t : t + 1, :]
        high = jnp.where(match_k, ((row >> 7) * 128).astype(F32), 0.0)
        low = jnp.where(match_k, (row & 127).astype(F32), 0.0)
        asked = jnp.concatenate([high, low], axis=1).astype(BF16)
        request = request + contract_lanes(jnp.concatenate([hot, hot], axis=1), asked)
        previous = prev_ref[t]
        truth = jnp.where(sub == lax.shift_right_logical(previous, 4), previous & 15, truth)
    wide = jnp.concatenate([request.astype(I32), jnp.zeros((128, 96), I32)], axis=1)
    request_ref[...] = jnp.where(lane == 32, truth, wide)


def project_kernel(params_ref, out_ref, table_ref):
    def step(block, half):
        start = pl.multiple_of(half * 4096 + block * 1024, 1024)
        values = params_ref[:, pl.ds(start, 1024)].reshape(59, 8, 128)
        p = [values[i] for i in range(59)]
        (ca, cb, cc) = conic(*p[:10])
        u = FOCAL * p[0] / p[2] + 8.0 * TW
        v = FOCAL * p[1] / p[2] + 8.0 * TH
        opacity = lax.logistic(p[10])
        basis = harmonics(*direction(*p[:3]))
        colors = []
        for channel in range(3):
            color = 0.5 + basis[0] * p[11 + 16 * channel]
            for degree in range(1, 16):
                color = color + basis[degree] * p[11 + 16 * channel + degree]
            colors.append(color)
        for c, value in enumerate([u, v, ca, cb, cc] + colors + [opacity]):
            spot = pl.ds(pl.multiple_of(32 * c + 8 * block, 8), 8)
            table_ref[spot, 128 * half : 128 * half + 128] = value

    for half in range(2):
        lax.fori_loop(0, 4, lambda b, unused, half=half: (step(b, half), unused)[1], 0)
    upper, middle, lower = split(table_ref[...], 3)
    out_ref[0:288, :] = upper
    out_ref[288:576, :] = middle
    out_ref[576:736, :] = lower[:160]


def pick_kernel(
    asked_ref, table_ref, image_ref, out_ref, high_ref, low_ref, found_ref, stage_ref
):
    asked = asked_ref[...]
    index = asked.astype(F32).T[:32, :].astype(I32)
    high_ref[...] = (index >> 7) & 31
    low_ref[...] = (index & 127) + 128 * (index >> 12)
    sub_high = iota((32, 256), 0)
    sub_low = iota((256, 256), 0)
    for k in range(0, 32, 2):
        hot = indicator(pair_rows(low_ref, k, 256) == sub_low)
        parts = jnp.dot(table_ref[...], hot, preferred_element_type=F32)
        both = parts[:288] + parts[288:576]
        whole = jnp.concatenate([both[:160] + parts[576:], both[160:]], axis=0)
        match = pair_rows(high_ref, k, 32) == sub_high
        for c in range(9):
            row = jnp.sum(
                jnp.where(match, whole[32 * c : 32 * c + 32], 0.0), axis=0, keepdims=True
            )
            found_ref[32 * c + k : 32 * c + k + 1, :] = row[:, :128]
            found_ref[32 * c + k + 1 : 32 * c + k + 2, :] = row[:, 128:]
    upper, middle, lower = split(found_ref[128:160, :], 3)
    found_ref[320:352, :] = lower.astype(F32)
    found_ref[352:, :] = jnp.zeros((32, 128), F32)
    upper, lower = split(found_ref[256:288, :], 2)
    found_ref[256:288, :] = upper.astype(F32)
    found_ref[288:320, :] = lower.astype(F32)
    truth = jnp.dot(
        indicator(asked[:, 32:33] == iota((128, 16), 1)), image_ref[...],
        preferred_element_type=F32,
    )
    spot = 0
    for i in range(3):
        block = found_ref[128 * i : 128 * (i + 1), :].T
        for part in split(block, 3 - i):
            stage_ref[pl.ds(spot, 128, stride=12), :] = part.astype(F32)
            spot += 1
    for i in range(6):
        stage_ref[pl.ds(6 + i, 128, stride=12), :] = truth[:, 128 * i : 128 * (i + 1)]
    out_ref[...] = stage_ref[...].astype(BF16)


def put_rows(out_ref, found_ref):
    for i in range(3):
        out_ref[pl.ds(i, 128, stride=3), :] = found_ref[128 * i : 128 * (i + 1), :].T


def swap_blocks(value):
    sub = iota((8, 128), 0)
    block = iota((8, 128), 1) >> 4
    for s in (4, 2, 1):
        up = pltpu.roll(pltpu.roll(value, 8 - s, 0), 16 * s, 1)
        down = up if s == 4 else pltpu.roll(pltpu.roll(value, s, 0), 128 - 16 * s, 1)
        sub_bit = sub & s
        block_bit = block & s
        value = jnp.where(
            sub_bit == block_bit, value, jnp.where(sub_bit < block_bit, up, down)
        )
    return value


def loss_and_slopes(images, target):
    loss = jnp.zeros((16, 1), F32)
    slopes = []
    for k in range(3):
        image = images[k]
        wanted = target[:, 256 * k : 256 * (k + 1)]
        difference = image - wanted
        smooth = jnp.sqrt(difference * difference + 0.0001)
        mean_r = jnp.sum(image, axis=1, keepdims=True) / 256.0
        mean_t = jnp.sum(wanted, axis=1, keepdims=True) / 256.0
        centered_r = image - mean_r
        centered_t = wanted - mean_t
        var_r = jnp.sum(centered_r * centered_r, axis=1, keepdims=True) / 256.0
        var_t = jnp.sum(centered_t * centered_t, axis=1, keepdims=True) / 256.0
        cov = jnp.sum(centered_r * centered_t, axis=1, keepdims=True) / 256.0
        top_m = 2.0 * mean_r * mean_t + 0.0001
        top_c = 2.0 * cov + 0.0009
        low_m = mean_r * mean_r + mean_t * mean_t + 0.0001
        low_v = var_r + var_t + 0.0009
        below = 1.0 / (low_m * low_v)
        similarity = top_m * top_c * below
        loss = loss + (0.8 / 3.0) * jnp.sum(smooth, axis=1, keepdims=True)
        loss = loss + (0.2 * 256.0 / 3.0) * (1.0 - similarity)
        by_mean = 2.0 * mean_t * top_c * below - similarity * 2.0 * mean_r / low_m
        by_cov = 2.0 * top_m * below
        by_var = -similarity / low_v
        slopes.append(
            (0.8 / 3.0) * difference / smooth
            - (0.2 / 3.0) * (by_mean + 2.0 * by_var * centered_r + by_cov * centered_t)
        )
    return loss, slopes


def render_kernel(
    arrived_ref, holder_ref, place_ref, tile_ref, prev_ref,
    picture_hbm, loss_ref, out_ref, picture_ref, picture_sem, stage_ref,
    ordered_ref, row_ref, dx_ref, alpha_ref, weight_ref, reach_ref, moment_ref, found_ref,
    code_ref, low_ref, part_ref,
):
    code_ref[...] = (place_ref[...] >> 4) * 128 + holder_ref[...]
    low_ref[...] = place_ref[...] & 15
    stage_ref[...] = arrived_ref[...].astype(F32)
    came = [stage_ref[pl.ds(i, 128, stride=12), :] for i in range(12)]
    table = [(came[0] + came[1] + came[2]).T, (came[3] + came[4]).T, came[5].T]
    folded = []
    for c in range(9):
        part = table[c // 4][32 * (c % 4) : 32 * (c % 4) + 32, :]
        if c == 4:
            part = part + table[2][64:96, :]
        if c == 8:
            part = part + table[2][32:64, :]
        folded.append(jnp.concatenate([part[:16], part[16:]], axis=1))
    pieces = jnp.concatenate(split(jnp.concatenate(folded, axis=0), 3), axis=0)
    sub_slot = iota((256, 256), 0)
    sub_place = iota((16, 256), 0)

    def pick(pair, unused):
        t = 2 * pair
        hot = indicator(pair_rows(code_ref, t, 256) == sub_slot)
        parts = jnp.dot(pieces, hot, preferred_element_type=F32)
        whole = parts[:144] + parts[144:288] + parts[288:]
        match = pair_rows(low_ref, t, 16) == sub_place
        for c in range(9):
            row = jnp.sum(
                jnp.where(match, whole[16 * c : 16 * c + 16], 0.0), axis=0, keepdims=True
            )
            ordered_ref[pl.ds(16 * c + t, 1), :] = row[:, :128]
            ordered_ref[pl.ds(16 * c + t + 1, 1), :] = row[:, 128:]
        return unused

    lax.fori_loop(0, 8, pick, 0, unroll=PICK_UNROLL)
    sub = iota((16, 128), 0)
    base_x = jnp.zeros((16, 128), F32)
    base_y = jnp.zeros((16, 128), F32)
    source = jnp.zeros((16, 128), I32)
    for t in range(16):
        number = tile_ref[t]
        tile_row = number // TW
        tile_column = number - tile_row * TW
        base_x = jnp.where(sub == t, (16 * tile_column + 8).astype(F32), base_x)
        base_y = jnp.where(sub == t, (16 * tile_row + 8).astype(F32), base_y)
        source = jnp.where(sub == t, lax.shift_right_logical(prev_ref[t], 4), source)
    ordered_ref[0:16, :] = ordered_ref[0:16, :] - base_x
    ordered_ref[16:32, :] = ordered_ref[16:32, :] - base_y
    ordered_ref[144:, :] = jnp.zeros((112, 128), F32)
    turned = [ordered_ref[0:128, :].T, ordered_ref[128:256, :].T]
    lane = iota((128, 128), 1)
    grid_x = (lane & 15).astype(F32) - 7.5
    for g in range(2):
        owner = (lane >> 4) + 8 * g

        def wide(c):
            return take_lane(turned[c // 8], owner + 16 * (c % 8))

        dx = grid_x - wide(0)
        dx_ref[g] = dx
        row_ref[g, 0] = (-0.5 * LOG2E) * wide(2) * dx * dx
        row_ref[g, 1] = (-LOG2E) * wide(3) * dx
        row_ref[g, 2] = (-0.5 * LOG2E) * wide(4)
        row_ref[g, 3] = wide(1)
        row_ref[g, 4] = wide(8)
        row_ref[g, 5] = wide(5)
        row_ref[g, 6] = wide(6)
        row_ref[g, 7] = wide(7)
    sub8 = iota((8, 128), 0)
    grid_y = [sub8.astype(F32) - 7.5, sub8.astype(F32) + 0.5]
    ones = jnp.ones((8, 128), F32)
    zero = jnp.zeros((8, 128), F32)

    def row_of(g, r, j):
        return spread(row_ref[g, r, pl.ds(j, 1), :], 8)

    def forward(j, state):
        reach = list(state[0])
        sums = list(state[1])
        for g in range(2):
            (part_a, part_b, part_c, gv, go, g0, g1, g2) = [row_of(g, r, j) for r in range(8)]
            for h in range(2):
                n = 2 * g + h
                dy = grid_y[h] - gv
                fall = jnp.exp2(part_a + dy * (part_b + part_c * dy))
                alpha = go * fall
                weight = alpha * reach[n]
                alpha_ref[j, n] = alpha
                weight_ref[j, n] = weight
                reach_ref[j, n] = fall * reach[n]
                reach[n] = reach[n] - weight
                sums[3 * n] = sums[3 * n] + weight * g0
                sums[3 * n + 1] = sums[3 * n + 1] + weight * g1
                sums[3 * n + 2] = sums[3 * n + 2] + weight * g2
        return (tuple(reach), tuple(sums))

    unused, sums = lax.fori_loop(
        0, 128, forward, (tuple([ones] * 4), tuple([zero] * 12)), unroll=FORWARD_UNROLL
    )
    chosen = indicator(source == iota((16, 128), 1))
    target = jnp.concatenate(
        [
            jnp.dot(chosen, came[6 + i].astype(BF16), preferred_element_type=F32)
            for i in range(6)
        ],
        axis=1,
    )
    images = []
    for k in range(3):
        image = jnp.concatenate(
            [
                jnp.concatenate(
                    [swap_blocks(sums[6 * g + k]), swap_blocks(sums[6 * g + 3 + k])], axis=1
                )
                for g in range(2)
            ],
            axis=0,
        )
        picture_ref[:, 256 * k : 256 * (k + 1)] = image
        images.append(image)
    picture_copy = pltpu.make_async_copy(picture_ref, picture_hbm, picture_sem)
    picture_copy.start()
    loss, slopes = loss_and_slopes(images, target)
    loss_ref[...] = jnp.broadcast_to(loss, (16, 128))
    slope = [
        [
            swap_blocks(slopes[k][8 * g : 8 * g + 8, 128 * h : 128 * h + 128])
            for k in range(3)
        ]
        for g in range(2)
        for h in range(2)
    ]
    grid_yy = [grid_y[h] * grid_y[h] for h in range(2)]

    def fold(first, second, distance):
        bit = (sub8 & distance) != 0
        if distance == 4:
            return jnp.where(bit, second, first) + pltpu.roll(
                jnp.where(bit, first, second), 4, 0
            )
        return jnp.where(
            bit,
            second + pltpu.roll(second, distance, 0),
            first + pltpu.roll(first, 8 - distance, 0),
        )

    def backward(block, state):
        behind = list(state)
        base = pl.multiple_of(120 - 8 * block, 8)
        for g in range(2):
            waiting = {}
            for s in range(7, -1, -1):
                j = base + s
                (g0, g1, g2) = [row_of(g, r, j) for r in (5, 6, 7)]
                pulls = []
                shares = []
                for h in range(2):
                    n = 2 * g + h
                    value = slope[n][0] * g0 + slope[n][1] * g1 + slope[n][2] * g2
                    gap = value - behind[n]
                    pulls.append(reach_ref[j, n] * gap)
                    behind[n] = behind[n] + alpha_ref[j, n] * gap
                    weight = weight_ref[j, n]
                    shares.append([weight * slope[n][k] for k in range(3)])
                found = [
                    pulls[0] + pulls[1],
                    pulls[0] * grid_y[0] + pulls[1] * grid_y[1],
                    pulls[0] * grid_yy[0] + pulls[1] * grid_yy[1],
                    shares[0][0] + shares[1][0],
                    shares[0][1] + shares[1][1],
                    shares[0][2] + shares[1][2],
                ]
                spot = s
                for distance in (1, 2, 4):
                    if spot & distance:
                        break
                    above = waiting.pop((distance, spot + distance))
                    found = [fold(a, b, distance) for a, b in zip(found, above)]
                    if distance == 4:
                        for q in range(6):
                            moment_ref[g, q, pl.ds(base, 8), :] = found[q]
                else:
                    continue
                waiting[(distance, spot)] = found
        return tuple(behind)

    lax.fori_loop(0, 16, backward, tuple([zero] * 4))
    totals = jnp.zeros((16, 1152), F32)
    for g in range(2):
        dx = dx_ref[g]
        gv = row_ref[g, 3]
        m0 = moment_ref[g, 0]
        m1 = moment_ref[g, 1]
        sx = dx * m0
        sy = m1 - gv * m0
        syy = moment_ref[g, 2] - gv * (m1 + sy)
        stack = jnp.concatenate(
            [m0, sx, sy, dx * sx, dx * sy, syy]
            + [moment_ref[g, q] for q in range(3, 6)],
            axis=0,
        )
        tile = iota((16, 256), 0)
        pick = indicator(tile == ((iota((16, 256), 1) >> 4) & 7) + 8 * g)
        totals = totals + contract_lanes(pick, jnp.concatenate(split(stack, 2), axis=1))
    (m0, sx, sy, sxx, sxy, syy, d_red, d_green, d_blue) = [
        totals[:, 128 * c : 128 * c + 128] for c in range(9)
    ]
    (ca, cb, cc) = [ordered_ref[16 * c : 16 * c + 16, :] for c in (2, 3, 4)]
    opacity = ordered_ref[128:144, :]
    results = [
        opacity * (ca * sx + cb * sy),
        opacity * (cb * sx + cc * sy),
        -0.5 * opacity * sxx,
        -opacity * sxy,
        -0.5 * opacity * syy,
        d_red,
        d_green,
        d_blue,
        m0,
    ]
    for c, result in enumerate(results):
        for p, part in enumerate(split(result, 2)):
            part_ref[p, 16 * c : 16 * c + 16, :] = part.astype(F32)
    sub_k = iota((32, 128), 0)
    sub_h = iota((128, 128), 0)

    def give(pair, total):
        hot = []
        left = [[], []]
        for n in range(2):
            tile = 2 * pair + n
            hot.append(indicator(spread(holder_ref[pl.ds(tile, 1), :], 128) == sub_h))
            match = spread(place_ref[pl.ds(tile, 1), :], 32) == sub_k
            for p in range(2):
                left[p].append(
                    jnp.concatenate(
                        [
                            jnp.where(match, part_ref[p, pl.ds(16 * c + tile, 1), :], 0.0)
                            for c in range(9)
                        ],
                        axis=0,
                    ).astype(BF16)
                )
        hot = jnp.concatenate(hot, axis=1)
        for p in range(2):
            total = total + contract_lanes(jnp.concatenate(left[p], axis=1), hot)
        return total

    total = lax.fori_loop(0, 8, give, jnp.zeros((288, 128), F32), unroll=GIVE_UNROLL)
    found_ref[0:288, :] = total
    found_ref[288:, :] = jnp.zeros((96, 128), F32)
    put_rows(out_ref, found_ref)
    picture_copy.wait()


def update_kernel(
    returned_ref, asked_ref, params_ref, out_hbm,
    high_ref, low_ref, piece_ref, sum_ref, out_ref, sems,
):
    index = asked_ref[...].astype(F32).T[:32, :].astype(I32)
    high_ref[...] = (index >> 7) & 31
    low_ref[...] = (index & 127) + 128 * (index >> 12)
    for i in range(3):
        block = returned_ref[pl.ds(i, 128, stride=3), :].T
        rows = 128 if i < 2 else 32
        block = block[:rows, :]
        upper = block.astype(BF16).astype(F32)
        piece_ref[0, 128 * i : 128 * i + rows, :] = upper
        piece_ref[1, 128 * i : 128 * i + rows, :] = block - upper
    sub_high = iota((32, 128), 0)
    sub_low = iota((256, 256), 0)

    def scatter(pair, total):
        k = 2 * pair
        left = [[], []]
        for n in (k, k + 1):
            match = spread(high_ref[pl.ds(n, 1), :], 32) == sub_high
            for p in range(2):
                left[p].append(
                    jnp.concatenate(
                        [
                            jnp.where(match, piece_ref[p, pl.ds(32 * c + n, 1), :], 0.0)
                            for c in range(9)
                        ],
                        axis=0,
                    ).astype(BF16)
                )
        hot = indicator(pair_rows(low_ref, k, 256) == sub_low)
        for p in range(2):
            total = total + contract_lanes(jnp.concatenate(left[p], axis=1), hot)
        return total

    total = lax.fori_loop(0, 16, scatter, jnp.zeros((288, 256), F32), unroll=SCATTER_UNROLL)
    sum_ref[0] = total[:, :128]
    sum_ref[1] = total[:, 128:]
    early = iota((8, 128), 0) < 3

    def leave(block):
        span = pl.ds(pl.multiple_of(block * 1024, 1024), 1024)
        return pltpu.make_async_copy(out_ref.at[:, span], out_hbm.at[:, span], sems.at[block])

    def pull(place, half):
        block = place + 4 * half
        start = pl.multiple_of(block * 1024, 1024)
        values = params_ref[:, pl.ds(start, 1024)].reshape(59, 8, 128)
        p = [values[i] for i in range(59)]
        g = [
            sum_ref[half, pl.ds(pl.multiple_of(32 * c + 8 * place, 8), 8), :] for c in range(9)
        ]
        unused_conic, pull_conic = jax.vjp(conic, *p[:10])
        unit, pull_unit = jax.vjp(direction, *p[:3])
        basis, pull_basis = jax.vjp(lambda *d: tuple(harmonics(*d)), *unit)
        d_basis = tuple(
            g[5] * p[11 + i] + g[6] * p[27 + i] + g[7] * p[43 + i] for i in range(16)
        )
        first = list(pull_conic((g[2], g[3], g[4])))
        for i, slope in enumerate(pull_unit(pull_basis(d_basis))):
            first[i] = first[i] + slope
        focal_z = FOCAL / p[2]
        opacity = lax.logistic(p[10])
        first[0] = first[0] + g[0] * focal_z
        first[1] = first[1] + g[1] * focal_z
        first[2] = first[2] - focal_z * ((g[0] * p[0] + g[1] * p[1]) / p[2])
        first.append(g[8] * (opacity * (1.0 - opacity)))
        blank = jnp.zeros((8, 128), F32)

        def turn(rows):
            return jnp.stack(rows, axis=0).reshape(8, 1024)

        out_ref[0:8, pl.ds(start, 1024)] = turn(first[:8])
        rest = turn(first[8:] + [blank] * 5)
        ends_all = turn([basis[i] for i in (13, 14, 15, 0, 1, 2, 3, 4)])
        middle_all = turn([basis[i] for i in range(5, 13)])
        for s in range(8):
            column = pl.ds(pl.multiple_of(start + 128 * s, 128), 128)
            ends = ends_all[:, 128 * s : 128 * s + 128]
            middle = middle_all[:, 128 * s : 128 * s + 128]
            (red, green, blue) = [
                spread(sum_ref[half, pl.ds(32 * c + 8 * place + s, 1), :], 8) for c in (5, 6, 7)
            ]
            out_ref[8:16, column] = jnp.where(early, rest[:, 128 * s : 128 * s + 128], ends * red)
            out_ref[16:24, column] = middle * red
            out_ref[24:32, column] = ends * jnp.where(early, red, green)
            out_ref[32:40, column] = middle * green
            out_ref[40:48, column] = ends * jnp.where(early, green, blue)
            out_ref[48:56, column] = middle * blue
            out_ref[56:59, column] = (ends * blue)[:3]
        leave(block).start()

    for half in range(2):
        lax.fori_loop(0, 4, lambda b, unused, half=half: (pull(b, half), unused)[1], 0, unroll=2)
    for block in range(8):
        leave(block).wait()


def vmem():
    return pl.BlockSpec(memory_space=pltpu.VMEM)


def smem():
    return pl.BlockSpec(memory_space=pltpu.SMEM)


def anywhere():
    return pl.BlockSpec(memory_space=pl.ANY)


def shape(dims, dtype=F32):
    return jax.ShapeDtypeStruct(dims, dtype)


PICK_UNROLL = 4
FORWARD_UNROLL = 4
SCATTER_UNROLL = 16
GIVE_UNROLL = 4
WIDE = pltpu.CompilerParams(vmem_limit_bytes=58 * 1024 * 1024)
ROOM = pltpu.CompilerParams(vmem_limit_bytes=40 * 1024 * 1024)


def swap(values):
    return lax.all_to_all(values, "dev", split_axis=0, concat_axis=0, tiled=True)


def body(
    params, entry_shard, entry_row, depth_order, live_count, tile_of_slot, prev_slot, gt_image
):
    request, holder, place = pl.pallas_call(
        route_kernel,
        out_shape=(shape((128, 128), I32), shape((16, 128), I32), shape((16, 128), I32)),
        in_specs=[anywhere()] * 5,
        out_specs=(vmem(),) * 3,
        scratch_shapes=[pltpu.VMEM((16, 128), I32)] * 3
        + [pltpu.SMEM((16,), I32)] * 2
        + [pltpu.SemaphoreType.DMA((5,))],
        compiler_params=WIDE,
        name="route",
    )(entry_shard, entry_row, depth_order, live_count, prev_slot)
    asked = swap(request)
    table = pl.pallas_call(
        project_kernel,
        out_shape=shape((736, 256), BF16),
        in_specs=[vmem()],
        out_specs=vmem(),
        scratch_shapes=[pltpu.VMEM((288, 256), F32)],
        compiler_params=ROOM,
        cost_estimate=pl.CostEstimate(
            flops=20_000_000, bytes_accessed=20_000_000, transcendentals=100_000
        ),
        name="project",
    )(params)
    picked = pl.pallas_call(
        pick_kernel,
        out_shape=shape((1536, 128), BF16),
        in_specs=[vmem(), vmem(), vmem()],
        out_specs=vmem(),
        scratch_shapes=[
            pltpu.VMEM((32, 128), I32),
            pltpu.VMEM((32, 128), I32),
            pltpu.VMEM((384, 128), F32),
            pltpu.VMEM((1536, 128), F32),
        ],
        compiler_params=ROOM,
        name="pick",
    )(asked, table, gt_image)
    arrived = swap(picked.reshape(128, 3, 4, 128)).reshape(1536, 128)
    picture, loss, outgoing = pl.pallas_call(
        render_kernel,
        out_shape=(shape((16, 768)), shape((16, 128)), shape((384, 128))),
        in_specs=[vmem()] * 3 + [smem(), smem()],
        out_specs=(anywhere(), vmem(), vmem()),
        scratch_shapes=[
            pltpu.VMEM((16, 768), F32),
            pltpu.SemaphoreType.DMA,
            pltpu.VMEM((1536, 128), F32),
            pltpu.VMEM((256, 128), F32),
            pltpu.VMEM((2, 8, 128, 128), F32),
            pltpu.VMEM((2, 128, 128), F32),
            pltpu.VMEM((128, 4, 8, 128), F32),
            pltpu.VMEM((128, 4, 8, 128), F32),
            pltpu.VMEM((128, 4, 8, 128), F32),
            pltpu.VMEM((2, 6, 128, 128), F32),
            pltpu.VMEM((384, 128), F32),
            pltpu.VMEM((16, 128), I32),
            pltpu.VMEM((16, 128), I32),
            pltpu.VMEM((2, 144, 128), F32),
        ],
        compiler_params=ROOM,
        name="render",
    )(arrived, holder, place, tile_of_slot, prev_slot)
    returned = swap(outgoing.reshape(128, 1, 384)).reshape(384, 128)
    gradients = pl.pallas_call(
        update_kernel,
        out_shape=shape((59, 8192)),
        in_specs=[vmem(), vmem(), vmem()],
        out_specs=anywhere(),
        scratch_shapes=[
            pltpu.VMEM((32, 128), I32),
            pltpu.VMEM((32, 128), I32),
            pltpu.VMEM((2, 288, 128), F32),
            pltpu.VMEM((2, 288, 128), F32),
            pltpu.VMEM((59, 8192), F32),
            pltpu.SemaphoreType.DMA((8,)),
        ],
        compiler_params=ROOM,
        name="update",
    )(returned, asked, params)
    return (gradients, picture, loss[:, 0])


def solution(mesh):
    return jax.shard_map(
        body,
        mesh=mesh,
        in_specs=(
            P(None, "dev"),
            P("dev", None),
            P("dev", None),
            P("dev", None),
            P("dev"),
            P("dev"),
            P("dev"),
            P("dev", None),
        ),
        out_specs=(P(None, "dev"), P("dev", None), P("dev")),
        check_vma=False,
    )
```

```python
import jax
import jax.numpy as jnp
from jax import lax
from jax.experimental import pallas as pl
from jax.experimental.pallas import tpu as pltpu
from jax.sharding import PartitionSpec as P

TW = 240
TH = 135
FOCAL = 1200.0
LOG2E = 1.4426950408889634
F32 = jnp.float32
BF16 = jnp.bfloat16
I32 = jnp.int32


def iota(shape, axis):
    return lax.broadcasted_iota(I32, shape, axis)


def take_lane(table, index):
    return jnp.take_along_axis(table, index, axis=1, mode="promise_in_bounds")


def conic(pos_x, pos_y, depth, ls0, ls1, ls2, q0, q1, q2, q3):
    scales = [jnp.exp(ls0), jnp.exp(ls1), jnp.exp(ls2)]
    inverse_q = lax.rsqrt(q0 * q0 + q1 * q1 + q2 * q2 + q3 * q3)
    w_part = q0 * inverse_q
    x_part = q1 * inverse_q
    y_part = q2 * inverse_q
    z_part = q3 * inverse_q
    rotation = [
        [
            1.0 - 2.0 * (y_part * y_part + z_part * z_part),
            2.0 * (x_part * y_part - w_part * z_part),
            2.0 * (x_part * z_part + w_part * y_part),
        ],
        [
            2.0 * (x_part * y_part + w_part * z_part),
            1.0 - 2.0 * (x_part * x_part + z_part * z_part),
            2.0 * (y_part * z_part - w_part * x_part),
        ],
        [
            2.0 * (x_part * z_part - w_part * y_part),
            2.0 * (y_part * z_part + w_part * x_part),
            1.0 - 2.0 * (x_part * x_part + y_part * y_part),
        ],
    ]
    inverse_z = 1.0 / depth
    focal_z = FOCAL * inverse_z
    ratio_x = pos_x * inverse_z
    ratio_y = pos_y * inverse_z
    slope_x = -focal_z * ratio_x
    slope_y = -focal_z * ratio_y
    first = [(focal_z * rotation[0][i] + slope_x * rotation[2][i]) * scales[i] for i in range(3)]
    second = [(focal_z * rotation[1][i] + slope_y * rotation[2][i]) * scales[i] for i in range(3)]
    spread_xx = first[0] * first[0] + first[1] * first[1] + first[2] * first[2] + 0.3
    spread_xy = first[0] * second[0] + first[1] * second[1] + first[2] * second[2]
    spread_yy = second[0] * second[0] + second[1] * second[1] + second[2] * second[2] + 0.3
    inverse_det = 1.0 / (spread_xx * spread_yy - spread_xy * spread_xy)
    return (spread_yy * inverse_det, -spread_xy * inverse_det, spread_xx * inverse_det)


def direction(pos_x, pos_y, depth):
    inverse_norm = lax.rsqrt(pos_x * pos_x + pos_y * pos_y + depth * depth)
    return (pos_x * inverse_norm, pos_y * inverse_norm, depth * inverse_norm)


def harmonics(unit_x, unit_y, unit_z):
    square_x = unit_x * unit_x
    square_y = unit_y * unit_y
    square_z = unit_z * unit_z
    return [
        0.28209479177387814 * jnp.ones_like(unit_x),
        -0.4886025119029199 * unit_y,
        0.4886025119029199 * unit_z,
        -0.4886025119029199 * unit_x,
        1.0925484305920792 * unit_x * unit_y,
        -1.0925484305920792 * unit_y * unit_z,
        0.31539156525252005 * (2.0 * square_z - square_x - square_y),
        -1.0925484305920792 * unit_x * unit_z,
        0.5462742152960396 * (square_x - square_y),
        -0.5900435899266435 * unit_y * (3.0 * square_x - square_y),
        2.890611442640554 * unit_x * unit_y * unit_z,
        -0.4570457994644658 * unit_y * (4.0 * square_z - square_x - square_y),
        0.3731763325901154 * unit_z * (2.0 * square_z - 3.0 * square_x - 3.0 * square_y),
        -0.4570457994644658 * unit_x * (4.0 * square_z - square_x - square_y),
        1.445305721320277 * unit_z * (square_x - square_y),
        -0.5900435899266435 * unit_x * (square_x - 3.0 * square_y),
    ]


def split(value, pieces):
    parts = []
    for _ in range(pieces - 1):
        part = value.astype(BF16)
        parts.append(part)
        value = value - part.astype(F32)
    parts.append(value.astype(BF16))
    return parts


def contract_lanes(left, right):
    return lax.dot_general(left, right, (((1,), (1,)), ((), ())), preferred_element_type=F32)


def indicator(condition):
    return jnp.where(condition, 1.0, 0.0).astype(BF16)


def spread(row, count):
    return jnp.broadcast_to(row, (count, row.shape[1]))


def pair_rows(ref, row, count):
    return jnp.concatenate(
        [spread(ref[pl.ds(row + n, 1), :], count) for n in range(2)], axis=1
    )


def route_kernel(
    shard_hbm, row_hbm, order_hbm, live_hbm, prev_hbm, request_ref, holder_ref, place_ref,
    shard_ref, row_ref, order_ref, live_ref, prev_ref, sems,
):
    tiles, length = shard_ref.shape
    copies = [
        pltpu.make_async_copy(source, target, sems.at[n])
        for n, (source, target) in enumerate(
            [
                (order_hbm, order_ref),
                (shard_hbm, shard_ref),
                (row_hbm, row_ref),
                (live_hbm, live_ref),
                (prev_hbm, prev_ref),
            ]
        )
    ]
    for copy in copies:
        copy.start()
    for copy in copies:
        copy.wait()
    order = order_ref[...]
    shards = take_lane(shard_ref[...], order)
    rows = take_lane(row_ref[...], order)
    sub = iota((128, 128), 0)
    lane = iota((128, 128), 1)
    wide_row = iota((128, 256), 0)
    wide_lane = iota((128, 256), 1)
    counter = indicator((wide_lane >= 128) | (wide_row < wide_lane))
    sub_k = iota((32, 128), 0)
    carry = jnp.zeros((128, 128), F32)
    request = jnp.zeros((128, 32), F32)
    truth = jnp.zeros((128, 128), I32)
    for t in range(tiles):
        live = order[t : t + 1, :] < live_ref[t]
        holder = jnp.where(live, shards[t : t + 1, :], -1)
        match = spread(holder, 128) == sub
        hot = indicator(match)
        counted = jnp.dot(hot, counter, preferred_element_type=F32)
        place = jnp.sum(
            jnp.where(match, counted[:, :128] + carry, 0.0), axis=0, keepdims=True
        ).astype(I32)
        carry = carry + counted[:, 128:]
        holder_ref[t : t + 1, :] = holder
        place_ref[t : t + 1, :] = jnp.where(live, place, -1)
        match_k = spread(place, 32) == sub_k
        row = rows[t : t + 1, :]
        high = jnp.where(match_k, ((row >> 7) * 128).astype(F32), 0.0)
        low = jnp.where(match_k, (row & 127).astype(F32), 0.0)
        asked = jnp.concatenate([high, low], axis=1).astype(BF16)
        request = request + contract_lanes(jnp.concatenate([hot, hot], axis=1), asked)
        previous = prev_ref[t]
        truth = jnp.where(sub == lax.shift_right_logical(previous, 4), previous & 15, truth)
    wide = jnp.concatenate([request.astype(I32), jnp.zeros((128, 96), I32)], axis=1)
    request_ref[...] = jnp.where(lane == 32, truth, wide)


def project_kernel(params_ref, out_ref, table_ref):
    def step(block, half):
        start = pl.multiple_of(half * 4096 + block * 1024, 1024)
        values = params_ref[:, pl.ds(start, 1024)].reshape(59, 8, 128)
        p = [values[i] for i in range(59)]
        (ca, cb, cc) = conic(*p[:10])
        u = FOCAL * p[0] / p[2] + 8.0 * TW
        v = FOCAL * p[1] / p[2] + 8.0 * TH
        opacity = lax.logistic(p[10])
        basis = harmonics(*direction(*p[:3]))
        colors = []
        for channel in range(3):
            color = 0.5 + basis[0] * p[11 + 16 * channel]
            for degree in range(1, 16):
                color = color + basis[degree] * p[11 + 16 * channel + degree]
            colors.append(color)
        for c, value in enumerate([u, v, ca, cb, cc] + colors + [opacity]):
            spot = pl.ds(pl.multiple_of(32 * c + 8 * block, 8), 8)
            table_ref[spot, 128 * half : 128 * half + 128] = value

    for half in range(2):
        lax.fori_loop(0, 4, lambda b, unused, half=half: (step(b, half), unused)[1], 0)
    upper, middle, lower = split(table_ref[...], 3)
    out_ref[0:288, :] = upper
    out_ref[288:576, :] = middle
    out_ref[576:736, :] = lower[:160]


def pick_kernel(
    asked_ref, table_ref, image_ref, out_ref, high_ref, low_ref, found_ref, stage_ref
):
    asked = asked_ref[...]
    index = asked.astype(F32).T[:32, :].astype(I32)
    high_ref[...] = (index >> 7) & 31
    low_ref[...] = (index & 127) + 128 * (index >> 12)
    sub_high = iota((32, 256), 0)
    sub_low = iota((256, 256), 0)
    for k in range(0, 32, 2):
        hot = indicator(pair_rows(low_ref, k, 256) == sub_low)
        parts = jnp.dot(table_ref[...], hot, preferred_element_type=F32)
        both = parts[:288] + parts[288:576]
        whole = jnp.concatenate([both[:160] + parts[576:], both[160:]], axis=0)
        match = pair_rows(high_ref, k, 32) == sub_high
        for c in range(9):
            row = jnp.sum(
                jnp.where(match, whole[32 * c : 32 * c + 32], 0.0), axis=0, keepdims=True
            )
            found_ref[32 * c + k : 32 * c + k + 1, :] = row[:, :128]
            found_ref[32 * c + k + 1 : 32 * c + k + 2, :] = row[:, 128:]
    upper, middle, lower = split(found_ref[128:160, :], 3)
    found_ref[320:352, :] = lower.astype(F32)
    found_ref[352:, :] = jnp.zeros((32, 128), F32)
    upper, lower = split(found_ref[256:288, :], 2)
    found_ref[256:288, :] = upper.astype(F32)
    found_ref[288:320, :] = lower.astype(F32)
    truth = jnp.dot(
        indicator(asked[:, 32:33] == iota((128, 16), 1)), image_ref[...],
        preferred_element_type=F32,
    )
    spot = 0
    for i in range(3):
        block = found_ref[128 * i : 128 * (i + 1), :].T
        for part in split(block, 3 - i):
            stage_ref[pl.ds(spot, 128, stride=12), :] = part.astype(F32)
            spot += 1
    for i in range(6):
        stage_ref[pl.ds(6 + i, 128, stride=12), :] = truth[:, 128 * i : 128 * (i + 1)]
    out_ref[...] = stage_ref[...].astype(BF16)


def put_rows(out_ref, found_ref):
    for i in range(3):
        out_ref[pl.ds(i, 128, stride=3), :] = found_ref[128 * i : 128 * (i + 1), :].T


def swap_blocks(value):
    sub = iota((8, 128), 0)
    block = iota((8, 128), 1) >> 4
    for s in (4, 2, 1):
        up = pltpu.roll(pltpu.roll(value, 8 - s, 0), 16 * s, 1)
        down = up if s == 4 else pltpu.roll(pltpu.roll(value, s, 0), 128 - 16 * s, 1)
        sub_bit = sub & s
        block_bit = block & s
        value = jnp.where(
            sub_bit == block_bit, value, jnp.where(sub_bit < block_bit, up, down)
        )
    return value


def loss_and_slopes(images, target):
    loss = jnp.zeros((16, 1), F32)
    slopes = []
    for k in range(3):
        image = images[k]
        wanted = target[:, 256 * k : 256 * (k + 1)]
        difference = image - wanted
        smooth = jnp.sqrt(difference * difference + 0.0001)
        mean_r = jnp.sum(image, axis=1, keepdims=True) / 256.0
        mean_t = jnp.sum(wanted, axis=1, keepdims=True) / 256.0
        centered_r = image - mean_r
        centered_t = wanted - mean_t
        var_r = jnp.sum(centered_r * centered_r, axis=1, keepdims=True) / 256.0
        var_t = jnp.sum(centered_t * centered_t, axis=1, keepdims=True) / 256.0
        cov = jnp.sum(centered_r * centered_t, axis=1, keepdims=True) / 256.0
        top_m = 2.0 * mean_r * mean_t + 0.0001
        top_c = 2.0 * cov + 0.0009
        low_m = mean_r * mean_r + mean_t * mean_t + 0.0001
        low_v = var_r + var_t + 0.0009
        below = 1.0 / (low_m * low_v)
        similarity = top_m * top_c * below
        loss = loss + (0.8 / 3.0) * jnp.sum(smooth, axis=1, keepdims=True)
        loss = loss + (0.2 * 256.0 / 3.0) * (1.0 - similarity)
        by_mean = 2.0 * mean_t * top_c * below - similarity * 2.0 * mean_r / low_m
        by_cov = 2.0 * top_m * below
        by_var = -similarity / low_v
        slopes.append(
            (0.8 / 3.0) * difference / smooth
            - (0.2 / 3.0) * (by_mean + 2.0 * by_var * centered_r + by_cov * centered_t)
        )
    return loss, slopes


def render_kernel(
    arrived_ref, holder_ref, place_ref, tile_ref, prev_ref,
    picture_hbm, loss_ref, out_ref, picture_ref, picture_sem, stage_ref,
    ordered_ref, row_ref, dx_ref, alpha_ref, weight_ref, reach_ref, moment_ref, found_ref,
    code_ref, low_ref, part_ref,
):
    code_ref[...] = (place_ref[...] >> 4) * 128 + holder_ref[...]
    low_ref[...] = place_ref[...] & 15
    stage_ref[...] = arrived_ref[...].astype(F32)
    came = [stage_ref[pl.ds(i, 128, stride=12), :] for i in range(12)]
    table = [(came[0] + came[1] + came[2]).T, (came[3] + came[4]).T, came[5].T]
    folded = []
    for c in range(9):
        part = table[c // 4][32 * (c % 4) : 32 * (c % 4) + 32, :]
        if c == 4:
            part = part + table[2][64:96, :]
        if c == 8:
            part = part + table[2][32:64, :]
        folded.append(jnp.concatenate([part[:16], part[16:]], axis=1))
    pieces = jnp.concatenate(split(jnp.concatenate(folded, axis=0), 3), axis=0)
    sub_slot = iota((256, 256), 0)
    sub_place = iota((16, 256), 0)

    def pick(pair, unused):
        t = 2 * pair
        hot = indicator(pair_rows(code_ref, t, 256) == sub_slot)
        parts = jnp.dot(pieces, hot, preferred_element_type=F32)
        whole = parts[:144] + parts[144:288] + parts[288:]
        match = pair_rows(low_ref, t, 16) == sub_place
        for c in range(9):
            row = jnp.sum(
                jnp.where(match, whole[16 * c : 16 * c + 16], 0.0), axis=0, keepdims=True
            )
            ordered_ref[pl.ds(16 * c + t, 1), :] = row[:, :128]
            ordered_ref[pl.ds(16 * c + t + 1, 1), :] = row[:, 128:]
        return unused

    lax.fori_loop(0, 8, pick, 0, unroll=PICK_UNROLL)
    sub = iota((16, 128), 0)
    base_x = jnp.zeros((16, 128), F32)
    base_y = jnp.zeros((16, 128), F32)
    source = jnp.zeros((16, 128), I32)
    for t in range(16):
        number = tile_ref[t]
        tile_row = number // TW
        tile_column = number - tile_row * TW
        base_x = jnp.where(sub == t, (16 * tile_column + 8).astype(F32), base_x)
        base_y = jnp.where(sub == t, (16 * tile_row + 8).astype(F32), base_y)
        source = jnp.where(sub == t, lax.shift_right_logical(prev_ref[t], 4), source)
    ordered_ref[0:16, :] = ordered_ref[0:16, :] - base_x
    ordered_ref[16:32, :] = ordered_ref[16:32, :] - base_y
    ordered_ref[144:, :] = jnp.zeros((112, 128), F32)
    turned = [ordered_ref[0:128, :].T, ordered_ref[128:256, :].T]
    lane = iota((128, 128), 1)
    grid_x = (lane & 15).astype(F32) - 7.5
    for g in range(2):
        owner = (lane >> 4) + 8 * g

        def wide(c):
            return take_lane(turned[c // 8], owner + 16 * (c % 8))

        dx = grid_x - wide(0)
        dx_ref[g] = dx
        row_ref[g, 0] = (-0.5 * LOG2E) * wide(2) * dx * dx
        row_ref[g, 1] = (-LOG2E) * wide(3) * dx
        row_ref[g, 2] = (-0.5 * LOG2E) * wide(4)
        row_ref[g, 3] = wide(1)
        row_ref[g, 4] = wide(8)
        row_ref[g, 5] = wide(5)
        row_ref[g, 6] = wide(6)
        row_ref[g, 7] = wide(7)
    sub8 = iota((8, 128), 0)
    grid_y = [sub8.astype(F32) - 7.5, sub8.astype(F32) + 0.5]
    ones = jnp.ones((8, 128), F32)
    zero = jnp.zeros((8, 128), F32)

    def row_of(g, r, j):
        return spread(row_ref[g, r, pl.ds(j, 1), :], 8)

    def forward(j, state):
        reach = list(state[0])
        sums = list(state[1])
        for g in range(2):
            (part_a, part_b, part_c, gv, go, g0, g1, g2) = [row_of(g, r, j) for r in range(8)]
            for h in range(2):
                n = 2 * g + h
                dy = grid_y[h] - gv
                fall = jnp.exp2(part_a + dy * (part_b + part_c * dy))
                alpha = go * fall
                weight = alpha * reach[n]
                alpha_ref[j, n] = alpha
                weight_ref[j, n] = weight
                reach_ref[j, n] = fall * reach[n]
                reach[n] = reach[n] - weight
                sums[3 * n] = sums[3 * n] + weight * g0
                sums[3 * n + 1] = sums[3 * n + 1] + weight * g1
                sums[3 * n + 2] = sums[3 * n + 2] + weight * g2
        return (tuple(reach), tuple(sums))

    unused, sums = lax.fori_loop(
        0, 128, forward, (tuple([ones] * 4), tuple([zero] * 12)), unroll=FORWARD_UNROLL
    )
    chosen = indicator(source == iota((16, 128), 1))
    target = jnp.concatenate(
        [
            jnp.dot(chosen, came[6 + i].astype(BF16), preferred_element_type=F32)
            for i in range(6)
        ],
        axis=1,
    )
    images = []
    for k in range(3):
        image = jnp.concatenate(
            [
                jnp.concatenate(
                    [swap_blocks(sums[6 * g + k]), swap_blocks(sums[6 * g + 3 + k])], axis=1
                )
                for g in range(2)
            ],
            axis=0,
        )
        picture_ref[:, 256 * k : 256 * (k + 1)] = image
        images.append(image)
    picture_copy = pltpu.make_async_copy(picture_ref, picture_hbm, picture_sem)
    picture_copy.start()
    loss, slopes = loss_and_slopes(images, target)
    loss_ref[...] = jnp.broadcast_to(loss, (16, 128))
    slope = [
        [
            swap_blocks(slopes[k][8 * g : 8 * g + 8, 128 * h : 128 * h + 128])
            for k in range(3)
        ]
        for g in range(2)
        for h in range(2)
    ]
    grid_yy = [grid_y[h] * grid_y[h] for h in range(2)]

    def fold(first, second, distance):
        bit = (sub8 & distance) != 0
        if distance == 4:
            return jnp.where(bit, second, first) + pltpu.roll(
                jnp.where(bit, first, second), 4, 0
            )
        return jnp.where(
            bit,
            second + pltpu.roll(second, distance, 0),
            first + pltpu.roll(first, 8 - distance, 0),
        )

    def backward(block, state):
        behind = list(state)
        base = pl.multiple_of(120 - 8 * block, 8)
        for g in range(2):
            waiting = {}
            for s in range(7, -1, -1):
                j = base + s
                (g0, g1, g2) = [row_of(g, r, j) for r in (5, 6, 7)]
                pulls = []
                shares = []
                for h in range(2):
                    n = 2 * g + h
                    value = slope[n][0] * g0 + slope[n][1] * g1 + slope[n][2] * g2
                    gap = value - behind[n]
                    pulls.append(reach_ref[j, n] * gap)
                    behind[n] = behind[n] + alpha_ref[j, n] * gap
                    weight = weight_ref[j, n]
                    shares.append([weight * slope[n][k] for k in range(3)])
                found = [
                    pulls[0] + pulls[1],
                    pulls[0] * grid_y[0] + pulls[1] * grid_y[1],
                    pulls[0] * grid_yy[0] + pulls[1] * grid_yy[1],
                    shares[0][0] + shares[1][0],
                    shares[0][1] + shares[1][1],
                    shares[0][2] + shares[1][2],
                ]
                spot = s
                for distance in (1, 2, 4):
                    if spot & distance:
                        break
                    above = waiting.pop((distance, spot + distance))
                    found = [fold(a, b, distance) for a, b in zip(found, above)]
                    if distance == 4:
                        for q in range(6):
                            moment_ref[g, q, pl.ds(base, 8), :] = found[q]
                else:
                    continue
                waiting[(distance, spot)] = found
        return tuple(behind)

    lax.fori_loop(0, 16, backward, tuple([zero] * 4))
    totals = jnp.zeros((16, 1152), F32)
    for g in range(2):
        dx = dx_ref[g]
        gv = row_ref[g, 3]
        m0 = moment_ref[g, 0]
        m1 = moment_ref[g, 1]
        sx = dx * m0
        sy = m1 - gv * m0
        syy = moment_ref[g, 2] - gv * (m1 + sy)
        stack = jnp.concatenate(
            [m0, sx, sy, dx * sx, dx * sy, syy]
            + [moment_ref[g, q] for q in range(3, 6)],
            axis=0,
        )
        tile = iota((16, 256), 0)
        pick = indicator(tile == ((iota((16, 256), 1) >> 4) & 7) + 8 * g)
        totals = totals + contract_lanes(pick, jnp.concatenate(split(stack, 2), axis=1))
    (m0, sx, sy, sxx, sxy, syy, d_red, d_green, d_blue) = [
        totals[:, 128 * c : 128 * c + 128] for c in range(9)
    ]
    (ca, cb, cc) = [ordered_ref[16 * c : 16 * c + 16, :] for c in (2, 3, 4)]
    opacity = ordered_ref[128:144, :]
    results = [
        opacity * (ca * sx + cb * sy),
        opacity * (cb * sx + cc * sy),
        -0.5 * opacity * sxx,
        -opacity * sxy,
        -0.5 * opacity * syy,
        d_red,
        d_green,
        d_blue,
        m0,
    ]
    for c, result in enumerate(results):
        for p, part in enumerate(split(result, 2)):
            part_ref[p, 16 * c : 16 * c + 16, :] = part.astype(F32)
    sub_k = iota((32, 128), 0)
    sub_h = iota((128, 128), 0)

    def give(pair, total):
        hot = []
        left = [[], []]
        for n in range(2):
            tile = 2 * pair + n
            hot.append(indicator(spread(holder_ref[pl.ds(tile, 1), :], 128) == sub_h))
            match = spread(place_ref[pl.ds(tile, 1), :], 32) == sub_k
            for p in range(2):
                left[p].append(
                    jnp.concatenate(
                        [
                            jnp.where(match, part_ref[p, pl.ds(16 * c + tile, 1), :], 0.0)
                            for c in range(9)
                        ],
                        axis=0,
                    ).astype(BF16)
                )
        hot = jnp.concatenate(hot, axis=1)
        for p in range(2):
            total = total + contract_lanes(jnp.concatenate(left[p], axis=1), hot)
        return total

    total = lax.fori_loop(0, 8, give, jnp.zeros((288, 128), F32), unroll=GIVE_UNROLL)
    found_ref[0:288, :] = total
    found_ref[288:, :] = jnp.zeros((96, 128), F32)
    put_rows(out_ref, found_ref)
    picture_copy.wait()


def update_kernel(
    returned_ref, asked_ref, params_ref, out_hbm,
    high_ref, low_ref, piece_ref, sum_ref, out_ref, sems,
):
    index = asked_ref[...].astype(F32).T[:32, :].astype(I32)
    high_ref[...] = (index >> 7) & 31
    low_ref[...] = (index & 127) + 128 * (index >> 12)
    for i in range(3):
        block = returned_ref[pl.ds(i, 128, stride=3), :].T
        rows = 128 if i < 2 else 32
        block = block[:rows, :]
        upper = block.astype(BF16).astype(F32)
        piece_ref[0, 128 * i : 128 * i + rows, :] = upper
        piece_ref[1, 128 * i : 128 * i + rows, :] = block - upper
    sub_high = iota((32, 128), 0)
    sub_low = iota((256, 256), 0)

    def scatter(pair, total):
        k = 2 * pair
        left = [[], []]
        for n in (k, k + 1):
            match = spread(high_ref[pl.ds(n, 1), :], 32) == sub_high
            for p in range(2):
                left[p].append(
                    jnp.concatenate(
                        [
                            jnp.where(match, piece_ref[p, pl.ds(32 * c + n, 1), :], 0.0)
                            for c in range(9)
                        ],
                        axis=0,
                    ).astype(BF16)
                )
        hot = indicator(pair_rows(low_ref, k, 256) == sub_low)
        for p in range(2):
            total = total + contract_lanes(jnp.concatenate(left[p], axis=1), hot)
        return total

    total = lax.fori_loop(0, 16, scatter, jnp.zeros((288, 256), F32), unroll=SCATTER_UNROLL)
    sum_ref[0] = total[:, :128]
    sum_ref[1] = total[:, 128:]
    early = iota((8, 128), 0) < 3

    def leave(block):
        span = pl.ds(pl.multiple_of(block * 1024, 1024), 1024)
        return pltpu.make_async_copy(out_ref.at[:, span], out_hbm.at[:, span], sems.at[block])

    def pull(place, half):
        block = place + 4 * half
        start = pl.multiple_of(block * 1024, 1024)
        values = params_ref[:, pl.ds(start, 1024)].reshape(59, 8, 128)
        p = [values[i] for i in range(59)]
        g = [
            sum_ref[half, pl.ds(pl.multiple_of(32 * c + 8 * place, 8), 8), :] for c in range(9)
        ]
        unused_conic, pull_conic = jax.vjp(conic, *p[:10])
        unit, pull_unit = jax.vjp(direction, *p[:3])
        basis, pull_basis = jax.vjp(lambda *d: tuple(harmonics(*d)), *unit)
        d_basis = tuple(
            g[5] * p[11 + i] + g[6] * p[27 + i] + g[7] * p[43 + i] for i in range(16)
        )
        first = list(pull_conic((g[2], g[3], g[4])))
        for i, slope in enumerate(pull_unit(pull_basis(d_basis))):
            first[i] = first[i] + slope
        focal_z = FOCAL / p[2]
        opacity = lax.logistic(p[10])
        first[0] = first[0] + g[0] * focal_z
        first[1] = first[1] + g[1] * focal_z
        first[2] = first[2] - focal_z * ((g[0] * p[0] + g[1] * p[1]) / p[2])
        first.append(g[8] * (opacity * (1.0 - opacity)))
        blank = jnp.zeros((8, 128), F32)

        def turn(rows):
            return jnp.stack(rows, axis=0).reshape(8, 1024)

        out_ref[0:8, pl.ds(start, 1024)] = turn(first[:8])
        rest = turn(first[8:] + [blank] * 5)
        ends_all = turn([basis[i] for i in (13, 14, 15, 0, 1, 2, 3, 4)])
        middle_all = turn([basis[i] for i in range(5, 13)])
        for s in range(8):
            column = pl.ds(pl.multiple_of(start + 128 * s, 128), 128)
            ends = ends_all[:, 128 * s : 128 * s + 128]
            middle = middle_all[:, 128 * s : 128 * s + 128]
            (red, green, blue) = [
                spread(sum_ref[half, pl.ds(32 * c + 8 * place + s, 1), :], 8) for c in (5, 6, 7)
            ]
            out_ref[8:16, column] = jnp.where(early, rest[:, 128 * s : 128 * s + 128], ends * red)
            out_ref[16:24, column] = middle * red
            out_ref[24:32, column] = ends * jnp.where(early, red, green)
            out_ref[32:40, column] = middle * green
            out_ref[40:48, column] = ends * jnp.where(early, green, blue)
            out_ref[48:56, column] = middle * blue
            out_ref[56:59, column] = (ends * blue)[:3]
        leave(block).start()

    for half in range(2):
        lax.fori_loop(0, 4, lambda b, unused, half=half: (pull(b, half), unused)[1], 0, unroll=2)
    for block in range(8):
        leave(block).wait()


def vmem():
    return pl.BlockSpec(memory_space=pltpu.VMEM)


def smem():
    return pl.BlockSpec(memory_space=pltpu.SMEM)


def anywhere():
    return pl.BlockSpec(memory_space=pl.ANY)


def shape(dims, dtype=F32):
    return jax.ShapeDtypeStruct(dims, dtype)


PICK_UNROLL = 4
FORWARD_UNROLL = 8
SCATTER_UNROLL = 16
GIVE_UNROLL = 4
WIDE = pltpu.CompilerParams(vmem_limit_bytes=58 * 1024 * 1024)
ROOM = pltpu.CompilerParams(vmem_limit_bytes=40 * 1024 * 1024)


def swap(values):
    return lax.all_to_all(values, "dev", split_axis=0, concat_axis=0, tiled=True)


def body(
    params, entry_shard, entry_row, depth_order, live_count, tile_of_slot, prev_slot, gt_image
):
    request, holder, place = pl.pallas_call(
        route_kernel,
        out_shape=(shape((128, 128), I32), shape((16, 128), I32), shape((16, 128), I32)),
        in_specs=[anywhere()] * 5,
        out_specs=(vmem(),) * 3,
        scratch_shapes=[pltpu.VMEM((16, 128), I32)] * 3
        + [pltpu.SMEM((16,), I32)] * 2
        + [pltpu.SemaphoreType.DMA((5,))],
        compiler_params=WIDE,
        name="route",
    )(entry_shard, entry_row, depth_order, live_count, prev_slot)
    asked = swap(request)
    table = pl.pallas_call(
        project_kernel,
        out_shape=shape((736, 256), BF16),
        in_specs=[vmem()],
        out_specs=vmem(),
        scratch_shapes=[pltpu.VMEM((288, 256), F32)],
        compiler_params=ROOM,
        cost_estimate=pl.CostEstimate(
            flops=20_000_000, bytes_accessed=20_000_000, transcendentals=100_000
        ),
        name="project",
    )(params)
    picked = pl.pallas_call(
        pick_kernel,
        out_shape=shape((1536, 128), BF16),
        in_specs=[vmem(), vmem(), vmem()],
        out_specs=vmem(),
        scratch_shapes=[
            pltpu.VMEM((32, 128), I32),
            pltpu.VMEM((32, 128), I32),
            pltpu.VMEM((384, 128), F32),
            pltpu.VMEM((1536, 128), F32),
        ],
        compiler_params=ROOM,
        name="pick",
    )(asked, table, gt_image)
    arrived = swap(picked.reshape(128, 3, 4, 128)).reshape(1536, 128)
    picture, loss, outgoing = pl.pallas_call(
        render_kernel,
        out_shape=(shape((16, 768)), shape((16, 128)), shape((384, 128))),
        in_specs=[vmem()] * 3 + [smem(), smem()],
        out_specs=(anywhere(), vmem(), vmem()),
        scratch_shapes=[
            pltpu.VMEM((16, 768), F32),
            pltpu.SemaphoreType.DMA,
            pltpu.VMEM((1536, 128), F32),
            pltpu.VMEM((256, 128), F32),
            pltpu.VMEM((2, 8, 128, 128), F32),
            pltpu.VMEM((2, 128, 128), F32),
            pltpu.VMEM((128, 4, 8, 128), F32),
            pltpu.VMEM((128, 4, 8, 128), F32),
            pltpu.VMEM((128, 4, 8, 128), F32),
            pltpu.VMEM((2, 6, 128, 128), F32),
            pltpu.VMEM((384, 128), F32),
            pltpu.VMEM((16, 128), I32),
            pltpu.VMEM((16, 128), I32),
            pltpu.VMEM((2, 144, 128), F32),
        ],
        compiler_params=ROOM,
        name="render",
    )(arrived, holder, place, tile_of_slot, prev_slot)
    returned = swap(outgoing.reshape(128, 1, 384)).reshape(384, 128)
    gradients = pl.pallas_call(
        update_kernel,
        out_shape=shape((59, 8192)),
        in_specs=[vmem(), vmem(), vmem()],
        out_specs=anywhere(),
        scratch_shapes=[
            pltpu.VMEM((32, 128), I32),
            pltpu.VMEM((32, 128), I32),
            pltpu.VMEM((2, 288, 128), F32),
            pltpu.VMEM((2, 288, 128), F32),
            pltpu.VMEM((59, 8192), F32),
            pltpu.SemaphoreType.DMA((8,)),
        ],
        compiler_params=ROOM,
        name="update",
    )(returned, asked, params)
    return (gradients, picture, loss[:, 0])


def solution(mesh):
    return jax.shard_map(
        body,
        mesh=mesh,
        in_specs=(
            P(None, "dev"),
            P("dev", None),
            P("dev", None),
            P("dev", None),
            P("dev"),
            P("dev"),
            P("dev"),
            P("dev", None),
        ),
        out_specs=(P(None, "dev"), P("dev", None), P("dev")),
        check_vma=False,
    )
```
